32 devices in a mesh: dp: 16 (over z, x, core), seq: 2 (over y).
Axes of the slice: x: 2, y: 2, z: 4, core: 2. Of those that a mesh axis runs over, the one named last changes fastest.
Arguments:
- hidden_in: bfloat16 [16, 1024, 1408], P('dp', 'seq'), may hold values from -6 to 6
- skip_in: bfloat16 [16, 1024, 1408], P('dp', 'seq'), may hold values from -6 to 6
- clip_text: bfloat16 [16, 77, 1024], P('dp'), may hold values from -6 to 6
- mt5_text: bfloat16 [16, 256, 2048], P('dp'), may hold values from -6 to 6
- time_ids: int32 [16], P('dp'), may hold values from 0 to 999
- null_text: int32 [16], P('dp'), may hold values 0 or 1
- loss_weight: float32 [16], P('dp'), may hold values from 0.3 to 3
- patch_pos: int32 [2, 16, 1024], P(None, 'dp', 'seq'), may hold values from 0 to 63, as said below
- out_cot: bfloat16 [16, 1024, 1408], P('dp', 'seq'), may hold values from -6 to 6
- skip_weight: bfloat16 [2816, 1408], P('dp', 'seq'), may hold values from -0.109375 to 0.109375
- time_first: bfloat16 [256, 1408], P('dp', 'seq'), may hold values from -0.375 to 0.375
- time_second: bfloat16 [1408, 1408], P('dp', 'seq'), may hold values from -0.15625 to 0.15625
- attn_qkv: bfloat16 [1408, 4224], P('dp', 'seq'), may hold values from -0.15625 to 0.15625
- attn_out: bfloat16 [1408, 1408], P('dp', 'seq'), may hold values from -2.5 to 2.5
- cross_qproj: bfloat16 [1408, 1408], P('dp', 'seq'), may hold values from -0.15625 to 0.15625
- cross_kvproj: bfloat16 [1024, 2816], P('dp', 'seq'), may hold values from -0.1875 to 0.1875
- cross_out: bfloat16 [1408, 1408], P('dp', 'seq'), may hold values from -1.5 to 1.5
- text_proj: bfloat16 [2048, 1024], P('dp', 'seq'), may hold values from -0.125 to 0.125
- mlp_up: bfloat16 [1408, 6336], P('dp', 'seq'), may hold values from -0.15625 to 0.15625
- mlp_down: bfloat16 [6336, 1408], P('dp', 'seq'), may hold values from -0.078125 to 0.078125
- norm_gains: float32 [4, 1408], replicated, may hold values from 0.5 to 1.5
- head_gains: float32 [4, 88], replicated, may hold values from 0.5 to 1.5
Outputs:
- block_out: bfloat16 [16, 1024, 1408], P('dp', 'seq')
- hidden_grad: float32 [16, 1024, 1408], P('dp', 'seq')
- skip_grad: float32 [16, 1024, 1408], P('dp', 'seq')
- grad_skipw: float32 [2816, 1408], P('dp', 'seq')
- grad_tfirst: float32 [256, 1408], P('dp', 'seq')
- grad_tsecond: float32 [1408, 1408], P('dp', 'seq')
- grad_qkv: float32 [1408, 4224], P('dp', 'seq')
- grad_aout: float32 [1408, 1408], P('dp', 'seq')
- grad_cquery: float32 [1408, 1408], P('dp', 'seq')
- grad_ckv: float32 [1024, 2816], P('dp', 'seq')
- grad_cout: float32 [1408, 1408], P('dp', 'seq')
- grad_tproj: float32 [2048, 1024], P('dp', 'seq')
- grad_up: float32 [1408, 6336], P('dp', 'seq')
- grad_down: float32 [6336, 1408], P('dp', 'seq')
- grad_ngains: float32 [4, 1408], replicated
- grad_hgains: float32 [4, 88], replicated
The draws below stay inside these ranges and needn't reach their ends.
Inputs may be any that keep to these rules, and one draw needn't show every extreme that they name: `patch_pos`: each image's patches are the cells of a 32 x 32 grid, each cell once, in an order of that image's own, shifted by a row and a column offset of that image.
All inputs are finite; a program needn't handle non-finite values. No bound on the sum of `null_text` on one device may be relied on, other than what follows from the above.
Results may differ from the reference program's by a relative error of at most 0.023.
Values may be sent and summed in bfloat16 or wider, within the bound.
A program may use at most 384 MiB of HBM per device.

```python
import math
import jax
import jax.numpy as jnp
from jax import lax

HEADS = 16
HEAD_DIM = 88
D = 1408
FF = 6336
FREQ = 256
TEXT_DIM = 1024
T5_DIM = 2048
CLIP_LEN = 77
T5_LEN = 256
GRID = 32
SEQ_LEN = 1024
IMAGES = 16


def draw_patch_pos(key, part):
    key = jax.random.fold_in(key, 11)
    offset_key, order_key = jax.random.split(key)
    offsets = jax.random.randint(offset_key, (2, IMAGES), 0, GRID)
    offsets = offsets.at[0, 0].set(0).at[1, 0].set(GRID)
    image_keys = jax.random.split(order_key, IMAGES)
    orders = jax.vmap(lambda one_key: jax.random.permutation(one_key, SEQ_LEN))(image_keys).astype(jnp.int32)
    layout = jnp.stack([orders // GRID, orders % GRID])
    return (layout + offsets[:, :, None]).astype(jnp.int32)


def plant(array, key, least, largest):
    longest = array.shape.index(max(array.shape))
    spots = []
    for shift in (0, 1):
        where = [jax.random.randint(jax.random.fold_in(key, axis), (), 0, length) for axis, length in enumerate(array.shape)]
        where[longest] = (where[longest] + shift) % array.shape[longest]
        spots.append(tuple(where))
    return array.at[spots[0]].set(least).at[spots[1]].set(largest)


def block_scale(rng, shape, cuts, low, high):
    def one(dim, parts):
        draws = jax.random.uniform(jax.random.fold_in(jax.random.fold_in(rng, 6), dim), (parts,), jnp.float32, low / len(cuts), high / len(cuts))
        return jnp.repeat(jnp.exp(draws), shape[dim] // parts).reshape((-1,) + (1,) * (len(shape) - dim - 1))

    factor_of = one(*cuts[0])
    for cut in cuts[1:]:
        factor_of = factor_of * one(*cut)
    return factor_of


def bell_draw(stream_key, extent, spread, reach, cuts=(), kind=jnp.bfloat16):
    entries = jax.random.normal(stream_key, extent, jnp.float32) * spread
    if len(cuts) > 0:
        entries = block_scale(stream_key, extent, cuts, -0.22, 0.18) * entries
    return jnp.clip(entries, min=-reach, max=reach).astype(kind)


def setup_inputs(seed: int = 0) -> dict:
    streams_of = jax.random.split(jax.random.key(seed), 23)
    return {
        "hidden_in": bell_draw(streams_of[0], (IMAGES, SEQ_LEN, D), 1.0, 6.0, ((0, 16), (1, 2))),
        "skip_in": bell_draw(streams_of[1], (IMAGES, SEQ_LEN, D), 1.0, 6.0, ((0, 16), (1, 2))),
        "clip_text": bell_draw(streams_of[2], (IMAGES, CLIP_LEN, TEXT_DIM), 1.0, 6.0, ((0, 16),)),
        "mt5_text": bell_draw(streams_of[3], (IMAGES, T5_LEN, T5_DIM), 1.0, 6.0, ((0, 16),)),
        "time_ids": plant(jax.random.randint(streams_of[4], (IMAGES,), 0, 1000), jax.random.fold_in(streams_of[4], 1), 0, 999).astype(jnp.int32),
        "null_text": plant((jax.random.randint(streams_of[5], (IMAGES,), 0, 4) < 1).astype(jnp.int32), jax.random.fold_in(streams_of[5], 1), 0, 1),
        "loss_weight": jnp.clip(jnp.exp(math.log(3.0) - 2.3025851 * jax.random.uniform(streams_of[6], (IMAGES,), jnp.float32) ** block_scale(streams_of[6], (IMAGES,), ((0, 16),), -0.2, 0.2)), 0.3, 3.0),
        "patch_pos": draw_patch_pos(jax.random.fold_in(streams_of[22], 71), 0),
        "out_cot": bell_draw(streams_of[8], (IMAGES, SEQ_LEN, D), 1.0, 6.0, ((0, 16), (1, 2))),
        "skip_weight": bell_draw(streams_of[9], (2 * D, D), (2 * D) ** -0.5, 0.109375, ((0, 16), (1, 2))),
        "time_first": bell_draw(streams_of[10], (FREQ, D), FREQ ** -0.5, 0.375, ((0, 16), (1, 2))),
        "time_second": bell_draw(streams_of[11], (D, D), D ** -0.5, 0.15625, ((0, 16), (1, 2))),
        "attn_qkv": bell_draw(streams_of[12], (D, 3 * D), D ** -0.5, 0.15625, ((0, 16), (1, 2))),
        "attn_out": bell_draw(streams_of[13], (D, D), (max(1, 4 * D // SEQ_LEN)) ** -0.5, 2.5, ((0, 16), (1, 2))),
        "cross_qproj": bell_draw(streams_of[14], (D, D), D ** -0.5, 0.15625, ((0, 16), (1, 2))),
        "cross_kvproj": bell_draw(streams_of[15], (TEXT_DIM, 2 * D), TEXT_DIM ** -0.5, 0.1875, ((0, 16), (1, 2))),
        "cross_out": bell_draw(streams_of[16], (D, D), (max(1, 4 * D // (CLIP_LEN + T5_LEN))) ** -0.5, 1.5, ((0, 16), (1, 2))),
        "text_proj": bell_draw(streams_of[17], (T5_DIM, TEXT_DIM), T5_DIM ** -0.5, 0.125, ((0, 16), (1, 2))),
        "mlp_up": bell_draw(streams_of[18], (D, FF), D ** -0.5, 0.15625, ((0, 16), (1, 2))),
        "mlp_down": bell_draw(streams_of[19], (FF, D), FF ** -0.5, 0.078125, ((0, 16), (1, 2))),
        "norm_gains": jnp.clip(1.0 + 0.1 * jax.random.normal(streams_of[20], (4, D), jnp.float32), 0.5, 1.5),
        "head_gains": jnp.clip(1.0 + 0.1 * jax.random.normal(streams_of[21], (4, HEAD_DIM), jnp.float32), 0.5, 1.5),
    }


@jax.custom_vjp
def low(v):
    return lax.optimization_barrier(v.astype(jnp.bfloat16)).astype(jnp.float32)

@jax.custom_vjp
def low_back(v):
    return v

def low_keep(v):
    return (low(v), None)

def low_pass(kept, grad):
    return (grad,)

def back_keep(v):
    return (v, None)

def back_low(kept, grad):
    return (low(grad),)
low.defvjp(low_keep, low_pass)
low_back.defvjp(back_keep, back_low)

def double_round(values):
    return low(low_back(values))

def matmul(left, right):
    return jnp.dot(left, right, precision=lax.Precision.HIGHEST)

def normalize(values):
    center = values - lax.optimization_barrier(jnp.mean(values, axis=-1, keepdims=True))
    variance = lax.optimization_barrier(jnp.mean(center * center, axis=-1, keepdims=True))
    return center * lax.rsqrt(variance + 1e-06)

def rotate(values, pos_rows, pos_cols):
    quarter = values.shape[-1] // 4
    frequency = 10000.0 ** (-jnp.arange(quarter, dtype=jnp.float32) / quarter)

    def turn(halfpart, position):
        angles = position[:, None] * frequency[None, :]
        cosine = jnp.cos(angles)[:, None, :]
        sine_part = jnp.sin(angles)[:, None, :]
        former = halfpart[..., :quarter]
        latter = halfpart[..., quarter:]
        return jnp.concatenate([former * cosine - latter * sine_part, former * sine_part + latter * cosine], -1)
    return jnp.concatenate([turn(values[..., :2 * quarter], pos_rows), turn(values[..., 2 * quarter:], pos_cols)], -1)

def time_features(step_ids):
    half_count = FREQ // 2
    frequency = jnp.exp(-math.log(10000.0) * jnp.arange(half_count, dtype=jnp.float32) / half_count)
    angles = step_ids.astype(jnp.float32)[:, None] * frequency[None, :]
    return jnp.concatenate([jnp.cos(angles), jnp.sin(angles)], -1)

def attend(queries, keyset, valueset):
    scores = low_back(jnp.einsum('qhd,khd->hqk', queries, keyset, precision=lax.Precision.HIGHEST) * HEAD_DIM ** (-0.5))
    weights = jax.nn.softmax(scores, axis=-1)
    return jnp.einsum('hqk,khd->qhd', low(weights), valueset, precision=lax.Precision.HIGHEST)

def image_forward(weight_set, gain_set, hidden, skip_part, clip_part, mt5_part, time_id, keep_text, pos_rows, pos_cols):
    w_skip, w_first, w_second, w_qkv, w_aout, w_cq, w_ckv, w_cout, w_text, w_up, w_down = weight_set
    norm_set, head_set = gain_set
    merged = low_back(matmul(jnp.concatenate([hidden, skip_part], -1), w_skip))
    resid = normalize(merged) * norm_set[0]
    feats = low(time_features(time_id[None]))
    shift = matmul(low(jax.nn.silu(matmul(feats, w_first))), w_second)
    normed = low(normalize(resid) * norm_set[1] + shift)
    packed = low_back(matmul(normed, w_qkv)).reshape(SEQ_LEN, 3, HEADS, HEAD_DIM)
    self_q = double_round(rotate(normalize(packed[:, 0]) * head_set[0], pos_rows, pos_cols))
    self_k = double_round(rotate(normalize(packed[:, 1]) * head_set[1], pos_rows, pos_cols))
    self_v = low(packed[:, 2])
    self_o = double_round(attend(self_q, self_k, self_v).reshape(SEQ_LEN, D))
    resid = resid + low_back(matmul(self_o, w_aout))
    normed = low(normalize(resid) * norm_set[2])
    cross_pre = low_back(matmul(normed, w_cq)).reshape(SEQ_LEN, HEADS, HEAD_DIM)
    cross_q = double_round(normalize(cross_pre) * head_set[2])
    context = jnp.concatenate([clip_part * keep_text, double_round(matmul(mt5_part, w_text)) * keep_text], 0)
    text_kv = low_back(matmul(context, w_ckv)).reshape(CLIP_LEN + T5_LEN, 2, HEADS, HEAD_DIM)
    cross_k = low(normalize(text_kv[:, 0]) * head_set[3])
    cross_v = low(text_kv[:, 1])
    cross_o = double_round(attend(cross_q, cross_k, cross_v).reshape(SEQ_LEN, D))
    resid = resid + low_back(matmul(cross_o, w_cout))
    normed = low(normalize(resid) * norm_set[3])
    upper = low_back(matmul(normed, w_up))
    active = low(jax.nn.gelu(upper, approximate=True))
    return resid + low_back(matmul(active, w_down))

def reference(hidden_in, skip_in, clip_text, mt5_text, time_ids, null_text, loss_weight, patch_pos, out_cot, skip_weight, time_first, time_second, attn_qkv, attn_out, cross_qproj, cross_kvproj, cross_out, text_proj, mlp_up, mlp_down, norm_gains, head_gains):
    weight_set = tuple((item.astype(jnp.float32) for item in (skip_weight, time_first, time_second, attn_qkv, attn_out, cross_qproj, cross_kvproj, cross_out, text_proj, mlp_up, mlp_down)))
    gain_set = (norm_gains, head_gains)
    keep_text = (1 - null_text).astype(jnp.float32)
    pos_rows = patch_pos[0].astype(jnp.float32)
    pos_cols = patch_pos[1].astype(jnp.float32)
    clip_data = clip_text.astype(jnp.float32)
    mt5_data = mt5_text.astype(jnp.float32)

    def forward(weights_in, gains_in, hidden, skip_part):

        def one_image(items):
            return jax.checkpoint(image_forward)(weights_in, gains_in, *items)
        return lax.map(one_image, (hidden, skip_part, clip_data, mt5_data, time_ids, keep_text, pos_rows, pos_cols))
    final, pullback = jax.vjp(forward, weight_set, gain_set, hidden_in.astype(jnp.float32), skip_in.astype(jnp.float32))
    scaled_cot = out_cot.astype(jnp.float32) * loss_weight[:, None, None]
    weight_grads, gain_grads, hidden_grad, skip_grad = pullback(scaled_cot)
    return (final.astype(jnp.bfloat16), hidden_grad, skip_grad, weight_grads[0], weight_grads[1], weight_grads[2], weight_grads[3], weight_grads[4], weight_grads[5], weight_grads[6], weight_grads[7], weight_grads[8], weight_grads[9], weight_grads[10], gain_grads[0], gain_grads[1])
```

```python
import math

import jax
import jax.numpy as jnp
from jax import lax
from jax.sharding import PartitionSpec as P

HEADS = 16
HEAD_DIM = 88
FREQ = 256


EPSILON = 1e-06
HIGHEST = lax.Precision.HIGHEST


def normalize(values):
    center = values - jnp.mean(values, axis=-1, keepdims=True)
    variance = jnp.mean(center * center, axis=-1, keepdims=True)
    return center * lax.rsqrt(variance + EPSILON)


def scaled_norm(values, gain_row):
    return normalize(values) * gain_row


def rotate(values, pos_rows, pos_cols):
    quarter = values.shape[-1] // 4
    frequency = 10000.0 ** (-jnp.arange(quarter, dtype=jnp.float32) / quarter)

    def turn(halfpart, position):
        angles = position[:, None] * frequency[None, :]
        cosine = jnp.cos(angles)[:, None, :]
        sine_part = jnp.sin(angles)[:, None, :]
        former = halfpart[..., :quarter]
        latter = halfpart[..., quarter:]
        return jnp.concatenate(
            [former * cosine - latter * sine_part, former * sine_part + latter * cosine], -1
        )

    return jnp.concatenate(
        [turn(values[..., : 2 * quarter], pos_rows), turn(values[..., 2 * quarter :], pos_cols)], -1
    )


def time_features(step_ids):
    half_count = FREQ // 2
    frequency = jnp.exp(-math.log(10000.0) * jnp.arange(half_count, dtype=jnp.float32) / half_count)
    angles = step_ids.astype(jnp.float32)[:, None] * frequency[None, :]
    return jnp.concatenate([jnp.cos(angles), jnp.sin(angles)], -1)


def project(left, right):
    return jnp.einsum("tc,cd->td", left, right, preferred_element_type=jnp.float32)


def project_back(grad_low, right):
    return jnp.einsum("td,cd->tc", grad_low, right, preferred_element_type=jnp.float32)


def weight_grad(left, grad_low):
    return jnp.einsum("tc,td->cd", left, grad_low, preferred_element_type=jnp.float32)


def body(
    hidden_in,
    skip_in,
    clip_text,
    mt5_text,
    time_ids,
    null_text,
    loss_weight,
    patch_pos,
    out_cot,
    skip_weight,
    time_first,
    time_second,
    attn_qkv,
    attn_out,
    cross_qproj,
    cross_kvproj,
    cross_out,
    text_proj,
    mlp_up,
    mlp_down,
    norm_gains,
    head_gains,
):
    images, local, width = hidden_in.shape
    groups = lax.axis_size("seq")
    heads_here = HEADS // groups
    narrow = width // groups
    tokens = images * local
    full_len = local * groups
    clip_len = clip_text.shape[1]
    text_len = clip_len + mt5_text.shape[1]
    score_scale = HEAD_DIM ** (-0.5)
    pos_rows = patch_pos[0].reshape(tokens).astype(jnp.float32)
    pos_cols = patch_pos[1].reshape(tokens).astype(jnp.float32)
    col_full = (
        lax.all_gather(skip_weight, "seq", axis=1, tiled=True),
        lax.all_gather(time_first, "seq", axis=1, tiled=True),
        lax.all_gather(time_second, "seq", axis=1, tiled=True),
        lax.all_gather(attn_qkv, "seq", axis=1, tiled=True),
        lax.all_gather(attn_out, "seq", axis=1, tiled=True),
        lax.all_gather(cross_qproj, "seq", axis=1, tiled=True),
        lax.all_gather(cross_kvproj, "seq", axis=1, tiled=True),
        lax.all_gather(cross_out, "seq", axis=1, tiled=True),
        lax.all_gather(text_proj, "seq", axis=1, tiled=True),
        lax.all_gather(mlp_up, "seq", axis=1, tiled=True),
        lax.all_gather(mlp_down, "seq", axis=1, tiled=True),
    )
    weight_set = (
        lax.all_gather(col_full[0], "dp", axis=0, tiled=True),
        lax.all_gather(col_full[1], "dp", axis=0, tiled=True),
        lax.all_gather(col_full[2], "dp", axis=0, tiled=True),
        lax.all_gather(col_full[3], "dp", axis=0, tiled=True),
        lax.all_gather(col_full[4], "dp", axis=0, tiled=True),
        lax.all_gather(col_full[5], "dp", axis=0, tiled=True),
        lax.all_gather(col_full[6], "dp", axis=0, tiled=True),
        lax.all_gather(col_full[7], "dp", axis=0, tiled=True),
        lax.all_gather(col_full[8], "dp", axis=0, tiled=True),
        lax.all_gather(col_full[9], "dp", axis=0, tiled=True),
        lax.all_gather(col_full[10], "dp", axis=0, tiled=True),
    )
    w_skip, w_first, w_second, w_qkv, w_aout, w_cq, w_ckv, w_cout, w_text, w_up, w_down = weight_set
    joined = jnp.concatenate([hidden_in, skip_in], -1).reshape(tokens, 2 * width)
    merged = project(joined, w_skip)
    resid0 = scaled_norm(merged, norm_gains[0])
    feats = time_features(time_ids).astype(jnp.bfloat16)
    before = project(feats, w_first)
    lifted = jax.nn.silu(before).astype(jnp.bfloat16)
    shift = project(lifted, w_second)
    shift_tok = jnp.repeat(shift, local, axis=0)
    normed1 = (scaled_norm(resid0, norm_gains[1]) + shift_tok).astype(jnp.bfloat16)
    packed = project(normed1, w_qkv).reshape(tokens, 3, HEADS, HEAD_DIM)

    def query_prep(values, gain_row):
        return rotate(scaled_norm(values, gain_row), pos_rows, pos_cols)

    self_q = query_prep(packed[:, 0], head_gains[0]).astype(jnp.bfloat16)
    self_k = query_prep(packed[:, 1], head_gains[1]).astype(jnp.bfloat16)
    self_v = packed[:, 2].astype(jnp.bfloat16)
    stacked = jnp.stack([self_q, self_k, self_v], 1).reshape(images, local, 3, width)

    def self_block(operand):
        queries, keyset, valueset = operand
        scores = (
            jnp.einsum("qd,kd->qk", queries, keyset, preferred_element_type=jnp.float32)
            * score_scale
        )
        top_score = jnp.max(scores, axis=-1, keepdims=True)
        exponent = jnp.exp(scores - top_score)
        totals = jnp.sum(exponent, axis=-1, keepdims=True)
        mixed_out = jnp.einsum(
            "qk,kd->qd",
            (exponent / totals).astype(jnp.bfloat16),
            valueset,
            preferred_element_type=jnp.float32,
        )
        return (mixed_out.astype(jnp.bfloat16), (top_score + jnp.log(totals))[:, 0])

    pieces = lax.all_to_all(stacked, "seq", split_axis=3, concat_axis=1, tiled=True)
    item_count = pieces.shape[0]
    length = pieces.shape[1]
    split_heads = pieces.reshape(item_count, length, 3, heads_here, HEAD_DIM)
    triple_set = jnp.transpose(split_heads, (2, 0, 3, 1, 4)).reshape(
        3, item_count * heads_here, length, HEAD_DIM
    )
    mixed_out, logsum = lax.map(self_block, (triple_set[0], triple_set[1], triple_set[2]))
    joined_heads = jnp.transpose(
        mixed_out.reshape(item_count, heads_here, length, HEAD_DIM), (0, 2, 1, 3)
    ).reshape(item_count, length, narrow)
    returned = lax.all_to_all(joined_heads, "seq", split_axis=1, concat_axis=2, tiled=True)
    self_logsum = logsum.reshape(item_count, heads_here, length)
    attn_flat = returned.reshape(tokens, width)
    resid1 = resid0 + project(attn_flat, w_aout)
    normed2 = scaled_norm(resid1, norm_gains[2]).astype(jnp.bfloat16)
    cross_pre = project(normed2, w_cq).reshape(tokens, HEADS, HEAD_DIM)
    cross_q = (
        scaled_norm(cross_pre, head_gains[2])
        .astype(jnp.bfloat16)
        .reshape(images, local, HEADS, HEAD_DIM)
    )
    keep_text = (1 - null_text).astype(jnp.bfloat16)
    projected = jnp.einsum(
        "btc,cd->btd", mt5_text, w_text, preferred_element_type=jnp.float32
    ).astype(jnp.bfloat16)
    context = jnp.concatenate([clip_text, projected], 1) * keep_text[:, None, None]
    text_kv = jnp.einsum("btc,cd->btd", context, w_ckv, preferred_element_type=jnp.float32).reshape(
        images, text_len, 2, HEADS, HEAD_DIM
    )
    cross_k = scaled_norm(text_kv[:, :, 0], head_gains[3]).astype(jnp.bfloat16)
    cross_v = text_kv[:, :, 1].astype(jnp.bfloat16)
    cross_scores = (
        jnp.einsum("bqhd,bkhd->bhqk", cross_q, cross_k, preferred_element_type=jnp.float32)
        * score_scale
    )
    cross_top = jnp.max(cross_scores, axis=-1, keepdims=True)
    cross_exp = jnp.exp(cross_scores - cross_top)
    cross_total = jnp.sum(cross_exp, axis=-1, keepdims=True)
    cross_logsum = cross_top + jnp.log(cross_total)
    cross_mix = jnp.einsum(
        "bhqk,bkhd->bqhd",
        (cross_exp / cross_total).astype(jnp.bfloat16),
        cross_v,
        preferred_element_type=jnp.float32,
    ).astype(jnp.bfloat16)
    cross_flat = cross_mix.reshape(tokens, width)
    resid2 = resid1 + project(cross_flat, w_cout)
    normed3 = scaled_norm(resid2, norm_gains[3]).astype(jnp.bfloat16)
    upper = project(normed3, w_up)
    active = jax.nn.gelu(upper, approximate=True).astype(jnp.bfloat16)
    final = resid2 + project(active, w_down)
    block_out = final.astype(jnp.bfloat16).reshape(images, local, width)
    again_full = (
        lax.all_gather(skip_weight, "seq", axis=1, tiled=True),
        lax.all_gather(time_first, "seq", axis=1, tiled=True),
        lax.all_gather(time_second, "seq", axis=1, tiled=True),
        lax.all_gather(attn_qkv, "seq", axis=1, tiled=True),
        lax.all_gather(attn_out, "seq", axis=1, tiled=True),
        lax.all_gather(cross_qproj, "seq", axis=1, tiled=True),
        lax.all_gather(cross_kvproj, "seq", axis=1, tiled=True),
        lax.all_gather(cross_out, "seq", axis=1, tiled=True),
        lax.all_gather(text_proj, "seq", axis=1, tiled=True),
        lax.all_gather(mlp_up, "seq", axis=1, tiled=True),
        lax.all_gather(mlp_down, "seq", axis=1, tiled=True),
    )
    weight_set = (
        lax.all_gather(again_full[0], "dp", axis=0, tiled=True),
        lax.all_gather(again_full[1], "dp", axis=0, tiled=True),
        lax.all_gather(again_full[2], "dp", axis=0, tiled=True),
        lax.all_gather(again_full[3], "dp", axis=0, tiled=True),
        lax.all_gather(again_full[4], "dp", axis=0, tiled=True),
        lax.all_gather(again_full[5], "dp", axis=0, tiled=True),
        lax.all_gather(again_full[6], "dp", axis=0, tiled=True),
        lax.all_gather(again_full[7], "dp", axis=0, tiled=True),
        lax.all_gather(again_full[8], "dp", axis=0, tiled=True),
        lax.all_gather(again_full[9], "dp", axis=0, tiled=True),
        lax.all_gather(again_full[10], "dp", axis=0, tiled=True),
    )
    w_skip, w_first, w_second, w_qkv, w_aout, w_cq, w_ckv, w_cout, w_text, w_up, w_down = weight_set
    scaled_cot = (out_cot.astype(jnp.float32) * loss_weight[:, None, None]).reshape(tokens, width)
    grad_low = scaled_cot.astype(jnp.bfloat16)
    g_down = weight_grad(active, grad_low)
    d_active = project_back(grad_low, w_down)
    upper_vals, gelu_back = jax.vjp(lambda values: jax.nn.gelu(values, approximate=True), upper)
    d_upper = gelu_back(d_active)[0].astype(jnp.bfloat16)
    g_up = weight_grad(normed3, d_upper)
    d_normed3 = project_back(d_upper, w_up)
    norm_vals, norm_back = jax.vjp(scaled_norm, resid2, norm_gains[3])
    d_resid, d_gain3 = norm_back(d_normed3)
    resid_grad = scaled_cot + d_resid
    grad_low = resid_grad.astype(jnp.bfloat16)
    g_cout = weight_grad(cross_flat, grad_low)
    d_cmix = (
        project_back(grad_low, w_cout).astype(jnp.bfloat16).reshape(images, local, HEADS, HEAD_DIM)
    )
    cross_weights = jnp.exp(cross_scores - cross_logsum)
    d_cweights = jnp.einsum("bqhd,bkhd->bhqk", d_cmix, cross_v, preferred_element_type=jnp.float32)
    row_dot = jnp.sum(cross_weights * d_cweights, axis=-1, keepdims=True)
    d_cscores = (cross_weights * (d_cweights - row_dot)).astype(jnp.bfloat16)
    d_cquery = (
        jnp.einsum("bhqk,bkhd->bqhd", d_cscores, cross_k, preferred_element_type=jnp.float32)
        * score_scale
    ).astype(jnp.bfloat16)
    d_ckey = (
        jnp.einsum("bhqk,bqhd->bkhd", d_cscores, cross_q, preferred_element_type=jnp.float32)
        * score_scale
    )
    d_cval = jnp.einsum(
        "bhqk,bqhd->bkhd",
        cross_weights.astype(jnp.bfloat16),
        d_cmix,
        preferred_element_type=jnp.float32,
    )
    cq_vals, cq_back = jax.vjp(scaled_norm, cross_pre, head_gains[2])
    d_cpre, d_hgain2 = cq_back(d_cquery.astype(jnp.float32).reshape(tokens, HEADS, HEAD_DIM))
    d_cpre_low = d_cpre.reshape(tokens, width).astype(jnp.bfloat16)
    g_cquery = weight_grad(normed2, d_cpre_low)
    d_normed2 = project_back(d_cpre_low, w_cq)
    norm_vals, norm_back = jax.vjp(scaled_norm, resid1, norm_gains[2])
    d_resid, d_gain2 = norm_back(d_normed2)
    resid_grad = resid_grad + d_resid
    ck_vals, ck_back = jax.vjp(scaled_norm, text_kv[:, :, 0], head_gains[3])
    d_kpre, d_hgain3 = ck_back(d_ckey)
    d_textkv = (
        jnp.stack([d_kpre, d_cval], 2).reshape(images, text_len, 2 * width).astype(jnp.bfloat16)
    )
    g_ckv = jnp.einsum("btc,btd->cd", context, d_textkv, preferred_element_type=jnp.float32)
    d_context = jnp.einsum("btd,cd->btc", d_textkv, w_ckv, preferred_element_type=jnp.float32)
    d_proj = (d_context[:, clip_len:] * keep_text.astype(jnp.float32)[:, None, None]).astype(
        jnp.bfloat16
    )
    g_tproj = jnp.einsum("btc,btd->cd", mt5_text, d_proj, preferred_element_type=jnp.float32)
    grad_low = resid_grad.astype(jnp.bfloat16)
    g_aout = weight_grad(attn_flat, grad_low)
    d_attn = project_back(grad_low, w_aout).astype(jnp.bfloat16).reshape(images, local, width)
    d_heads = lax.all_to_all(d_attn, "seq", split_axis=2, concat_axis=1, tiled=True)

    def self_back(operand):
        queries, keyset, valueset, d_mixed, logsum = operand
        scores = (
            jnp.einsum("qd,kd->qk", queries, keyset, preferred_element_type=jnp.float32)
            * score_scale
        )
        weights = jnp.exp(scores - logsum[:, None])
        d_weights = jnp.einsum("qd,kd->qk", d_mixed, valueset, preferred_element_type=jnp.float32)
        row_sum = jnp.sum(weights * d_weights, axis=-1, keepdims=True)
        d_scores = (weights * (d_weights - row_sum)).astype(jnp.bfloat16)
        d_query = (
            jnp.einsum("qk,kd->qd", d_scores, keyset, preferred_element_type=jnp.float32)
            * score_scale
        )
        d_key = (
            jnp.einsum("qk,qd->kd", d_scores, queries, preferred_element_type=jnp.float32)
            * score_scale
        )
        d_value = jnp.einsum(
            "qk,qd->kd", weights.astype(jnp.bfloat16), d_mixed, preferred_element_type=jnp.float32
        )
        return (
            d_query.astype(jnp.bfloat16),
            d_key.astype(jnp.bfloat16),
            d_value.astype(jnp.bfloat16),
        )

    head_split = pieces.reshape(images, full_len, 3, heads_here, HEAD_DIM)
    triple_set = jnp.transpose(head_split, (2, 0, 3, 1, 4)).reshape(
        3, images * heads_here, full_len, HEAD_DIM
    )
    d_split = jnp.transpose(
        d_heads.reshape(images, full_len, heads_here, HEAD_DIM), (0, 2, 1, 3)
    ).reshape(images * heads_here, full_len, HEAD_DIM)
    d_query, d_key, d_value = lax.map(
        self_back,
        (
            triple_set[0],
            triple_set[1],
            triple_set[2],
            d_split,
            self_logsum.reshape(images * heads_here, full_len),
        ),
    )
    d_triple = jnp.stack([d_query, d_key, d_value], 0).reshape(
        3, images, heads_here, full_len, HEAD_DIM
    )
    d_triple = jnp.transpose(d_triple, (1, 3, 0, 2, 4)).reshape(images, full_len, 3, narrow)
    d_stacked = lax.all_to_all(d_triple, "seq", split_axis=1, concat_axis=3, tiled=True)
    d_packed_in = d_stacked.reshape(tokens, 3, HEADS, HEAD_DIM).astype(jnp.float32)
    q_vals, q_back = jax.vjp(query_prep, packed[:, 0], head_gains[0])
    d_qpre, d_hgain0 = q_back(d_packed_in[:, 0])
    k_vals, k_back = jax.vjp(query_prep, packed[:, 1], head_gains[1])
    d_kself, d_hgain1 = k_back(d_packed_in[:, 1])
    d_packed = (
        jnp.stack([d_qpre, d_kself, d_packed_in[:, 2]], 1)
        .reshape(tokens, 3 * width)
        .astype(jnp.bfloat16)
    )
    g_qkv = weight_grad(normed1, d_packed)
    d_normed1 = project_back(d_packed, w_qkv)
    d_shift = jnp.sum(d_normed1.reshape(images, local, width), axis=1)
    norm_vals, norm_back = jax.vjp(scaled_norm, resid0, norm_gains[1])
    d_resid, d_gain1 = norm_back(d_normed1)
    resid_grad = resid_grad + d_resid
    g_tsecond = jnp.einsum("bc,bd->cd", lifted.astype(jnp.float32), d_shift, precision=HIGHEST)
    d_lifted = jnp.einsum("bd,cd->bc", d_shift, w_second.astype(jnp.float32), precision=HIGHEST)
    silu_vals, silu_back = jax.vjp(jax.nn.silu, before)
    d_before = silu_back(d_lifted)[0]
    g_tfirst = jnp.einsum("bc,bd->cd", feats.astype(jnp.float32), d_before, precision=HIGHEST)
    norm_vals, norm_back = jax.vjp(scaled_norm, merged, norm_gains[0])
    d_merged, d_gain0 = norm_back(resid_grad)
    d_merged_low = d_merged.astype(jnp.bfloat16)
    g_skipw = weight_grad(joined, d_merged_low)
    d_joined = project_back(d_merged_low, w_skip)
    hidden_grad = d_joined[:, :width].reshape(images, local, width)
    skip_grad = d_joined[:, width:].reshape(images, local, width)
    row_sums = (
        lax.psum_scatter(
            g_skipw.astype(jnp.bfloat16), "dp", scatter_dimension=0, tiled=True
        ).astype(jnp.float32),
        lax.psum_scatter(
            g_tfirst.astype(jnp.bfloat16), "dp", scatter_dimension=0, tiled=True
        ).astype(jnp.float32),
        lax.psum_scatter(
            g_tsecond.astype(jnp.bfloat16), "dp", scatter_dimension=0, tiled=True
        ).astype(jnp.float32),
        lax.psum_scatter(g_qkv.astype(jnp.bfloat16), "dp", scatter_dimension=0, tiled=True).astype(
            jnp.float32
        ),
        lax.psum_scatter(g_aout.astype(jnp.bfloat16), "dp", scatter_dimension=0, tiled=True).astype(
            jnp.float32
        ),
        lax.psum_scatter(
            g_cquery.astype(jnp.bfloat16), "dp", scatter_dimension=0, tiled=True
        ).astype(jnp.float32),
        lax.psum_scatter(g_ckv.astype(jnp.bfloat16), "dp", scatter_dimension=0, tiled=True).astype(
            jnp.float32
        ),
        lax.psum_scatter(g_cout.astype(jnp.bfloat16), "dp", scatter_dimension=0, tiled=True).astype(
            jnp.float32
        ),
        lax.psum_scatter(
            g_tproj.astype(jnp.bfloat16), "dp", scatter_dimension=0, tiled=True
        ).astype(jnp.float32),
        lax.psum_scatter(g_up.astype(jnp.bfloat16), "dp", scatter_dimension=0, tiled=True).astype(
            jnp.float32
        ),
        lax.psum_scatter(g_down.astype(jnp.bfloat16), "dp", scatter_dimension=0, tiled=True).astype(
            jnp.float32
        ),
    )
    owned = (
        lax.psum_scatter(
            row_sums[0].astype(jnp.bfloat16), "seq", scatter_dimension=1, tiled=True
        ).astype(jnp.float32),
        lax.psum_scatter(
            row_sums[1].astype(jnp.bfloat16), "seq", scatter_dimension=1, tiled=True
        ).astype(jnp.float32),
        lax.psum_scatter(
            row_sums[2].astype(jnp.bfloat16), "seq", scatter_dimension=1, tiled=True
        ).astype(jnp.float32),
        lax.psum_scatter(
            row_sums[3].astype(jnp.bfloat16), "seq", scatter_dimension=1, tiled=True
        ).astype(jnp.float32),
        lax.psum_scatter(
            row_sums[4].astype(jnp.bfloat16), "seq", scatter_dimension=1, tiled=True
        ).astype(jnp.float32),
        lax.psum_scatter(
            row_sums[5].astype(jnp.bfloat16), "seq", scatter_dimension=1, tiled=True
        ).astype(jnp.float32),
        lax.psum_scatter(
            row_sums[6].astype(jnp.bfloat16), "seq", scatter_dimension=1, tiled=True
        ).astype(jnp.float32),
        lax.psum_scatter(
            row_sums[7].astype(jnp.bfloat16), "seq", scatter_dimension=1, tiled=True
        ).astype(jnp.float32),
        lax.psum_scatter(
            row_sums[8].astype(jnp.bfloat16), "seq", scatter_dimension=1, tiled=True
        ).astype(jnp.float32),
        lax.psum_scatter(
            row_sums[9].astype(jnp.bfloat16), "seq", scatter_dimension=1, tiled=True
        ).astype(jnp.float32),
        lax.psum_scatter(
            row_sums[10].astype(jnp.bfloat16), "seq", scatter_dimension=1, tiled=True
        ).astype(jnp.float32),
    )
    gain_totals = lax.psum(
        (
            jnp.stack([d_gain0, d_gain1, d_gain2, d_gain3], 0),
            jnp.stack([d_hgain0, d_hgain1, d_hgain2, d_hgain3], 0),
        ),
        ("dp", "seq"),
    )
    return (
        block_out,
        hidden_grad,
        skip_grad,
        owned[0],
        owned[1],
        owned[2],
        owned[3],
        owned[4],
        owned[5],
        owned[6],
        owned[7],
        owned[8],
        owned[9],
        owned[10],
        gain_totals[0],
        gain_totals[1],
    )


BOTH = ("dp", "seq")
FLIP = [(0, 1), (1, 0)]
LOG2E = 1.4426950408889634
LANES = 128


def swap(value, bit):
    return lax.ppermute(value, "dp", [(i, i ^ bit) for i in range(16)])


def swap_seq(value):
    return lax.ppermute(value, "seq", FLIP)


def core_holds(dp_index, seq_index):
    return dp_index % 2 == dp_index // 8


def seq_holds(dp_index, seq_index):
    return seq_index == dp_index // 8


def hop_pairs(holds, outward):
    pairs = []
    for i in range(16):
        for s in range(2):
            if holds(i, s):
                there = ((i ^ 8) * 2 + s, i * 2 + s)
                pairs.append(there[::-1] if outward else there)
    return pairs


def corner_pairs(outward):
    first, second = [], []
    for i in range(16):
        h = i // 8
        base = i - i % 2
        if i % 2 == 0:
            for core in range(2):
                source = (base + core) * 2 + h
                first.append((source, (base + 1 - core) * 2 + core))
            core = 1 - h
            second.append(((base + core) * 2 + h, (base + core) * 2 + 1 - h))
    if not outward:
        return [p[::-1] for p in first], [p[::-1] for p in second]
    return first, second


def pair(flag, own, other, axis=0):
    return jnp.where(
        flag == 0,
        jnp.concatenate([own, other], axis),
        jnp.concatenate([other, own], axis),
    )


def pick(flag, first, second):
    return jnp.where(flag == 0, first, second)


class Spot:
    def __init__(self):
        self.d = lax.axis_index("dp")
        self.y = lax.axis_index("seq")
        self.z = self.d // 4
        self.x = (self.d // 2) % 2
        self.c = self.d % 2
        self.b = self.z % 2
        self.h = self.z // 2


class Flow:
    def __init__(self):
        self.chains = {}
        self.done = {}

    def add(self, name, chain):
        self.chains[name] = [chain, None, next(chain)]

    def step(self, values, names):
        for name in names:
            entry = self.chains[name]
            if entry[1] is not None:
                try:
                    entry[1:] = [None, entry[0].send(entry[1])]
                except StopIteration as end:
                    self.done[name] = end.value
                    del self.chains[name]
        moving = [name for name in names if name in self.chains]
        arrays = [[array for _, array in self.chains[name][2]] for name in moving]
        ended = [self.done[name] for name in names if name in self.done]
        values, arrays, ended = lax.optimization_barrier((list(values), arrays, ended))
        for name, value in zip([n for n in names if n in self.done], ended):
            self.done[name] = value
        for name, given in zip(moving, arrays):
            entry = self.chains[name]
            entry[1] = [route(array) for (route, _), array in zip(entry[2], given)]
        return values

    def finish(self, name):
        while name in self.chains:
            self.step([], [name])
        return self.done[name]


def by_core(value):
    return swap(value, 1)


def by_x(value):
    return swap(value, 2)


def by_z(value):
    return swap(value, 4)


def by_routes(pairs):
    return lambda value: lax.ppermute(value, BOTH, pairs)


def join(parts):
    if len(parts) == 1:
        return parts[0].astype(jnp.bfloat16)
    return jnp.concatenate([part.astype(jnp.float32) for part in parts], axis=1).astype(
        jnp.bfloat16
    )


def assemble(spot, sources, spans, over_seq, x_first):
    count = len(sources) // 2

    def piece(level, i, j):
        near = sources[level * count : (level + 1) * count]
        if not over_seq:
            return choose(choose(near[0], 0, i), 0, j)
        if x_first:
            parts = [choose(choose(source, 0, i), 0, j) for source in near]
        else:
            both = jnp.where(i == 0, choose(near[0], 1, j), choose(near[1], 1, j))
            parts = [both[0], both[1]]
        return pair(spot.y, parts[0], parts[1], 1)

    blocks = []
    for f in range(2):
        for j in range(2):
            for i in range(2):
                place = i ^ spot.x, j ^ spot.b
                blocks.append(jnp.where(spot.c == f, piece(0, *place), piece(1, *place)))
    outs, at = [], 0
    for span in spans:
        outs.append(jnp.concatenate([block[at : at + span] for block in blocks], 0))
        at += span
    return outs


def assemble_columns(spot, own, other):
    whole = pair(spot.c, own, other, 2)
    return pair(spot.b, whole[0], whole[1], 0)


def gather_rows(spot, shards):
    mates = yield [(by_core, shard) for shard in shards]
    blocks = [pair(spot.c, s, m) for s, m in zip(shards, mates)]
    hop = by_routes(hop_pairs(core_holds, True))
    fars = yield [(hop, block) for block in blocks]
    blocks = [jnp.where(spot.c == spot.h, block, far) for block, far in zip(blocks, fars)]
    nears = yield [(by_z, block) for block in blocks]
    lines = [jnp.stack([block, near]) for block, near in zip(blocks, nears)]
    sides = yield [(by_x, line) for line in lines]
    owns = [jnp.stack([line, side]) for line, side in zip(lines, sides)]
    fars = yield [(by_core, own) for own in owns]
    return [
        assemble(spot, [own, far], [own.shape[2]], False, True)[0] for own, far in zip(owns, fars)
    ]


def gather_both(spot, shards, x_first):
    mates = yield [(by_core, jnp.concatenate(shards, 0))]
    at, blocks = 0, []
    for shard in shards:
        rows = shard.shape[0]
        blocks.append(pair(spot.c, shard, mates[0][at : at + rows]))
        at += rows
    block = jnp.concatenate(blocks, 0)
    (far,) = yield [(by_routes(hop_pairs(core_holds, True)), block)]
    block = jnp.where(spot.c == spot.h, block, far)
    (near,) = yield [(by_z, block)]
    line = jnp.stack([block, near])
    (side,) = yield [(by_x if x_first else swap_seq, line)]
    own = jnp.stack([line, side])
    (other,) = yield [(swap_seq if x_first else by_x, own)]
    fars = yield [(by_core, own), (by_core, other)]
    return assemble(spot, [own, other, *fars], [b.shape[0] for b in blocks], True, x_first)


def gather_down(spot, shard):
    first, second = corner_pairs(False)
    crossed, across = yield [(by_routes(first), shard), (by_routes(second), shard)]
    mine = jnp.where(spot.c == spot.y, shard, across)
    block = pair(spot.c, mine, crossed)
    (far,) = yield [(by_routes(hop_pairs(seq_holds, True)), block)]
    block = jnp.where(spot.y == spot.h, block, far)
    (near,) = yield [(by_z, block)]
    line = jnp.stack([block, near])
    (side,) = yield [(by_x, line)]
    own = pair(spot.x, line, side, 1)
    (other,) = yield [(by_core, own)]
    return assemble_columns(spot, own, other)


def narrow(value):
    return value.astype(jnp.bfloat16)


def wide(value):
    return value.astype(jnp.float32)


def choose(value, axis, index):
    return lax.dynamic_index_in_dim(value, index, axis, keepdims=False)


def dot_rows(left, right):
    return jnp.einsum("tc,td->cd", left, right, preferred_element_type=jnp.float32)


def settle_x(spot, part):
    (given,) = yield [(by_x, choose(part, 1, 1 - spot.x))]
    return narrow(wide(choose(part, 1, spot.x)) + wide(given))


def settle_z(spot, part, holds):
    (given,) = yield [(by_z, choose(part, 0, 1 - spot.b))]
    block = wide(choose(part, 0, spot.b)) + wide(given)
    (given,) = yield [(by_routes(hop_pairs(holds, False)), narrow(block))]
    return block + wide(given)


def split_rows(spot, block):
    pieces = block.reshape(2, block.shape[0] // 2, block.shape[1])
    (given,) = yield [(by_core, narrow(choose(pieces, 0, 1 - spot.c)))]
    return jnp.where(spot.c == spot.h, choose(pieces, 0, spot.c), wide(given))


def quarters(own):
    rows, cols = own.shape
    return own.reshape(2, 2, rows // 4, cols)


def reduce_both(spot, halves, grads):
    mine = pick(spot.c, halves[0], halves[1])
    theirs = pick(spot.c, halves[1], halves[0])
    grad_own = pick(spot.y, grads[0], grads[1])
    grad_other = pick(spot.y, grads[1], grads[0])
    given = yield [(by_core, narrow(dot_rows(theirs, g))) for g in (grad_own, grad_other)]
    own = dot_rows(mine, grad_own) + wide(given[0])
    other = dot_rows(mine, grad_other) + wide(given[1])
    (given,) = yield [(swap_seq, narrow(other))]
    part = quarters(narrow(own + wide(given)))
    part = yield from settle_x(spot, part)
    block = yield from settle_z(spot, part, core_holds)
    return (yield from split_rows(spot, block))


def reduce_rows(spot, halves, grad):
    mine = pick(spot.c, halves[0], halves[1])
    theirs = pick(spot.c, halves[1], halves[0])
    (given,) = yield [(by_core, narrow(dot_rows(theirs, grad)))]
    part = quarters(narrow(dot_rows(mine, grad) + wide(given)))
    part = yield from settle_x(spot, part)
    block = yield from settle_z(spot, part, core_holds)
    return (yield from split_rows(spot, block))


def reduce_down(spot, left, grads):
    mine = pick(spot.c, grads[0], grads[1])
    theirs = pick(spot.c, grads[1], grads[0])
    (given,) = yield [(by_core, narrow(dot_rows(left, theirs)))]
    part = quarters(narrow(dot_rows(left, mine) + wide(given)))
    part = yield from settle_x(spot, part)
    block = yield from settle_z(spot, part, seq_holds)
    pieces = block.reshape(2, block.shape[0] // 2, block.shape[1])
    same, cross = choose(pieces, 0, spot.c), choose(pieces, 0, 1 - spot.c)
    first, second = corner_pairs(True)
    crossed, across = yield [(by_routes(first), narrow(cross)), (by_routes(second), narrow(same))]
    inner = jnp.where(spot.y == spot.h, same, wide(across))
    return jnp.where(spot.c == spot.y, inner, wide(crossed))


def total_over_all(value):
    for bit in (1, 2, 4, 8):
        value = value + swap(value, bit)
    return value + swap_seq(value)


def gather_images(spot, value):
    for bit, flag in ((1, spot.c), (2, spot.x), (4, spot.b), (8, spot.h)):
        value = pair(flag, value, swap(value, bit))
    return value


def partner(lane):
    quarter = HEAD_DIM // 4
    return jnp.where((lane // quarter) % 2 == 0, lane + quarter, lane - quarter)


def attend(q_src, kv_src, gains, cosine, sine, heads, q_at, k_at, v_at, keys):
    width = heads * HEAD_DIM

    def heads_of(source, at):
        return source[:, at : at + width].reshape(source.shape[0], heads, HEAD_DIM)

    def prepared(source, at, which):
        v = normalize(heads_of(source, at)) * gains[which]
        if cosine is not None:
            other = v[..., partner(jnp.arange(HEAD_DIM))]
            v = v * cosine[:, None, :HEAD_DIM] + other * sine[:, None, :HEAD_DIM]
        return v.astype(jnp.bfloat16)

    q, k = prepared(q_src, q_at, 0), prepared(kv_src, k_at, 1)
    v = heads_of(kv_src, v_at).astype(jnp.bfloat16)
    s = jnp.einsum("qhd,khd->hqk", q, k, preferred_element_type=jnp.float32) * HEAD_DIM**-0.5
    s = jnp.where(jnp.arange(kv_src.shape[0]) < keys, s, -1e9)
    p = jax.nn.softmax(s, axis=-1).astype(jnp.bfloat16)
    o = jnp.einsum("hqk,khd->qhd", p, v, preferred_element_type=jnp.float32)
    return o.reshape(q_src.shape[0], width)


def attend_forward(
    q_src, kv_src, cosine, sine, gains, helpers, heads, q_at, k_at, v_at, keys
):
    q32, kv32 = q_src.astype(jnp.float32), kv_src.astype(jnp.float32)
    o, back = jax.vjp(
        lambda a, b, g: attend(a, b, g, cosine, sine, heads, q_at, k_at, v_at, keys),
        q32,
        kv32,
        gains[:2, :HEAD_DIM],
    )
    return narrow(o), back, None, None


def attend_backward(
    q_src, kv_src, cosine, sine, gains, helpers, back, kn, vn, out, grad_out, heads, q_at, k_at, v_at
):
    dq, dk, dg = back(grad_out.astype(jnp.float32))
    dg = jnp.pad(dg * gains[:2, :HEAD_DIM], ((0, 0), (0, LANES - HEAD_DIM)))
    if q_src is kv_src:
        return narrow(dq + dk), dg
    return narrow(dq), narrow(dk), dg


def rope_tables(pos_rows, pos_cols):
    quarter = HEAD_DIM // 4
    frequency = 10000.0 ** (-jnp.arange(quarter, dtype=jnp.float32) / quarter)
    row_angles = pos_rows[:, None] * frequency[None, :]
    col_angles = pos_cols[:, None] * frequency[None, :]
    angles = jnp.concatenate([row_angles, row_angles, col_angles, col_angles], -1)
    sign = jnp.where((jnp.arange(HEAD_DIM) // quarter) % 2 == 0, -1.0, 1.0)
    wide = ((0, 0), (0, LANES - HEAD_DIM))
    return jnp.pad(jnp.cos(angles), wide), jnp.pad(jnp.sin(angles) * sign[None, :], wide)


def gain_rows(gains):
    lane = jnp.arange(HEAD_DIM)
    return jnp.pad(
        jnp.concatenate([gains, gains[:, partner(lane)]], 0), ((0, 0), (0, LANES - HEAD_DIM))
    )


def gelu(values):
    return jax.nn.gelu(values, approximate=True)


def halves_of(value):
    mid = value.shape[1] // 2
    return value[:, :mid], value[:, mid:]


def norm_parts(values):
    center = values - jnp.mean(values, axis=-1, keepdims=True)
    scale = lax.rsqrt(jnp.mean(center * center, axis=-1, keepdims=True) + EPSILON)
    return center * scale, scale


def norm_grad(grad, values, gain):
    normal, scale = norm_parts(values)
    gain_grad = jnp.sum(grad * normal, axis=0)
    grad = grad * gain
    mean = jnp.mean(grad, axis=-1, keepdims=True)
    mean_product = jnp.mean(grad * normal, axis=-1, keepdims=True)
    return scale * (grad - mean - normal * mean_product), gain_grad


def fast_body(
    hidden_in,
    skip_in,
    clip_text,
    mt5_text,
    time_ids,
    null_text,
    loss_weight,
    patch_pos,
    out_cot,
    skip_weight,
    time_first,
    time_second,
    attn_qkv,
    attn_out,
    cross_qproj,
    cross_kvproj,
    cross_out,
    text_proj,
    mlp_up,
    mlp_down,
    norm_gains,
    head_gains,
):
    spot = Spot()
    _, local, width = hidden_in.shape
    narrow_width = width // 2
    heads_here = HEADS // 2
    clip_len = clip_text.shape[1]
    text_len = clip_len + mt5_text.shape[1]
    text_pad = -(-text_len // LANES) * LANES
    y = spot.y
    bf16 = jnp.bfloat16

    time_rows = lax.all_gather(jnp.concatenate([time_first, time_second], 0), "dp")
    time_cut = time_first.shape[0]
    time_weights = [
        rows.reshape(-1, narrow_width) for rows in (time_rows[:, :time_cut], time_rows[:, time_cut:])
    ]
    flow = Flow()
    hidden = hidden_in[0]
    skip = skip_in[0]
    scaled_cot = out_cot[0].astype(jnp.float32) * loss_weight[0]
    cot_low = narrow(scaled_cot)
    pos = patch_pos[:, 0].astype(jnp.float32)
    pos_far = swap_seq(pos)

    def both_halves(value, axis=1):
        return pair(y, value, swap_seq(value), axis)

    a, m, e = (attn_qkv[:, i * narrow_width : (i + 1) * narrow_width] for i in range(3))
    moved = swap_seq(m)
    qkv_shard = jnp.concatenate([pick(y, a, moved), pick(y, e, a), pick(y, moved, e)], 1)

    flow.add("skip", gather_both(spot, [skip_weight], False))
    flow.add("qkv", gather_rows(spot, [qkv_shard]))
    flow.add("text", gather_rows(spot, [text_proj, cross_kvproj]))
    flow.add("outs", gather_both(spot, [attn_out, cross_qproj, cross_out], False))
    flow.add("up", gather_rows(spot, [mlp_up]))
    flow.add("down", gather_down(spot, mlp_down))
    flow.step([], ["skip", "qkv", "text", "outs", "up", "down"])
    flow.step([], ["skip"])
    flow.step([], ["skip", "qkv"])
    flow.step([], ["skip", "qkv", "text"])
    cot_far = swap_seq(cot_low)
    flow.step([], ["skip", "text", "outs"])
    flow.step([], ["skip", "qkv", "outs", "up"])

    feats = time_features(time_ids).astype(bf16)
    before = both_halves(project(feats, time_weights[0]))
    lifted = jax.nn.silu(before).astype(bf16)
    shift = both_halves(project(lifted, time_weights[1]))

    cosine, sine = rope_tables(*jnp.concatenate([pos, pos_far], 1))
    helpers = []
    hidden, skip, cot_far = flow.step([hidden, skip, cot_far], ["skip", "qkv", "text", "outs"])
    (w_skip,) = flow.done["skip"]
    w_hidden, w_far = w_skip[:width], w_skip[width:]
    merged = project(hidden, w_hidden) + project(skip, w_far)
    resid0 = scaled_norm(merged, norm_gains[0])
    normed1 = narrow(scaled_norm(resid0, norm_gains[1]) + shift)
    (normed1,) = flow.step([normed1], ["qkv", "text", "up", "down"])
    (w_qkv,) = flow.done["qkv"]

    normed1_both = jnp.concatenate([normed1, swap_seq(normed1)], 0)
    packed = narrow(project(normed1_both, w_qkv))
    self_gains = gain_rows(head_gains[0:2])
    (packed,) = flow.step([packed], ["outs", "down", "text"])
    self_o, self_q, self_k, self_v = attend_forward(
        packed,
        packed,
        cosine,
        sine,
        self_gains,
        helpers,
        heads_here,
        0,
        narrow_width,
        2 * narrow_width,
        2 * local,
    )
    (self_o,) = flow.step([self_o], ["outs", "up", "down"])
    far_o = swap_seq(self_o[local:])

    w_text, w_ckv = flow.done["text"]
    keep_text = (1 - null_text[0]).astype(bf16)
    projected = both_halves(narrow(project(mt5_text[0], w_text)))
    context = jnp.concatenate([clip_text[0], projected], 0) * keep_text
    context = jnp.pad(context, ((0, text_pad - text_len), (0, 0)))
    text_kv = both_halves(narrow(project(context, w_ckv)))
    text_kv, own_o, far_o = flow.step([text_kv, self_o[:local], far_o], ["outs", "up", "down"])

    w_aout, w_cq, w_cout = flow.done["outs"]
    attn_halves = pick(y, own_o, far_o), pick(y, far_o, own_o)
    attn_flat = jnp.concatenate(attn_halves, 1)
    resid1 = resid0 + project(attn_flat, w_aout)
    normed2 = narrow(scaled_norm(resid1, norm_gains[2]))
    cross_pre = narrow(project(normed2, w_cq))
    cross_gains = gain_rows(head_gains[2:4])
    cross_o, cross_q, cross_k, cross_v = attend_forward(
        cross_pre, text_kv, None, None, cross_gains, helpers, HEADS, 0, 0, width, text_len
    )
    resid2 = resid1 + project(cross_o, w_cout)
    normed3 = narrow(scaled_norm(resid2, norm_gains[3]))
    (normed3,) = flow.step([normed3], ["up", "down"])
    w_up, w_down = flow.finish("up")[0], flow.finish("down")

    normed3_both = jnp.concatenate([normed3, swap_seq(normed3)], 0)
    upper = narrow(project(normed3_both, w_up))
    active = narrow(gelu(upper.astype(jnp.float32)))
    mixed = project(active, w_down)
    final = resid2 + mixed[:local] + wide(swap_seq(narrow(mixed[local:])))
    block_out = narrow(lax.optimization_barrier(final))[None]

    cot_both = jnp.concatenate([cot_low, cot_far], 0)
    d_active = project_back(cot_both, w_down)
    _, gelu_back = jax.vjp(gelu, upper.astype(jnp.float32))
    d_upper = narrow(gelu_back(d_active)[0])
    flow.add("g_down", reduce_down(spot, active, halves_of(cot_both)))
    (d_upper,) = flow.step([d_upper], ["g_down"])
    d_both = project_back(d_upper, w_up)
    d_far = swap_seq(narrow(d_both[local:]))
    flow.add("g_up", reduce_rows(spot, halves_of(normed3_both), d_upper))
    d_own, d_far = flow.step([d_both[:local], d_far], ["g_down", "g_up"])
    d_normed3 = d_own + wide(d_far)
    d_resid, d_gain3 = norm_grad(d_normed3, resid2, norm_gains[3])
    resid_grad = scaled_cot + d_resid

    grad_low = narrow(resid_grad)
    d_cmix = narrow(project_back(grad_low, w_cout))
    flow.add("g_cout", reduce_both(spot, halves_of(cross_o), halves_of(grad_low)))
    (d_cmix,) = flow.step([d_cmix], ["g_cout"])
    d_cpre, d_textkv, d_cross_gains = attend_backward(
        cross_pre,
        text_kv,
        None,
        None,
        cross_gains,
        helpers,
        cross_q,
        cross_k,
        cross_v,
        cross_o,
        d_cmix,
        HEADS,
        0,
        0,
        width,
    )
    flow.add("g_cquery", reduce_both(spot, halves_of(normed2), halves_of(d_cpre)))
    d_cpre, d_textkv = flow.step([d_cpre, d_textkv], ["g_down", "g_up", "g_cout", "g_cquery"])
    d_text = halves_of(d_textkv)
    d_text_far = swap_seq(pick(y, d_text[1], d_text[0]))
    d_normed2 = project_back(d_cpre, w_cq)
    d_resid, d_gain2 = norm_grad(d_normed2, resid1, norm_gains[2])
    resid_grad = resid_grad + d_resid
    grad_low = narrow(resid_grad)
    d_attn = halves_of(narrow(project_back(grad_low, w_aout)))
    d_far = swap_seq(pick(y, d_attn[1], d_attn[0]))
    d_text = narrow(wide(pick(y, d_text[0], d_text[1])) + wide(d_text_far))
    flow.add("g_aout", reduce_both(spot, attn_halves, halves_of(grad_low)))
    flow.add("g_ckv", reduce_rows(spot, halves_of(context), d_text))
    d_context = halves_of(project_back(d_text[clip_len:text_len], w_ckv))
    d_context_far = swap_seq(narrow(pick(y, d_context[1], d_context[0])))
    d_proj = pick(y, d_context[0], d_context[1]) + wide(d_context_far)
    d_proj = narrow(d_proj * keep_text.astype(jnp.float32))
    flow.add("g_tproj", reduce_rows(spot, halves_of(mt5_text[0]), d_proj))

    d_heads = jnp.concatenate([pick(y, d_attn[0], d_attn[1]), d_far], 0)
    (d_heads,) = flow.step(
        [d_heads], ["g_down", "g_cout", "g_cquery", "g_aout", "g_ckv", "g_tproj"]
    )
    d_packed, d_self_gains = attend_backward(
        packed,
        packed,
        cosine,
        sine,
        self_gains,
        helpers,
        self_q,
        self_k,
        self_v,
        self_o,
        d_heads,
        heads_here,
        0,
        narrow_width,
        2 * narrow_width,
    )
    (d_packed,) = flow.step(
        [d_packed], ["g_down", "g_up", "g_cout", "g_cquery", "g_aout", "g_ckv", "g_tproj"]
    )
    d_both = project_back(d_packed, w_qkv)
    d_far = swap_seq(narrow(d_both[local:]))
    flow.add("g_qkv", reduce_rows(spot, halves_of(normed1_both), d_packed))
    d_own, d_far = flow.step(
        [d_both[:local], d_far],
        ["g_up", "g_cout", "g_cquery", "g_aout", "g_ckv", "g_tproj", "g_qkv"],
    )
    d_normed1 = d_own + wide(d_far)

    d_shift = jnp.sum(d_normed1, axis=0)
    d_resid, d_gain1 = norm_grad(d_normed1, resid0, norm_gains[1])
    resid_grad = resid_grad + d_resid
    d_merged, d_gain0 = norm_grad(resid_grad, merged, norm_gains[0])
    d_merged = narrow(d_merged)
    flow.add("g_skip", reduce_both(spot, (hidden, skip), halves_of(d_merged)))
    (d_merged,) = flow.step(
        [d_merged],
        ["g_skip", "g_up", "g_cout", "g_cquery", "g_aout", "g_ckv", "g_tproj", "g_qkv"],
    )
    hidden_grad = project_back(d_merged, w_hidden)[None]
    skip_grad = project_back(d_merged, w_far)[None]

    d_shift = d_shift + swap_seq(d_shift)
    features = jnp.pad(feats.astype(jnp.float32), ((0, 0), (0, width - FREQ)))
    rows = gather_images(spot, jnp.stack([before[0], features[0], d_shift], 0)[None])
    before_all, features_all, d_shift_all = rows[:, 0], rows[:, 1, :FREQ], rows[:, 2]
    silu_all, silu_back = jax.vjp(jax.nn.silu, before_all)
    lifted_all = wide(narrow(silu_all))
    d_shift_cols = pick(y, *halves_of(d_shift_all))
    d_lifted = jnp.einsum(
        "bd,cd->bc", d_shift_cols, time_weights[1].astype(jnp.float32), precision=HIGHEST
    )
    d_before = silu_back(d_lifted + swap_seq(d_lifted))[0]

    def block(left, cols, left_rows):
        mine = lax.dynamic_slice_in_dim(left, spot.d * left_rows, left_rows, 1)
        return jnp.einsum("bc,bd->cd", mine, cols, precision=HIGHEST)

    g_tsecond = block(lifted_all, d_shift_cols, time_second.shape[0])
    g_tfirst = block(features_all, pick(y, *halves_of(d_before)), time_first.shape[0])

    d_head_gains = jnp.concatenate([d_self_gains, d_cross_gains], 0)[:, :HEAD_DIM] / head_gains
    d_norm_gains = jnp.stack([d_gain0, d_gain1, d_gain2, d_gain3], 0)
    totals = total_over_all(
        jnp.concatenate([d_norm_gains.reshape(-1), d_head_gains.reshape(-1)])
    )
    norm_total = totals[: 4 * width].reshape(4, width)
    head_total = totals[4 * width :].reshape(4, HEAD_DIM)

    while flow.chains:
        flow.step([], list(flow.chains))
    names = ["skip", "qkv", "aout", "cquery", "ckv", "cout", "tproj", "up", "down"]
    g_skipw, g_qkv, g_aout, g_cquery, g_ckv, g_cout, g_tproj, g_up, g_down = (
        flow.done["g_" + name] for name in names
    )
    q_cols, k_cols, v_cols = (
        g_qkv[:, i * narrow_width : (i + 1) * narrow_width] for i in range(3)
    )
    moved = wide(swap_seq(narrow(pick(y, v_cols, q_cols))))
    g_qkv = jnp.concatenate([pick(y, q_cols, k_cols), moved, pick(y, k_cols, v_cols)], 1)
    return (
        block_out,
        hidden_grad,
        skip_grad,
        g_skipw,
        g_tfirst,
        g_tsecond,
        g_qkv,
        g_aout,
        g_cquery,
        g_ckv,
        g_cout,
        g_tproj,
        g_up,
        g_down,
        norm_total,
        head_total,
    )


def solution(mesh):
    placed = (
        P("dp", "seq", None),
        P("dp", "seq", None),
        P("dp", None, None),
        P("dp", None, None),
        P("dp"),
        P("dp"),
        P("dp"),
        P(None, "dp", "seq"),
        P("dp", "seq", None),
        P("dp", "seq"),
        P("dp", "seq"),
        P("dp", "seq"),
        P("dp", "seq"),
        P("dp", "seq"),
        P("dp", "seq"),
        P("dp", "seq"),
        P("dp", "seq"),
        P("dp", "seq"),
        P("dp", "seq"),
        P("dp", "seq"),
        P(),
        P(),
    )
    split = mesh.shape["dp"] == 16 and mesh.shape["seq"] == 2
    return jax.shard_map(
        fast_body if split else body,
        mesh=mesh,
        in_specs=placed,
        out_specs=(
            P("dp", "seq", None),
            P("dp", "seq", None),
            P("dp", "seq", None),
            P("dp", "seq"),
            P("dp", "seq"),
            P("dp", "seq"),
            P("dp", "seq"),
            P("dp", "seq"),
            P("dp", "seq"),
            P("dp", "seq"),
            P("dp", "seq"),
            P("dp", "seq"),
            P("dp", "seq"),
            P("dp", "seq"),
            P(),
            P(),
        ),
        check_vma=False,
    )
```

```python
import math

import jax
import jax.numpy as jnp
from jax import lax
from jax.sharding import PartitionSpec as P

DP = "dp"
SEQ = "seq"
HEADS = 16
HEAD_DIM = 88
FREQ = 256


EPSILON = 1e-06
HIGHEST = lax.Precision.HIGHEST


def normalize(values):
    center = values - jnp.mean(values, axis=-1, keepdims=True)
    variance = jnp.mean(center * center, axis=-1, keepdims=True)
    return center * lax.rsqrt(variance + EPSILON)


def scaled_norm(values, gain_row):
    return normalize(values) * gain_row


def rotate(values, pos_rows, pos_cols):
    quarter = values.shape[-1] // 4
    frequency = 10000.0 ** (-jnp.arange(quarter, dtype=jnp.float32) / quarter)

    def turn(halfpart, position):
        angles = position[:, None] * frequency[None, :]
        cosine = jnp.cos(angles)[:, None, :]
        sine_part = jnp.sin(angles)[:, None, :]
        former = halfpart[..., :quarter]
        latter = halfpart[..., quarter:]
        return jnp.concatenate(
            [former * cosine - latter * sine_part, former * sine_part + latter * cosine], -1
        )

    return jnp.concatenate(
        [turn(values[..., : 2 * quarter], pos_rows), turn(values[..., 2 * quarter :], pos_cols)], -1
    )


def time_features(step_ids):
    half_count = FREQ // 2
    frequency = jnp.exp(-math.log(10000.0) * jnp.arange(half_count, dtype=jnp.float32) / half_count)
    angles = step_ids.astype(jnp.float32)[:, None] * frequency[None, :]
    return jnp.concatenate([jnp.cos(angles), jnp.sin(angles)], -1)


def project(left, right):
    return jnp.einsum("tc,cd->td", left, right, preferred_element_type=jnp.float32)


def project_back(grad_low, right):
    return jnp.einsum("td,cd->tc", grad_low, right, preferred_element_type=jnp.float32)


def weight_grad(left, grad_low):
    return jnp.einsum("tc,td->cd", left, grad_low, preferred_element_type=jnp.float32)


def whole_body(
    hidden_in,
    skip_in,
    clip_text,
    mt5_text,
    time_ids,
    null_text,
    loss_weight,
    patch_pos,
    out_cot,
    skip_weight,
    time_first,
    time_second,
    attn_qkv,
    attn_out,
    cross_qproj,
    cross_kvproj,
    cross_out,
    text_proj,
    mlp_up,
    mlp_down,
    norm_gains,
    head_gains,
):
    images, local, width = hidden_in.shape
    groups = lax.axis_size(SEQ)
    heads_here = HEADS // groups
    narrow = width // groups
    tokens = images * local
    full_len = local * groups
    clip_len = clip_text.shape[1]
    text_len = clip_len + mt5_text.shape[1]
    score_scale = HEAD_DIM ** (-0.5)
    pos_rows = patch_pos[0].reshape(tokens).astype(jnp.float32)
    pos_cols = patch_pos[1].reshape(tokens).astype(jnp.float32)
    col_full = (
        lax.all_gather(skip_weight, SEQ, axis=1, tiled=True),
        lax.all_gather(time_first, SEQ, axis=1, tiled=True),
        lax.all_gather(time_second, SEQ, axis=1, tiled=True),
        lax.all_gather(attn_qkv, SEQ, axis=1, tiled=True),
        lax.all_gather(attn_out, SEQ, axis=1, tiled=True),
        lax.all_gather(cross_qproj, SEQ, axis=1, tiled=True),
        lax.all_gather(cross_kvproj, SEQ, axis=1, tiled=True),
        lax.all_gather(cross_out, SEQ, axis=1, tiled=True),
        lax.all_gather(text_proj, SEQ, axis=1, tiled=True),
        lax.all_gather(mlp_up, SEQ, axis=1, tiled=True),
        lax.all_gather(mlp_down, SEQ, axis=1, tiled=True),
    )
    weight_set = (
        lax.all_gather(col_full[0], DP, axis=0, tiled=True),
        lax.all_gather(col_full[1], DP, axis=0, tiled=True),
        lax.all_gather(col_full[2], DP, axis=0, tiled=True),
        lax.all_gather(col_full[3], DP, axis=0, tiled=True),
        lax.all_gather(col_full[4], DP, axis=0, tiled=True),
        lax.all_gather(col_full[5], DP, axis=0, tiled=True),
        lax.all_gather(col_full[6], DP, axis=0, tiled=True),
        lax.all_gather(col_full[7], DP, axis=0, tiled=True),
        lax.all_gather(col_full[8], DP, axis=0, tiled=True),
        lax.all_gather(col_full[9], DP, axis=0, tiled=True),
        lax.all_gather(col_full[10], DP, axis=0, tiled=True),
    )
    w_skip, w_first, w_second, w_qkv, w_aout, w_cq, w_ckv, w_cout, w_text, w_up, w_down = weight_set
    joined = jnp.concatenate([hidden_in, skip_in], -1).reshape(tokens, 2 * width)
    merged = project(joined, w_skip)
    resid0 = scaled_norm(merged, norm_gains[0])
    feats = time_features(time_ids).astype(jnp.bfloat16)
    before = project(feats, w_first)
    lifted = jax.nn.silu(before).astype(jnp.bfloat16)
    shift = project(lifted, w_second)
    shift_tok = jnp.repeat(shift, local, axis=0)
    normed1 = (scaled_norm(resid0, norm_gains[1]) + shift_tok).astype(jnp.bfloat16)
    packed = project(normed1, w_qkv).reshape(tokens, 3, HEADS, HEAD_DIM)

    def query_prep(values, gain_row):
        return rotate(scaled_norm(values, gain_row), pos_rows, pos_cols)

    self_q = query_prep(packed[:, 0], head_gains[0]).astype(jnp.bfloat16)
    self_k = query_prep(packed[:, 1], head_gains[1]).astype(jnp.bfloat16)
    self_v = packed[:, 2].astype(jnp.bfloat16)
    stacked = jnp.stack([self_q, self_k, self_v], 1).reshape(images, local, 3, width)

    def self_block(operand):
        queries, keyset, valueset = operand
        scores = (
            jnp.einsum("qd,kd->qk", queries, keyset, preferred_element_type=jnp.float32)
            * score_scale
        )
        top_score = jnp.max(scores, axis=-1, keepdims=True)
        exponent = jnp.exp(scores - top_score)
        totals = jnp.sum(exponent, axis=-1, keepdims=True)
        mixed_out = jnp.einsum(
            "qk,kd->qd",
            (exponent / totals).astype(jnp.bfloat16),
            valueset,
            preferred_element_type=jnp.float32,
        )
        return (mixed_out.astype(jnp.bfloat16), (top_score + jnp.log(totals))[:, 0])

    pieces = lax.all_to_all(stacked, SEQ, split_axis=3, concat_axis=1, tiled=True)
    item_count = pieces.shape[0]
    length = pieces.shape[1]
    split_heads = pieces.reshape(item_count, length, 3, heads_here, HEAD_DIM)
    triple_set = jnp.transpose(split_heads, (2, 0, 3, 1, 4)).reshape(
        3, item_count * heads_here, length, HEAD_DIM
    )
    mixed_out, logsum = lax.map(self_block, (triple_set[0], triple_set[1], triple_set[2]))
    joined_heads = jnp.transpose(
        mixed_out.reshape(item_count, heads_here, length, HEAD_DIM), (0, 2, 1, 3)
    ).reshape(item_count, length, narrow)
    returned = lax.all_to_all(joined_heads, SEQ, split_axis=1, concat_axis=2, tiled=True)
    self_logsum = logsum.reshape(item_count, heads_here, length)
    attn_flat = returned.reshape(tokens, width)
    resid1 = resid0 + project(attn_flat, w_aout)
    normed2 = scaled_norm(resid1, norm_gains[2]).astype(jnp.bfloat16)
    cross_pre = project(normed2, w_cq).reshape(tokens, HEADS, HEAD_DIM)
    cross_q = (
        scaled_norm(cross_pre, head_gains[2])
        .astype(jnp.bfloat16)
        .reshape(images, local, HEADS, HEAD_DIM)
    )
    keep_text = (1 - null_text).astype(jnp.bfloat16)
    projected = jnp.einsum(
        "btc,cd->btd", mt5_text, w_text, preferred_element_type=jnp.float32
    ).astype(jnp.bfloat16)
    context = jnp.concatenate([clip_text, projected], 1) * keep_text[:, None, None]
    text_kv = jnp.einsum("btc,cd->btd", context, w_ckv, preferred_element_type=jnp.float32).reshape(
        images, text_len, 2, HEADS, HEAD_DIM
    )
    cross_k = scaled_norm(text_kv[:, :, 0], head_gains[3]).astype(jnp.bfloat16)
    cross_v = text_kv[:, :, 1].astype(jnp.bfloat16)
    cross_scores = (
        jnp.einsum("bqhd,bkhd->bhqk", cross_q, cross_k, preferred_element_type=jnp.float32)
        * score_scale
    )
    cross_top = jnp.max(cross_scores, axis=-1, keepdims=True)
    cross_exp = jnp.exp(cross_scores - cross_top)
    cross_total = jnp.sum(cross_exp, axis=-1, keepdims=True)
    cross_logsum = cross_top + jnp.log(cross_total)
    cross_mix = jnp.einsum(
        "bhqk,bkhd->bqhd",
        (cross_exp / cross_total).astype(jnp.bfloat16),
        cross_v,
        preferred_element_type=jnp.float32,
    ).astype(jnp.bfloat16)
    cross_flat = cross_mix.reshape(tokens, width)
    resid2 = resid1 + project(cross_flat, w_cout)
    normed3 = scaled_norm(resid2, norm_gains[3]).astype(jnp.bfloat16)
    upper = project(normed3, w_up)
    active = jax.nn.gelu(upper, approximate=True).astype(jnp.bfloat16)
    final = resid2 + project(active, w_down)
    block_out = final.astype(jnp.bfloat16).reshape(images, local, width)
    again_full = (
        lax.all_gather(skip_weight, SEQ, axis=1, tiled=True),
        lax.all_gather(time_first, SEQ, axis=1, tiled=True),
        lax.all_gather(time_second, SEQ, axis=1, tiled=True),
        lax.all_gather(attn_qkv, SEQ, axis=1, tiled=True),
        lax.all_gather(attn_out, SEQ, axis=1, tiled=True),
        lax.all_gather(cross_qproj, SEQ, axis=1, tiled=True),
        lax.all_gather(cross_kvproj, SEQ, axis=1, tiled=True),
        lax.all_gather(cross_out, SEQ, axis=1, tiled=True),
        lax.all_gather(text_proj, SEQ, axis=1, tiled=True),
        lax.all_gather(mlp_up, SEQ, axis=1, tiled=True),
        lax.all_gather(mlp_down, SEQ, axis=1, tiled=True),
    )
    weight_set = (
        lax.all_gather(again_full[0], DP, axis=0, tiled=True),
        lax.all_gather(again_full[1], DP, axis=0, tiled=True),
        lax.all_gather(again_full[2], DP, axis=0, tiled=True),
        lax.all_gather(again_full[3], DP, axis=0, tiled=True),
        lax.all_gather(again_full[4], DP, axis=0, tiled=True),
        lax.all_gather(again_full[5], DP, axis=0, tiled=True),
        lax.all_gather(again_full[6], DP, axis=0, tiled=True),
        lax.all_gather(again_full[7], DP, axis=0, tiled=True),
        lax.all_gather(again_full[8], DP, axis=0, tiled=True),
        lax.all_gather(again_full[9], DP, axis=0, tiled=True),
        lax.all_gather(again_full[10], DP, axis=0, tiled=True),
    )
    w_skip, w_first, w_second, w_qkv, w_aout, w_cq, w_ckv, w_cout, w_text, w_up, w_down = weight_set
    scaled_cot = (out_cot.astype(jnp.float32) * loss_weight[:, None, None]).reshape(tokens, width)
    grad_low = scaled_cot.astype(jnp.bfloat16)
    g_down = weight_grad(active, grad_low)
    d_active = project_back(grad_low, w_down)
    upper_vals, gelu_back = jax.vjp(lambda values: jax.nn.gelu(values, approximate=True), upper)
    d_upper = gelu_back(d_active)[0].astype(jnp.bfloat16)
    g_up = weight_grad(normed3, d_upper)
    d_normed3 = project_back(d_upper, w_up)
    norm_vals, norm_back = jax.vjp(scaled_norm, resid2, norm_gains[3])
    d_resid, d_gain3 = norm_back(d_normed3)
    resid_grad = scaled_cot + d_resid
    grad_low = resid_grad.astype(jnp.bfloat16)
    g_cout = weight_grad(cross_flat, grad_low)
    d_cmix = (
        project_back(grad_low, w_cout).astype(jnp.bfloat16).reshape(images, local, HEADS, HEAD_DIM)
    )
    cross_weights = jnp.exp(cross_scores - cross_logsum)
    d_cweights = jnp.einsum("bqhd,bkhd->bhqk", d_cmix, cross_v, preferred_element_type=jnp.float32)
    row_dot = jnp.sum(cross_weights * d_cweights, axis=-1, keepdims=True)
    d_cscores = (cross_weights * (d_cweights - row_dot)).astype(jnp.bfloat16)
    d_cquery = (
        jnp.einsum("bhqk,bkhd->bqhd", d_cscores, cross_k, preferred_element_type=jnp.float32)
        * score_scale
    ).astype(jnp.bfloat16)
    d_ckey = (
        jnp.einsum("bhqk,bqhd->bkhd", d_cscores, cross_q, preferred_element_type=jnp.float32)
        * score_scale
    )
    d_cval = jnp.einsum(
        "bhqk,bqhd->bkhd",
        cross_weights.astype(jnp.bfloat16),
        d_cmix,
        preferred_element_type=jnp.float32,
    )
    cq_vals, cq_back = jax.vjp(scaled_norm, cross_pre, head_gains[2])
    d_cpre, d_hgain2 = cq_back(d_cquery.astype(jnp.float32).reshape(tokens, HEADS, HEAD_DIM))
    d_cpre_low = d_cpre.reshape(tokens, width).astype(jnp.bfloat16)
    g_cquery = weight_grad(normed2, d_cpre_low)
    d_normed2 = project_back(d_cpre_low, w_cq)
    norm_vals, norm_back = jax.vjp(scaled_norm, resid1, norm_gains[2])
    d_resid, d_gain2 = norm_back(d_normed2)
    resid_grad = resid_grad + d_resid
    ck_vals, ck_back = jax.vjp(scaled_norm, text_kv[:, :, 0], head_gains[3])
    d_kpre, d_hgain3 = ck_back(d_ckey)
    d_textkv = (
        jnp.stack([d_kpre, d_cval], 2).reshape(images, text_len, 2 * width).astype(jnp.bfloat16)
    )
    g_ckv = jnp.einsum("btc,btd->cd", context, d_textkv, preferred_element_type=jnp.float32)
    d_context = jnp.einsum("btd,cd->btc", d_textkv, w_ckv, preferred_element_type=jnp.float32)
    d_proj = (d_context[:, clip_len:] * keep_text.astype(jnp.float32)[:, None, None]).astype(
        jnp.bfloat16
    )
    g_tproj = jnp.einsum("btc,btd->cd", mt5_text, d_proj, preferred_element_type=jnp.float32)
    grad_low = resid_grad.astype(jnp.bfloat16)
    g_aout = weight_grad(attn_flat, grad_low)
    d_attn = project_back(grad_low, w_aout).astype(jnp.bfloat16).reshape(images, local, width)
    d_heads = lax.all_to_all(d_attn, SEQ, split_axis=2, concat_axis=1, tiled=True)

    def self_back(operand):
        queries, keyset, valueset, d_mixed, logsum = operand
        scores = (
            jnp.einsum("qd,kd->qk", queries, keyset, preferred_element_type=jnp.float32)
            * score_scale
        )
        weights = jnp.exp(scores - logsum[:, None])
        d_weights = jnp.einsum("qd,kd->qk", d_mixed, valueset, preferred_element_type=jnp.float32)
        row_sum = jnp.sum(weights * d_weights, axis=-1, keepdims=True)
        d_scores = (weights * (d_weights - row_sum)).astype(jnp.bfloat16)
        d_query = (
            jnp.einsum("qk,kd->qd", d_scores, keyset, preferred_element_type=jnp.float32)
            * score_scale
        )
        d_key = (
            jnp.einsum("qk,qd->kd", d_scores, queries, preferred_element_type=jnp.float32)
            * score_scale
        )
        d_value = jnp.einsum(
            "qk,qd->kd", weights.astype(jnp.bfloat16), d_mixed, preferred_element_type=jnp.float32
        )
        return (
            d_query.astype(jnp.bfloat16),
            d_key.astype(jnp.bfloat16),
            d_value.astype(jnp.bfloat16),
        )

    head_split = pieces.reshape(images, full_len, 3, heads_here, HEAD_DIM)
    triple_set = jnp.transpose(head_split, (2, 0, 3, 1, 4)).reshape(
        3, images * heads_here, full_len, HEAD_DIM
    )
    d_split = jnp.transpose(
        d_heads.reshape(images, full_len, heads_here, HEAD_DIM), (0, 2, 1, 3)
    ).reshape(images * heads_here, full_len, HEAD_DIM)
    d_query, d_key, d_value = lax.map(
        self_back,
        (
            triple_set[0],
            triple_set[1],
            triple_set[2],
            d_split,
            self_logsum.reshape(images * heads_here, full_len),
        ),
    )
    d_triple = jnp.stack([d_query, d_key, d_value], 0).reshape(
        3, images, heads_here, full_len, HEAD_DIM
    )
    d_triple = jnp.transpose(d_triple, (1, 3, 0, 2, 4)).reshape(images, full_len, 3, narrow)
    d_stacked = lax.all_to_all(d_triple, SEQ, split_axis=1, concat_axis=3, tiled=True)
    d_packed_in = d_stacked.reshape(tokens, 3, HEADS, HEAD_DIM).astype(jnp.float32)
    q_vals, q_back = jax.vjp(query_prep, packed[:, 0], head_gains[0])
    d_qpre, d_hgain0 = q_back(d_packed_in[:, 0])
    k_vals, k_back = jax.vjp(query_prep, packed[:, 1], head_gains[1])
    d_kself, d_hgain1 = k_back(d_packed_in[:, 1])
    d_packed = (
        jnp.stack([d_qpre, d_kself, d_packed_in[:, 2]], 1)
        .reshape(tokens, 3 * width)
        .astype(jnp.bfloat16)
    )
    g_qkv = weight_grad(normed1, d_packed)
    d_normed1 = project_back(d_packed, w_qkv)
    d_shift = jnp.sum(d_normed1.reshape(images, local, width), axis=1)
    norm_vals, norm_back = jax.vjp(scaled_norm, resid0, norm_gains[1])
    d_resid, d_gain1 = norm_back(d_normed1)
    resid_grad = resid_grad + d_resid
    g_tsecond = jnp.einsum("bc,bd->cd", lifted.astype(jnp.float32), d_shift, precision=HIGHEST)
    d_lifted = jnp.einsum("bd,cd->bc", d_shift, w_second.astype(jnp.float32), precision=HIGHEST)
    silu_vals, silu_back = jax.vjp(jax.nn.silu, before)
    d_before = silu_back(d_lifted)[0]
    g_tfirst = jnp.einsum("bc,bd->cd", feats.astype(jnp.float32), d_before, precision=HIGHEST)
    norm_vals, norm_back = jax.vjp(scaled_norm, merged, norm_gains[0])
    d_merged, d_gain0 = norm_back(resid_grad)
    d_merged_low = d_merged.astype(jnp.bfloat16)
    g_skipw = weight_grad(joined, d_merged_low)
    d_joined = project_back(d_merged_low, w_skip)
    hidden_grad = d_joined[:, :width].reshape(images, local, width)
    skip_grad = d_joined[:, width:].reshape(images, local, width)
    row_sums = (
        lax.psum_scatter(
            g_skipw.astype(jnp.bfloat16), DP, scatter_dimension=0, tiled=True
        ).astype(jnp.float32),
        lax.psum_scatter(
            g_tfirst.astype(jnp.bfloat16), DP, scatter_dimension=0, tiled=True
        ).astype(jnp.float32),
        lax.psum_scatter(
            g_tsecond.astype(jnp.bfloat16), DP, scatter_dimension=0, tiled=True
        ).astype(jnp.float32),
        lax.psum_scatter(g_qkv.astype(jnp.bfloat16), DP, scatter_dimension=0, tiled=True).astype(
            jnp.float32
        ),
        lax.psum_scatter(g_aout.astype(jnp.bfloat16), DP, scatter_dimension=0, tiled=True).astype(
            jnp.float32
        ),
        lax.psum_scatter(
            g_cquery.astype(jnp.bfloat16), DP, scatter_dimension=0, tiled=True
        ).astype(jnp.float32),
        lax.psum_scatter(g_ckv.astype(jnp.bfloat16), DP, scatter_dimension=0, tiled=True).astype(
            jnp.float32
        ),
        lax.psum_scatter(g_cout.astype(jnp.bfloat16), DP, scatter_dimension=0, tiled=True).astype(
            jnp.float32
        ),
        lax.psum_scatter(
            g_tproj.astype(jnp.bfloat16), DP, scatter_dimension=0, tiled=True
        ).astype(jnp.float32),
        lax.psum_scatter(g_up.astype(jnp.bfloat16), DP, scatter_dimension=0, tiled=True).astype(
            jnp.float32
        ),
        lax.psum_scatter(g_down.astype(jnp.bfloat16), DP, scatter_dimension=0, tiled=True).astype(
            jnp.float32
        ),
    )
    owned = (
        lax.psum_scatter(
            row_sums[0].astype(jnp.bfloat16), SEQ, scatter_dimension=1, tiled=True
        ).astype(jnp.float32),
        lax.psum_scatter(
            row_sums[1].astype(jnp.bfloat16), SEQ, scatter_dimension=1, tiled=True
        ).astype(jnp.float32),
        lax.psum_scatter(
            row_sums[2].astype(jnp.bfloat16), SEQ, scatter_dimension=1, tiled=True
        ).astype(jnp.float32),
        lax.psum_scatter(
            row_sums[3].astype(jnp.bfloat16), SEQ, scatter_dimension=1, tiled=True
        ).astype(jnp.float32),
        lax.psum_scatter(
            row_sums[4].astype(jnp.bfloat16), SEQ, scatter_dimension=1, tiled=True
        ).astype(jnp.float32),
        lax.psum_scatter(
            row_sums[5].astype(jnp.bfloat16), SEQ, scatter_dimension=1, tiled=True
        ).astype(jnp.float32),
        lax.psum_scatter(
            row_sums[6].astype(jnp.bfloat16), SEQ, scatter_dimension=1, tiled=True
        ).astype(jnp.float32),
        lax.psum_scatter(
            row_sums[7].astype(jnp.bfloat16), SEQ, scatter_dimension=1, tiled=True
        ).astype(jnp.float32),
        lax.psum_scatter(
            row_sums[8].astype(jnp.bfloat16), SEQ, scatter_dimension=1, tiled=True
        ).astype(jnp.float32),
        lax.psum_scatter(
            row_sums[9].astype(jnp.bfloat16), SEQ, scatter_dimension=1, tiled=True
        ).astype(jnp.float32),
        lax.psum_scatter(
            row_sums[10].astype(jnp.bfloat16), SEQ, scatter_dimension=1, tiled=True
        ).astype(jnp.float32),
    )
    gain_totals = lax.psum(
        (
            jnp.stack([d_gain0, d_gain1, d_gain2, d_gain3], 0),
            jnp.stack([d_hgain0, d_hgain1, d_hgain2, d_hgain3], 0),
        ),
        (DP, SEQ),
    )
    return (
        block_out,
        hidden_grad,
        skip_grad,
        owned[0],
        owned[1],
        owned[2],
        owned[3],
        owned[4],
        owned[5],
        owned[6],
        owned[7],
        owned[8],
        owned[9],
        owned[10],
        gain_totals[0],
        gain_totals[1],
    )


BOTH = (DP, SEQ)
FLIP = [(0, 1), (1, 0)]
LOG2E = 1.4426950408889634
LANES = 128


def swap(value, bit):
    return lax.ppermute(value, DP, [(i, i ^ bit) for i in range(16)])


def swap_seq(value):
    return lax.ppermute(value, SEQ, FLIP)


def core_holds(dp_index, seq_index):
    return dp_index % 2 == dp_index // 8


def seq_holds(dp_index, seq_index):
    return seq_index == dp_index // 8


def hop_pairs(holds, outward):
    pairs = []
    for i in range(16):
        for s in range(2):
            if holds(i, s):
                there = ((i ^ 8) * 2 + s, i * 2 + s)
                pairs.append(there[::-1] if outward else there)
    return pairs


def corner_pairs(outward):
    first, second = [], []
    for i in range(16):
        h = i // 8
        base = i - i % 2
        if i % 2 == 0:
            for core in range(2):
                source = (base + core) * 2 + h
                first.append((source, (base + 1 - core) * 2 + core))
            core = 1 - h
            second.append(((base + core) * 2 + h, (base + core) * 2 + 1 - h))
    if not outward:
        return [p[::-1] for p in first], [p[::-1] for p in second]
    return first, second


def pair(flag, own, other, axis=0):
    return jnp.where(
        flag == 0,
        jnp.concatenate([own, other], axis),
        jnp.concatenate([other, own], axis),
    )


def pick(flag, first, second):
    return jnp.where(flag == 0, first, second)


class Spot:
    def __init__(self):
        self.d = lax.axis_index(DP)
        self.y = lax.axis_index(SEQ)
        self.z = self.d // 4
        self.x = (self.d // 2) % 2
        self.c = self.d % 2
        self.b = self.z % 2
        self.h = self.z // 2


class Flow:
    def __init__(self):
        self.chains = {}
        self.done = {}

    def add(self, name, chain):
        self.chains[name] = [chain, None, next(chain)]

    def step(self, values, names):
        for name in names:
            entry = self.chains[name]
            if entry[1] is not None:
                try:
                    entry[1:] = [None, entry[0].send(entry[1])]
                except StopIteration as end:
                    self.done[name] = end.value
                    del self.chains[name]
        moving = [name for name in names if name in self.chains]
        arrays = [[array for _, array in self.chains[name][2]] for name in moving]
        ended = [self.done[name] for name in names if name in self.done]
        values, arrays, ended = lax.optimization_barrier((list(values), arrays, ended))
        for name, value in zip([n for n in names if n in self.done], ended):
            self.done[name] = value
        for name, given in zip(moving, arrays):
            entry = self.chains[name]
            entry[1] = [route(array) for (route, _), array in zip(entry[2], given)]
        return values

    def finish(self, name):
        while name in self.chains:
            self.step([], [name])
        return self.done[name]


def by_core(value):
    return swap(value, 1)


def by_x(value):
    return swap(value, 2)


def by_z(value):
    return swap(value, 4)


def by_routes(pairs):
    return lambda value: lax.ppermute(value, BOTH, pairs)


def narrow(value):
    return value.astype(jnp.bfloat16)


def wide(value):
    return value.astype(jnp.float32)


def choose(value, axis, index):
    return lax.dynamic_index_in_dim(value, index, axis, keepdims=False)


def dot_rows(left, right):
    return jnp.einsum("tc,td->cd", left, right, preferred_element_type=jnp.float32)


def settle_x(spot, part):
    (given,) = yield [(by_x, choose(part, 1, 1 - spot.x))]
    return narrow(wide(choose(part, 1, spot.x)) + wide(given))


def settle_z(spot, part, holds):
    (given,) = yield [(by_z, choose(part, 0, 1 - spot.b))]
    block = wide(choose(part, 0, spot.b)) + wide(given)
    (given,) = yield [(by_routes(hop_pairs(holds, False)), narrow(block))]
    return block + wide(given)


def split_rows(spot, block):
    pieces = block.reshape(2, block.shape[0] // 2, block.shape[1])
    (given,) = yield [(by_core, narrow(choose(pieces, 0, 1 - spot.c)))]
    return jnp.where(spot.c == spot.h, choose(pieces, 0, spot.c), wide(given))


def quarters(own):
    rows, cols = own.shape
    return own.reshape(2, 2, rows // 4, cols)


def reduce_both(spot, halves, grads):
    mine = pick(spot.c, halves[0], halves[1])
    theirs = pick(spot.c, halves[1], halves[0])
    grad_own = pick(spot.y, grads[0], grads[1])
    grad_other = pick(spot.y, grads[1], grads[0])
    given = yield [(by_core, narrow(dot_rows(theirs, g))) for g in (grad_own, grad_other)]
    own = dot_rows(mine, grad_own) + wide(given[0])
    other = dot_rows(mine, grad_other) + wide(given[1])
    (given,) = yield [(swap_seq, narrow(other))]
    part = quarters(narrow(own + wide(given)))
    part = yield from settle_x(spot, part)
    block = yield from settle_z(spot, part, core_holds)
    return (yield from split_rows(spot, block))


def reduce_rows(spot, halves, grad):
    mine = pick(spot.c, halves[0], halves[1])
    theirs = pick(spot.c, halves[1], halves[0])
    (given,) = yield [(by_core, narrow(dot_rows(theirs, grad)))]
    part = quarters(narrow(dot_rows(mine, grad) + wide(given)))
    part = yield from settle_x(spot, part)
    block = yield from settle_z(spot, part, core_holds)
    return (yield from split_rows(spot, block))


def reduce_down(spot, left, grads):
    mine = pick(spot.c, grads[0], grads[1])
    theirs = pick(spot.c, grads[1], grads[0])
    (given,) = yield [(by_core, narrow(dot_rows(left, theirs)))]
    part = quarters(narrow(dot_rows(left, mine) + wide(given)))
    part = yield from settle_x(spot, part)
    block = yield from settle_z(spot, part, seq_holds)
    pieces = block.reshape(2, block.shape[0] // 2, block.shape[1])
    same, cross = choose(pieces, 0, spot.c), choose(pieces, 0, 1 - spot.c)
    first, second = corner_pairs(True)
    crossed, across = yield [(by_routes(first), narrow(cross)), (by_routes(second), narrow(same))]
    inner = jnp.where(spot.y == spot.h, same, wide(across))
    return jnp.where(spot.c == spot.y, inner, wide(crossed))


def total_over_all(value):
    for bit in (1, 2, 4, 8):
        value = value + swap(value, bit)
    return value + swap_seq(value)


def gather_images(spot, value):
    for bit, flag in ((1, spot.c), (2, spot.x), (4, spot.b), (8, spot.h)):
        value = pair(flag, value, swap(value, bit))
    return value


def attend(q_src, kv_src, gains, cosine, sine, heads, q_at, k_at, v_at, keys):
    width = heads * HEAD_DIM

    def heads_of(source, at):
        return source[:, at : at + width].reshape(source.shape[0], heads, HEAD_DIM)

    def prepared(source, at, which):
        v = normalize(heads_of(source, at)) * gains[which]
        if cosine is not None:
            q1, q2, q3, q4 = jnp.split(v, 4, axis=-1)
            other = jnp.concatenate([q2, q1, q4, q3], -1)
            v = v * cosine[:, None, :HEAD_DIM] + other * sine[:, None, :HEAD_DIM]
        return v.astype(jnp.bfloat16)

    q, k = prepared(q_src, q_at, 0), prepared(kv_src, k_at, 1)
    v = heads_of(kv_src, v_at).astype(jnp.bfloat16)
    s = jnp.einsum("qhd,khd->hqk", q, k, preferred_element_type=jnp.float32) * HEAD_DIM**-0.5
    s = jnp.where(jnp.arange(kv_src.shape[0]) < keys, s, -1e9)
    p = jax.nn.softmax(s, axis=-1).astype(jnp.bfloat16)
    o = jnp.einsum("hqk,khd->qhd", p, v, preferred_element_type=jnp.float32)
    return o.reshape(q_src.shape[0], width)


def attend_forward(
    q_src, kv_src, cosine, sine, gains, helpers, heads, q_at, k_at, v_at, keys
):
    q32, kv32 = q_src.astype(jnp.float32), kv_src.astype(jnp.float32)
    o, back = jax.vjp(
        lambda a, b, g: attend(a, b, g, cosine, sine, heads, q_at, k_at, v_at, keys),
        q32,
        kv32,
        gains[:2, :HEAD_DIM],
    )
    return narrow(o), back, None, None


def attend_backward(
    q_src, kv_src, cosine, sine, gains, helpers, back, kn, vn, out, grad_out, heads, q_at, k_at, v_at
):
    dq, dk, dg = back(grad_out.astype(jnp.float32))
    dg = jnp.pad(dg * gains[:2, :HEAD_DIM], ((0, 0), (0, LANES - HEAD_DIM)))
    if q_src is kv_src:
        return narrow(dq + dk), dg
    return narrow(dq), narrow(dk), dg


def rope_tables(pos_rows, pos_cols):
    quarter = HEAD_DIM // 4
    frequency = 10000.0 ** (-jnp.arange(quarter, dtype=jnp.float32) / quarter)
    row_angles = pos_rows[:, None] * frequency[None, :]
    col_angles = pos_cols[:, None] * frequency[None, :]
    angles = jnp.concatenate([row_angles, row_angles, col_angles, col_angles], -1)
    sign = jnp.where((jnp.arange(HEAD_DIM) // quarter) % 2 == 0, -1.0, 1.0)
    wide = ((0, 0), (0, LANES - HEAD_DIM))
    return jnp.pad(jnp.cos(angles), wide), jnp.pad(jnp.sin(angles) * sign[None, :], wide)


def gain_rows(gains):
    return jnp.pad(gains, ((0, 0), (0, LANES - HEAD_DIM)))


def gelu(values):
    return jax.nn.gelu(values, approximate=True)


def halves_of(value):
    mid = value.shape[1] // 2
    return value[:, :mid], value[:, mid:]


def norm_parts(values):
    center = values - jnp.mean(values, axis=-1, keepdims=True)
    scale = lax.rsqrt(jnp.mean(center * center, axis=-1, keepdims=True) + EPSILON)
    return center * scale, scale


def norm_grad(grad, values, gain):
    normal, scale = norm_parts(values)
    gain_grad = jnp.sum(grad * normal, axis=0)
    grad = grad * gain
    mean = jnp.mean(grad, axis=-1, keepdims=True)
    mean_product = jnp.mean(grad * normal, axis=-1, keepdims=True)
    return scale * (grad - mean - normal * mean_product), gain_grad


def fast_body(
    hidden_in,
    skip_in,
    clip_text,
    mt5_text,
    time_ids,
    null_text,
    loss_weight,
    patch_pos,
    out_cot,
    skip_weight,
    time_first,
    time_second,
    attn_qkv,
    attn_out,
    cross_qproj,
    cross_kvproj,
    cross_out,
    text_proj,
    mlp_up,
    mlp_down,
    norm_gains,
    head_gains,
):
    spot = Spot()
    _, local, width = hidden_in.shape
    narrow_width = width // 2
    heads_here = HEADS // 2
    clip_len = clip_text.shape[1]
    text_len = clip_len + mt5_text.shape[1]
    text_pad = -(-text_len // LANES) * LANES
    y = spot.y
    bf16 = jnp.bfloat16

    time_rows = lax.all_gather(jnp.concatenate([time_first, time_second], 0), DP)
    time_cut = time_first.shape[0]
    time_weights = [
        rows.reshape(-1, narrow_width) for rows in (time_rows[:, :time_cut], time_rows[:, time_cut:])
    ]
    flow = Flow()
    hidden = hidden_in[0]
    skip = skip_in[0]
    scaled_cot = out_cot[0].astype(jnp.float32) * loss_weight[0]
    cot_low = narrow(scaled_cot)
    pos = patch_pos[:, 0].astype(jnp.float32)
    pos_far = swap_seq(pos)

    def both_halves(value, axis=1):
        return pair(y, value, swap_seq(value), axis)

    a, m, e = (attn_qkv[:, i * narrow_width : (i + 1) * narrow_width] for i in range(3))
    moved = swap_seq(m)
    qkv_shard = jnp.concatenate([pick(y, a, moved), pick(y, e, a), pick(y, moved, e)], 1)

    def gather(shard):
        return lax.all_gather(shard, DP, axis=0, tiled=True)

    def with_far(own):
        return own, swap_seq(own)

    def times(value, sides):
        return pair(y, project(value, sides[0]), project(value, sides[1]), 1)

    def times_back(grad, sides):
        first, second = halves_of(grad)
        own, far = pick(y, first, second), pick(y, second, first)
        return project_back(own, sides[0]) + project_back(far, sides[1])

    w_skip = with_far(gather(skip_weight))
    w_qkv = gather(qkv_shard)
    w_text = gather(text_proj)
    w_ckv = gather(cross_kvproj)
    out_rows = lax.all_gather(jnp.concatenate([attn_out, cross_qproj, cross_out], 0), DP)
    out_sides = with_far(out_rows.reshape(out_rows.shape[0], 3, -1, narrow_width))
    w_aout, w_cq, w_cout = (
        tuple(side[:, k].reshape(-1, narrow_width) for side in out_sides) for k in range(3)
    )
    w_up = gather(mlp_up)
    down_rows = gather(mlp_down)
    half_rows = down_rows.shape[0] // 2
    upper_rows, lower_rows = down_rows[:half_rows], down_rows[half_rows:]
    w_down = pick(y, upper_rows, lower_rows), swap_seq(pick(y, lower_rows, upper_rows))
    cot_far = swap_seq(cot_low)

    feats = time_features(time_ids).astype(bf16)
    before = both_halves(project(feats, time_weights[0]))
    lifted = jax.nn.silu(before).astype(bf16)
    shift = both_halves(project(lifted, time_weights[1]))

    cosine, sine = rope_tables(*jnp.concatenate([pos, pos_far], 1))
    helpers = []
    merged = times(jnp.concatenate([hidden, skip], -1), w_skip)
    resid0 = scaled_norm(merged, norm_gains[0])
    normed1 = narrow(scaled_norm(resid0, norm_gains[1]) + shift)

    normed1_both = jnp.concatenate([normed1, swap_seq(normed1)], 0)
    packed = narrow(project(normed1_both, w_qkv))
    self_gains = gain_rows(head_gains[0:2])
    self_o, self_q, self_k, self_v = attend_forward(
        packed,
        packed,
        cosine,
        sine,
        self_gains,
        helpers,
        heads_here,
        0,
        narrow_width,
        2 * narrow_width,
        2 * local,
    )
    far_o = swap_seq(self_o[local:])

    keep_text = (1 - null_text[0]).astype(bf16)
    projected = both_halves(narrow(project(mt5_text[0], w_text)))
    context = jnp.concatenate([clip_text[0], projected], 0) * keep_text
    context = jnp.pad(context, ((0, text_pad - text_len), (0, 0)))
    text_kv = both_halves(narrow(project(context, w_ckv)))
    own_o = self_o[:local]

    attn_halves = pick(y, own_o, far_o), pick(y, far_o, own_o)
    attn_flat = jnp.concatenate(attn_halves, 1)
    resid1 = resid0 + times(attn_flat, w_aout)
    normed2 = narrow(scaled_norm(resid1, norm_gains[2]))
    cross_pre = narrow(times(normed2, w_cq))
    cross_gains = gain_rows(head_gains[2:4])
    cross_o, cross_q, cross_k, cross_v = attend_forward(
        cross_pre, text_kv, None, None, cross_gains, helpers, HEADS, 0, 0, width, text_len
    )
    resid2 = resid1 + times(cross_o, w_cout)
    normed3 = narrow(scaled_norm(resid2, norm_gains[3]))

    normed3_both = jnp.concatenate([normed3, swap_seq(normed3)], 0)
    upper = narrow(project(normed3_both, w_up))
    active = narrow(gelu(upper.astype(jnp.float32)))
    mixed = times(active, w_down)
    final = resid2 + mixed[:local] + wide(swap_seq(narrow(mixed[local:])))
    block_out = narrow(final)[None]

    cot_both = jnp.concatenate([cot_low, cot_far], 0)
    d_active = times_back(cot_both, w_down)
    _, gelu_back = jax.vjp(gelu, upper.astype(jnp.float32))
    d_upper = narrow(gelu_back(d_active)[0])
    flow.add(8, reduce_down(spot, active, halves_of(cot_both)))
    (d_upper,) = flow.step([d_upper], [8])
    d_both = project_back(d_upper, w_up)
    d_far = swap_seq(narrow(d_both[local:]))
    flow.add(7, reduce_rows(spot, halves_of(normed3_both), d_upper))
    d_own, d_far = flow.step([d_both[:local], d_far], [8, 7])
    d_normed3 = d_own + wide(d_far)
    d_resid, d_gain3 = norm_grad(d_normed3, resid2, norm_gains[3])
    resid_grad = scaled_cot + d_resid

    grad_low = narrow(resid_grad)
    d_cmix = narrow(times_back(grad_low, w_cout))
    flow.add(5, reduce_both(spot, halves_of(cross_o), halves_of(grad_low)))
    (d_cmix,) = flow.step([d_cmix], [5])
    d_cpre, d_textkv, d_cross_gains = attend_backward(
        cross_pre,
        text_kv,
        None,
        None,
        cross_gains,
        helpers,
        cross_q,
        cross_k,
        cross_v,
        cross_o,
        d_cmix,
        HEADS,
        0,
        0,
        width,
    )
    flow.add(3, reduce_both(spot, halves_of(normed2), halves_of(d_cpre)))
    d_cpre, d_textkv = flow.step([d_cpre, d_textkv], [8, 7, 5, 3])
    d_text = halves_of(d_textkv)
    d_text_far = swap_seq(pick(y, d_text[1], d_text[0]))
    d_normed2 = times_back(d_cpre, w_cq)
    d_resid, d_gain2 = norm_grad(d_normed2, resid1, norm_gains[2])
    resid_grad = resid_grad + d_resid
    grad_low = narrow(resid_grad)
    d_attn = halves_of(narrow(times_back(grad_low, w_aout)))
    d_far = swap_seq(pick(y, d_attn[1], d_attn[0]))
    d_text = narrow(wide(pick(y, d_text[0], d_text[1])) + wide(d_text_far))
    flow.add(2, reduce_both(spot, attn_halves, halves_of(grad_low)))
    flow.add(4, reduce_rows(spot, halves_of(context), d_text))
    d_context = halves_of(project_back(d_text[clip_len:text_len], w_ckv))
    d_context_far = swap_seq(narrow(pick(y, d_context[1], d_context[0])))
    d_proj = pick(y, d_context[0], d_context[1]) + wide(d_context_far)
    d_proj = narrow(d_proj * keep_text.astype(jnp.float32))
    flow.add(6, reduce_rows(spot, halves_of(mt5_text[0]), d_proj))

    d_heads = jnp.concatenate([pick(y, d_attn[0], d_attn[1]), d_far], 0)
    (d_heads,) = flow.step(
        [d_heads], [8, 5, 3, 2, 4, 6]
    )
    d_packed, d_self_gains = attend_backward(
        packed,
        packed,
        cosine,
        sine,
        self_gains,
        helpers,
        self_q,
        self_k,
        self_v,
        self_o,
        d_heads,
        heads_here,
        0,
        narrow_width,
        2 * narrow_width,
    )
    (d_packed,) = flow.step(
        [d_packed], [8, 7, 5, 3, 2, 4, 6]
    )
    d_both = project_back(d_packed, w_qkv)
    d_far = swap_seq(narrow(d_both[local:]))
    flow.add(1, reduce_rows(spot, halves_of(normed1_both), d_packed))
    d_own, d_far = flow.step(
        [d_both[:local], d_far],
        [7, 5, 3, 2, 4, 6, 1],
    )
    d_normed1 = d_own + wide(d_far)

    d_shift = jnp.sum(d_normed1, axis=0)
    d_resid, d_gain1 = norm_grad(d_normed1, resid0, norm_gains[1])
    resid_grad = resid_grad + d_resid
    d_merged, d_gain0 = norm_grad(resid_grad, merged, norm_gains[0])
    d_merged = narrow(d_merged)
    flow.add(0, reduce_both(spot, (hidden, skip), halves_of(d_merged)))
    (d_merged,) = flow.step(
        [d_merged],
        [0, 7, 5, 3, 2, 4, 6, 1],
    )
    d_joined = times_back(d_merged, w_skip)
    hidden_grad, skip_grad = d_joined[:, :width][None], d_joined[:, width:][None]

    d_shift = d_shift + swap_seq(d_shift)
    features = jnp.pad(feats.astype(jnp.float32), ((0, 0), (0, width - FREQ)))
    rows = gather_images(spot, jnp.stack([before[0], features[0], d_shift], 0)[None])
    before_all, features_all, d_shift_all = rows[:, 0], rows[:, 1, :FREQ], rows[:, 2]
    silu_all, silu_back = jax.vjp(jax.nn.silu, before_all)
    lifted_all = wide(narrow(silu_all))
    d_shift_cols = pick(y, *halves_of(d_shift_all))
    d_lifted = jnp.einsum(
        "bd,cd->bc", d_shift_cols, time_weights[1].astype(jnp.float32), precision=HIGHEST
    )
    d_before = silu_back(d_lifted + swap_seq(d_lifted))[0]

    def block(left, cols, left_rows):
        mine = lax.dynamic_slice_in_dim(left, spot.d * left_rows, left_rows, 1)
        return jnp.einsum("bc,bd->cd", mine, cols, precision=HIGHEST)

    g_tsecond = block(lifted_all, d_shift_cols, time_second.shape[0])
    g_tfirst = block(features_all, pick(y, *halves_of(d_before)), time_first.shape[0])

    d_head_gains = jnp.concatenate([d_self_gains, d_cross_gains], 0)[:, :HEAD_DIM] / head_gains
    d_norm_gains = jnp.stack([d_gain0, d_gain1, d_gain2, d_gain3], 0)
    totals = total_over_all(
        jnp.concatenate([d_norm_gains.reshape(-1), d_head_gains.reshape(-1)])
    )
    norm_total = totals[: 4 * width].reshape(4, width)
    head_total = totals[4 * width :].reshape(4, HEAD_DIM)

    while flow.chains:
        flow.step([], list(flow.chains))
    g_skipw, g_qkv, g_aout, g_cquery, g_ckv, g_cout, g_tproj, g_up, g_down = (
        flow.done[name] for name in range(9)
    )
    q_cols, k_cols, v_cols = (
        g_qkv[:, i * narrow_width : (i + 1) * narrow_width] for i in range(3)
    )
    moved = wide(swap_seq(narrow(pick(y, v_cols, q_cols))))
    g_qkv = jnp.concatenate([pick(y, q_cols, k_cols), moved, pick(y, k_cols, v_cols)], 1)
    return (
        block_out,
        hidden_grad,
        skip_grad,
        g_skipw,
        g_tfirst,
        g_tsecond,
        g_qkv,
        g_aout,
        g_cquery,
        g_ckv,
        g_cout,
        g_tproj,
        g_up,
        g_down,
        norm_total,
        head_total,
    )


def solution(mesh):
    placed = (
        P(DP, SEQ, None),
        P(DP, SEQ, None),
        P(DP, None, None),
        P(DP, None, None),
        P(DP),
        P(DP),
        P(DP),
        P(None, DP, SEQ),
        P(DP, SEQ, None),
        P(DP, SEQ),
        P(DP, SEQ),
        P(DP, SEQ),
        P(DP, SEQ),
        P(DP, SEQ),
        P(DP, SEQ),
        P(DP, SEQ),
        P(DP, SEQ),
        P(DP, SEQ),
        P(DP, SEQ),
        P(DP, SEQ),
        P(),
        P(),
    )
    split = mesh.shape[DP] == 16 and mesh.shape[SEQ] == 2
    return jax.shard_map(
        fast_body if split else whole_body,
        mesh=mesh,
        in_specs=placed,
        out_specs=(
            P(DP, SEQ, None),
            P(DP, SEQ, None),
            P(DP, SEQ, None),
            P(DP, SEQ),
            P(DP, SEQ),
            P(DP, SEQ),
            P(DP, SEQ),
            P(DP, SEQ),
            P(DP, SEQ),
            P(DP, SEQ),
            P(DP, SEQ),
            P(DP, SEQ),
            P(DP, SEQ),
            P(DP, SEQ),
            P(),
            P(),
        ),
        check_vma=False,
    )
```

```python
import math

import jax
import jax.numpy as jnp
from jax import lax
from jax.sharding import PartitionSpec as P

DP = "dp"
SEQ = "seq"
HEADS = 16
HEAD_DIM = 88
FREQ = 256


EPSILON = 1e-06
HIGHEST = lax.Precision.HIGHEST


def normalize(values):
    center = values - jnp.mean(values, axis=-1, keepdims=True)
    variance = jnp.mean(center * center, axis=-1, keepdims=True)
    return center * lax.rsqrt(variance + EPSILON)


def scaled_norm(values, gain_row):
    return normalize(values) * gain_row


def rotate(values, pos_rows, pos_cols):
    quarter = values.shape[-1] // 4
    frequency = 10000.0 ** (-jnp.arange(quarter, dtype=jnp.float32) / quarter)

    def turn(halfpart, position):
        angles = position[:, None] * frequency[None, :]
        cosine = jnp.cos(angles)[:, None, :]
        sine_part = jnp.sin(angles)[:, None, :]
        former = halfpart[..., :quarter]
        latter = halfpart[..., quarter:]
        return jnp.concatenate(
            [former * cosine - latter * sine_part, former * sine_part + latter * cosine], -1
        )

    return jnp.concatenate(
        [turn(values[..., : 2 * quarter], pos_rows), turn(values[..., 2 * quarter :], pos_cols)], -1
    )


def time_features(step_ids):
    half_count = FREQ // 2
    frequency = jnp.exp(-math.log(10000.0) * jnp.arange(half_count, dtype=jnp.float32) / half_count)
    angles = step_ids.astype(jnp.float32)[:, None] * frequency[None, :]
    return jnp.concatenate([jnp.cos(angles), jnp.sin(angles)], -1)


def project(left, right):
    return jnp.einsum("tc,cd->td", left, right, preferred_element_type=jnp.float32)


def project_back(grad_low, right):
    return jnp.einsum("td,cd->tc", grad_low, right, preferred_element_type=jnp.float32)


def weight_grad(left, grad_low):
    return jnp.einsum("tc,td->cd", left, grad_low, preferred_element_type=jnp.float32)


def whole_body(
    hidden_in,
    skip_in,
    clip_text,
    mt5_text,
    time_ids,
    null_text,
    loss_weight,
    patch_pos,
    out_cot,
    skip_weight,
    time_first,
    time_second,
    attn_qkv,
    attn_out,
    cross_qproj,
    cross_kvproj,
    cross_out,
    text_proj,
    mlp_up,
    mlp_down,
    norm_gains,
    head_gains,
):
    images, local, width = hidden_in.shape
    groups = lax.axis_size(SEQ)
    heads_here = HEADS // groups
    narrow = width // groups
    tokens = images * local
    full_len = local * groups
    clip_len = clip_text.shape[1]
    text_len = clip_len + mt5_text.shape[1]
    score_scale = HEAD_DIM ** (-0.5)
    pos_rows = patch_pos[0].reshape(tokens).astype(jnp.float32)
    pos_cols = patch_pos[1].reshape(tokens).astype(jnp.float32)
    col_full = (
        lax.all_gather(skip_weight, SEQ, axis=1, tiled=True),
        lax.all_gather(time_first, SEQ, axis=1, tiled=True),
        lax.all_gather(time_second, SEQ, axis=1, tiled=True),
        lax.all_gather(attn_qkv, SEQ, axis=1, tiled=True),
        lax.all_gather(attn_out, SEQ, axis=1, tiled=True),
        lax.all_gather(cross_qproj, SEQ, axis=1, tiled=True),
        lax.all_gather(cross_kvproj, SEQ, axis=1, tiled=True),
        lax.all_gather(cross_out, SEQ, axis=1, tiled=True),
        lax.all_gather(text_proj, SEQ, axis=1, tiled=True),
        lax.all_gather(mlp_up, SEQ, axis=1, tiled=True),
        lax.all_gather(mlp_down, SEQ, axis=1, tiled=True),
    )
    weight_set = (
        lax.all_gather(col_full[0], DP, axis=0, tiled=True),
        lax.all_gather(col_full[1], DP, axis=0, tiled=True),
        lax.all_gather(col_full[2], DP, axis=0, tiled=True),
        lax.all_gather(col_full[3], DP, axis=0, tiled=True),
        lax.all_gather(col_full[4], DP, axis=0, tiled=True),
        lax.all_gather(col_full[5], DP, axis=0, tiled=True),
        lax.all_gather(col_full[6], DP, axis=0, tiled=True),
        lax.all_gather(col_full[7], DP, axis=0, tiled=True),
        lax.all_gather(col_full[8], DP, axis=0, tiled=True),
        lax.all_gather(col_full[9], DP, axis=0, tiled=True),
        lax.all_gather(col_full[10], DP, axis=0, tiled=True),
    )
    w_skip, w_first, w_second, w_qkv, w_aout, w_cq, w_ckv, w_cout, w_text, w_up, w_down = weight_set
    joined = jnp.concatenate([hidden_in, skip_in], -1).reshape(tokens, 2 * width)
    merged = project(joined, w_skip)
    resid0 = scaled_norm(merged, norm_gains[0])
    feats = time_features(time_ids).astype(jnp.bfloat16)
    before = project(feats, w_first)
    lifted = jax.nn.silu(before).astype(jnp.bfloat16)
    shift = project(lifted, w_second)
    shift_tok = jnp.repeat(shift, local, axis=0)
    normed1 = (scaled_norm(resid0, norm_gains[1]) + shift_tok).astype(jnp.bfloat16)
    packed = project(normed1, w_qkv).reshape(tokens, 3, HEADS, HEAD_DIM)

    def query_prep(values, gain_row):
        return rotate(scaled_norm(values, gain_row), pos_rows, pos_cols)

    self_q = query_prep(packed[:, 0], head_gains[0]).astype(jnp.bfloat16)
    self_k = query_prep(packed[:, 1], head_gains[1]).astype(jnp.bfloat16)
    self_v = packed[:, 2].astype(jnp.bfloat16)
    stacked = jnp.stack([self_q, self_k, self_v], 1).reshape(images, local, 3, width)

    def self_block(operand):
        queries, keyset, valueset = operand
        scores = (
            jnp.einsum("qd,kd->qk", queries, keyset, preferred_element_type=jnp.float32)
            * score_scale
        )
        top_score = jnp.max(scores, axis=-1, keepdims=True)
        exponent = jnp.exp(scores - top_score)
        totals = jnp.sum(exponent, axis=-1, keepdims=True)
        mixed_out = jnp.einsum(
            "qk,kd->qd",
            (exponent / totals).astype(jnp.bfloat16),
            valueset,
            preferred_element_type=jnp.float32,
        )
        return (mixed_out.astype(jnp.bfloat16), (top_score + jnp.log(totals))[:, 0])

    pieces = lax.all_to_all(stacked, SEQ, split_axis=3, concat_axis=1, tiled=True)
    item_count = pieces.shape[0]
    length = pieces.shape[1]
    split_heads = pieces.reshape(item_count, length, 3, heads_here, HEAD_DIM)
    triple_set = jnp.transpose(split_heads, (2, 0, 3, 1, 4)).reshape(
        3, item_count * heads_here, length, HEAD_DIM
    )
    mixed_out, logsum = lax.map(self_block, (triple_set[0], triple_set[1], triple_set[2]))
    joined_heads = jnp.transpose(
        mixed_out.reshape(item_count, heads_here, length, HEAD_DIM), (0, 2, 1, 3)
    ).reshape(item_count, length, narrow)
    returned = lax.all_to_all(joined_heads, SEQ, split_axis=1, concat_axis=2, tiled=True)
    self_logsum = logsum.reshape(item_count, heads_here, length)
    attn_flat = returned.reshape(tokens, width)
    resid1 = resid0 + project(attn_flat, w_aout)
    normed2 = scaled_norm(resid1, norm_gains[2]).astype(jnp.bfloat16)
    cross_pre = project(normed2, w_cq).reshape(tokens, HEADS, HEAD_DIM)
    cross_q = (
        scaled_norm(cross_pre, head_gains[2])
        .astype(jnp.bfloat16)
        .reshape(images, local, HEADS, HEAD_DIM)
    )
    keep_text = (1 - null_text).astype(jnp.bfloat16)
    projected = jnp.einsum(
        "btc,cd->btd", mt5_text, w_text, preferred_element_type=jnp.float32
    ).astype(jnp.bfloat16)
    context = jnp.concatenate([clip_text, projected], 1) * keep_text[:, None, None]
    text_kv = jnp.einsum("btc,cd->btd", context, w_ckv, preferred_element_type=jnp.float32).reshape(
        images, text_len, 2, HEADS, HEAD_DIM
    )
    cross_k = scaled_norm(text_kv[:, :, 0], head_gains[3]).astype(jnp.bfloat16)
    cross_v = text_kv[:, :, 1].astype(jnp.bfloat16)
    cross_scores = (
        jnp.einsum("bqhd,bkhd->bhqk", cross_q, cross_k, preferred_element_type=jnp.float32)
        * score_scale
    )
    cross_top = jnp.max(cross_scores, axis=-1, keepdims=True)
    cross_exp = jnp.exp(cross_scores - cross_top)
    cross_total = jnp.sum(cross_exp, axis=-1, keepdims=True)
    cross_logsum = cross_top + jnp.log(cross_total)
    cross_mix = jnp.einsum(
        "bhqk,bkhd->bqhd",
        (cross_exp / cross_total).astype(jnp.bfloat16),
        cross_v,
        preferred_element_type=jnp.float32,
    ).astype(jnp.bfloat16)
    cross_flat = cross_mix.reshape(tokens, width)
    resid2 = resid1 + project(cross_flat, w_cout)
    normed3 = scaled_norm(resid2, norm_gains[3]).astype(jnp.bfloat16)
    upper = project(normed3, w_up)
    active = jax.nn.gelu(upper, approximate=True).astype(jnp.bfloat16)
    final = resid2 + project(active, w_down)
    block_out = final.astype(jnp.bfloat16).reshape(images, local, width)
    again_full = (
        lax.all_gather(skip_weight, SEQ, axis=1, tiled=True),
        lax.all_gather(time_first, SEQ, axis=1, tiled=True),
        lax.all_gather(time_second, SEQ, axis=1, tiled=True),
        lax.all_gather(attn_qkv, SEQ, axis=1, tiled=True),
        lax.all_gather(attn_out, SEQ, axis=1, tiled=True),
        lax.all_gather(cross_qproj, SEQ, axis=1, tiled=True),
        lax.all_gather(cross_kvproj, SEQ, axis=1, tiled=True),
        lax.all_gather(cross_out, SEQ, axis=1, tiled=True),
        lax.all_gather(text_proj, SEQ, axis=1, tiled=True),
        lax.all_gather(mlp_up, SEQ, axis=1, tiled=True),
        lax.all_gather(mlp_down, SEQ, axis=1, tiled=True),
    )
    weight_set = (
        lax.all_gather(again_full[0], DP, axis=0, tiled=True),
        lax.all_gather(again_full[1], DP, axis=0, tiled=True),
        lax.all_gather(again_full[2], DP, axis=0, tiled=True),
        lax.all_gather(again_full[3], DP, axis=0, tiled=True),
        lax.all_gather(again_full[4], DP, axis=0, tiled=True),
        lax.all_gather(again_full[5], DP, axis=0, tiled=True),
        lax.all_gather(again_full[6], DP, axis=0, tiled=True),
        lax.all_gather(again_full[7], DP, axis=0, tiled=True),
        lax.all_gather(again_full[8], DP, axis=0, tiled=True),
        lax.all_gather(again_full[9], DP, axis=0, tiled=True),
        lax.all_gather(again_full[10], DP, axis=0, tiled=True),
    )
    w_skip, w_first, w_second, w_qkv, w_aout, w_cq, w_ckv, w_cout, w_text, w_up, w_down = weight_set
    scaled_cot = (out_cot.astype(jnp.float32) * loss_weight[:, None, None]).reshape(tokens, width)
    grad_low = scaled_cot.astype(jnp.bfloat16)
    g_down = weight_grad(active, grad_low)
    d_active = project_back(grad_low, w_down)
    upper_vals, gelu_back = jax.vjp(lambda values: jax.nn.gelu(values, approximate=True), upper)
    d_upper = gelu_back(d_active)[0].astype(jnp.bfloat16)
    g_up = weight_grad(normed3, d_upper)
    d_normed3 = project_back(d_upper, w_up)
    norm_vals, norm_back = jax.vjp(scaled_norm, resid2, norm_gains[3])
    d_resid, d_gain3 = norm_back(d_normed3)
    resid_grad = scaled_cot + d_resid
    grad_low = resid_grad.astype(jnp.bfloat16)
    g_cout = weight_grad(cross_flat, grad_low)
    d_cmix = (
        project_back(grad_low, w_cout).astype(jnp.bfloat16).reshape(images, local, HEADS, HEAD_DIM)
    )
    cross_weights = jnp.exp(cross_scores - cross_logsum)
    d_cweights = jnp.einsum("bqhd,bkhd->bhqk", d_cmix, cross_v, preferred_element_type=jnp.float32)
    row_dot = jnp.sum(cross_weights * d_cweights, axis=-1, keepdims=True)
    d_cscores = (cross_weights * (d_cweights - row_dot)).astype(jnp.bfloat16)
    d_cquery = (
        jnp.einsum("bhqk,bkhd->bqhd", d_cscores, cross_k, preferred_element_type=jnp.float32)
        * score_scale
    ).astype(jnp.bfloat16)
    d_ckey = (
        jnp.einsum("bhqk,bqhd->bkhd", d_cscores, cross_q, preferred_element_type=jnp.float32)
        * score_scale
    )
    d_cval = jnp.einsum(
        "bhqk,bqhd->bkhd",
        cross_weights.astype(jnp.bfloat16),
        d_cmix,
        preferred_element_type=jnp.float32,
    )
    cq_vals, cq_back = jax.vjp(scaled_norm, cross_pre, head_gains[2])
    d_cpre, d_hgain2 = cq_back(d_cquery.astype(jnp.float32).reshape(tokens, HEADS, HEAD_DIM))
    d_cpre_low = d_cpre.reshape(tokens, width).astype(jnp.bfloat16)
    g_cquery = weight_grad(normed2, d_cpre_low)
    d_normed2 = project_back(d_cpre_low, w_cq)
    norm_vals, norm_back = jax.vjp(scaled_norm, resid1, norm_gains[2])
    d_resid, d_gain2 = norm_back(d_normed2)
    resid_grad = resid_grad + d_resid
    ck_vals, ck_back = jax.vjp(scaled_norm, text_kv[:, :, 0], head_gains[3])
    d_kpre, d_hgain3 = ck_back(d_ckey)
    d_textkv = (
        jnp.stack([d_kpre, d_cval], 2).reshape(images, text_len, 2 * width).astype(jnp.bfloat16)
    )
    g_ckv = jnp.einsum("btc,btd->cd", context, d_textkv, preferred_element_type=jnp.float32)
    d_context = jnp.einsum("btd,cd->btc", d_textkv, w_ckv, preferred_element_type=jnp.float32)
    d_proj = (d_context[:, clip_len:] * keep_text.astype(jnp.float32)[:, None, None]).astype(
        jnp.bfloat16
    )
    g_tproj = jnp.einsum("btc,btd->cd", mt5_text, d_proj, preferred_element_type=jnp.float32)
    grad_low = resid_grad.astype(jnp.bfloat16)
    g_aout = weight_grad(attn_flat, grad_low)
    d_attn = project_back(grad_low, w_aout).astype(jnp.bfloat16).reshape(images, local, width)
    d_heads = lax.all_to_all(d_attn, SEQ, split_axis=2, concat_axis=1, tiled=True)

    def self_back(operand):
        queries, keyset, valueset, d_mixed, logsum = operand
        scores = (
            jnp.einsum("qd,kd->qk", queries, keyset, preferred_element_type=jnp.float32)
            * score_scale
        )
        weights = jnp.exp(scores - logsum[:, None])
        d_weights = jnp.einsum("qd,kd->qk", d_mixed, valueset, preferred_element_type=jnp.float32)
        row_sum = jnp.sum(weights * d_weights, axis=-1, keepdims=True)
        d_scores = (weights * (d_weights - row_sum)).astype(jnp.bfloat16)
        d_query = (
            jnp.einsum("qk,kd->qd", d_scores, keyset, preferred_element_type=jnp.float32)
            * score_scale
        )
        d_key = (
            jnp.einsum("qk,qd->kd", d_scores, queries, preferred_element_type=jnp.float32)
            * score_scale
        )
        d_value = jnp.einsum(
            "qk,qd->kd", weights.astype(jnp.bfloat16), d_mixed, preferred_element_type=jnp.float32
        )
        return (
            d_query.astype(jnp.bfloat16),
            d_key.astype(jnp.bfloat16),
            d_value.astype(jnp.bfloat16),
        )

    head_split = pieces.reshape(images, full_len, 3, heads_here, HEAD_DIM)
    triple_set = jnp.transpose(head_split, (2, 0, 3, 1, 4)).reshape(
        3, images * heads_here, full_len, HEAD_DIM
    )
    d_split = jnp.transpose(
        d_heads.reshape(images, full_len, heads_here, HEAD_DIM), (0, 2, 1, 3)
    ).reshape(images * heads_here, full_len, HEAD_DIM)
    d_query, d_key, d_value = lax.map(
        self_back,
        (
            triple_set[0],
            triple_set[1],
            triple_set[2],
            d_split,
            self_logsum.reshape(images * heads_here, full_len),
        ),
    )
    d_triple = jnp.stack([d_query, d_key, d_value], 0).reshape(
        3, images, heads_here, full_len, HEAD_DIM
    )
    d_triple = jnp.transpose(d_triple, (1, 3, 0, 2, 4)).reshape(images, full_len, 3, narrow)
    d_stacked = lax.all_to_all(d_triple, SEQ, split_axis=1, concat_axis=3, tiled=True)
    d_packed_in = d_stacked.reshape(tokens, 3, HEADS, HEAD_DIM).astype(jnp.float32)
    q_vals, q_back = jax.vjp(query_prep, packed[:, 0], head_gains[0])
    d_qpre, d_hgain0 = q_back(d_packed_in[:, 0])
    k_vals, k_back = jax.vjp(query_prep, packed[:, 1], head_gains[1])
    d_kself, d_hgain1 = k_back(d_packed_in[:, 1])
    d_packed = (
        jnp.stack([d_qpre, d_kself, d_packed_in[:, 2]], 1)
        .reshape(tokens, 3 * width)
        .astype(jnp.bfloat16)
    )
    g_qkv = weight_grad(normed1, d_packed)
    d_normed1 = project_back(d_packed, w_qkv)
    d_shift = jnp.sum(d_normed1.reshape(images, local, width), axis=1)
    norm_vals, norm_back = jax.vjp(scaled_norm, resid0, norm_gains[1])
    d_resid, d_gain1 = norm_back(d_normed1)
    resid_grad = resid_grad + d_resid
    g_tsecond = jnp.einsum("bc,bd->cd", lifted.astype(jnp.float32), d_shift, precision=HIGHEST)
    d_lifted = jnp.einsum("bd,cd->bc", d_shift, w_second.astype(jnp.float32), precision=HIGHEST)
    silu_vals, silu_back = jax.vjp(jax.nn.silu, before)
    d_before = silu_back(d_lifted)[0]
    g_tfirst = jnp.einsum("bc,bd->cd", feats.astype(jnp.float32), d_before, precision=HIGHEST)
    norm_vals, norm_back = jax.vjp(scaled_norm, merged, norm_gains[0])
    d_merged, d_gain0 = norm_back(resid_grad)
    d_merged_low = d_merged.astype(jnp.bfloat16)
    g_skipw = weight_grad(joined, d_merged_low)
    d_joined = project_back(d_merged_low, w_skip)
    hidden_grad = d_joined[:, :width].reshape(images, local, width)
    skip_grad = d_joined[:, width:].reshape(images, local, width)
    row_sums = (
        lax.psum_scatter(
            g_skipw.astype(jnp.bfloat16), DP, scatter_dimension=0, tiled=True
        ).astype(jnp.float32),
        lax.psum_scatter(
            g_tfirst.astype(jnp.bfloat16), DP, scatter_dimension=0, tiled=True
        ).astype(jnp.float32),
        lax.psum_scatter(
            g_tsecond.astype(jnp.bfloat16), DP, scatter_dimension=0, tiled=True
        ).astype(jnp.float32),
        lax.psum_scatter(g_qkv.astype(jnp.bfloat16), DP, scatter_dimension=0, tiled=True).astype(
            jnp.float32
        ),
        lax.psum_scatter(g_aout.astype(jnp.bfloat16), DP, scatter_dimension=0, tiled=True).astype(
            jnp.float32
        ),
        lax.psum_scatter(
            g_cquery.astype(jnp.bfloat16), DP, scatter_dimension=0, tiled=True
        ).astype(jnp.float32),
        lax.psum_scatter(g_ckv.astype(jnp.bfloat16), DP, scatter_dimension=0, tiled=True).astype(
            jnp.float32
        ),
        lax.psum_scatter(g_cout.astype(jnp.bfloat16), DP, scatter_dimension=0, tiled=True).astype(
            jnp.float32
        ),
        lax.psum_scatter(
            g_tproj.astype(jnp.bfloat16), DP, scatter_dimension=0, tiled=True
        ).astype(jnp.float32),
        lax.psum_scatter(g_up.astype(jnp.bfloat16), DP, scatter_dimension=0, tiled=True).astype(
            jnp.float32
        ),
        lax.psum_scatter(g_down.astype(jnp.bfloat16), DP, scatter_dimension=0, tiled=True).astype(
            jnp.float32
        ),
    )
    owned = (
        lax.psum_scatter(
            row_sums[0].astype(jnp.bfloat16), SEQ, scatter_dimension=1, tiled=True
        ).astype(jnp.float32),
        lax.psum_scatter(
            row_sums[1].astype(jnp.bfloat16), SEQ, scatter_dimension=1, tiled=True
        ).astype(jnp.float32),
        lax.psum_scatter(
            row_sums[2].astype(jnp.bfloat16), SEQ, scatter_dimension=1, tiled=True
        ).astype(jnp.float32),
        lax.psum_scatter(
            row_sums[3].astype(jnp.bfloat16), SEQ, scatter_dimension=1, tiled=True
        ).astype(jnp.float32),
        lax.psum_scatter(
            row_sums[4].astype(jnp.bfloat16), SEQ, scatter_dimension=1, tiled=True
        ).astype(jnp.float32),
        lax.psum_scatter(
            row_sums[5].astype(jnp.bfloat16), SEQ, scatter_dimension=1, tiled=True
        ).astype(jnp.float32),
        lax.psum_scatter(
            row_sums[6].astype(jnp.bfloat16), SEQ, scatter_dimension=1, tiled=True
        ).astype(jnp.float32),
        lax.psum_scatter(
            row_sums[7].astype(jnp.bfloat16), SEQ, scatter_dimension=1, tiled=True
        ).astype(jnp.float32),
        lax.psum_scatter(
            row_sums[8].astype(jnp.bfloat16), SEQ, scatter_dimension=1, tiled=True
        ).astype(jnp.float32),
        lax.psum_scatter(
            row_sums[9].astype(jnp.bfloat16), SEQ, scatter_dimension=1, tiled=True
        ).astype(jnp.float32),
        lax.psum_scatter(
            row_sums[10].astype(jnp.bfloat16), SEQ, scatter_dimension=1, tiled=True
        ).astype(jnp.float32),
    )
    gain_totals = lax.psum(
        (
            jnp.stack([d_gain0, d_gain1, d_gain2, d_gain3], 0),
            jnp.stack([d_hgain0, d_hgain1, d_hgain2, d_hgain3], 0),
        ),
        (DP, SEQ),
    )
    return (
        block_out,
        hidden_grad,
        skip_grad,
        owned[0],
        owned[1],
        owned[2],
        owned[3],
        owned[4],
        owned[5],
        owned[6],
        owned[7],
        owned[8],
        owned[9],
        owned[10],
        gain_totals[0],
        gain_totals[1],
    )


BOTH = (DP, SEQ)
FLIP = [(0, 1), (1, 0)]
LOG2E = 1.4426950408889634
LANES = 128


def swap(value, bit):
    return lax.ppermute(value, DP, [(i, i ^ bit) for i in range(16)])


def swap_seq(value):
    return lax.ppermute(value, SEQ, FLIP)


def core_holds(dp_index, seq_index):
    return dp_index % 2 == dp_index // 8


def seq_holds(dp_index, seq_index):
    return seq_index == dp_index // 8


def hop_pairs(holds, outward):
    pairs = []
    for i in range(16):
        for s in range(2):
            if holds(i, s):
                there = ((i ^ 8) * 2 + s, i * 2 + s)
                pairs.append(there[::-1] if outward else there)
    return pairs


def corner_pairs(outward):
    first, second = [], []
    for i in range(16):
        h = i // 8
        base = i - i % 2
        if i % 2 == 0:
            for core in range(2):
                source = (base + core) * 2 + h
                first.append((source, (base + 1 - core) * 2 + core))
            core = 1 - h
            second.append(((base + core) * 2 + h, (base + core) * 2 + 1 - h))
    if not outward:
        return [p[::-1] for p in first], [p[::-1] for p in second]
    return first, second


def pair(flag, own, other, axis=0):
    return jnp.where(
        flag == 0,
        jnp.concatenate([own, other], axis),
        jnp.concatenate([other, own], axis),
    )


def pick(flag, first, second):
    return jnp.where(flag == 0, first, second)


class Spot:
    def __init__(self):
        self.d = lax.axis_index(DP)
        self.y = lax.axis_index(SEQ)
        self.z = self.d // 4
        self.x = (self.d // 2) % 2
        self.c = self.d % 2
        self.b = self.z % 2
        self.h = self.z // 2


class Flow:
    def __init__(self):
        self.chains = {}
        self.done = {}

    def add(self, name, chain):
        self.chains[name] = [chain, None, next(chain)]

    def step(self, values, names):
        for name in names:
            entry = self.chains[name]
            if entry[1] is not None:
                try:
                    entry[1:] = [None, entry[0].send(entry[1])]
                except StopIteration as end:
                    self.done[name] = end.value
                    del self.chains[name]
        moving = [name for name in names if name in self.chains]
        arrays = [[array for _, array in self.chains[name][2]] for name in moving]
        ended = [self.done[name] for name in names if name in self.done]
        values, arrays, ended = lax.optimization_barrier((list(values), arrays, ended))
        for name, value in zip([n for n in names if n in self.done], ended):
            self.done[name] = value
        for name, given in zip(moving, arrays):
            entry = self.chains[name]
            entry[1] = [route(array) for (route, _), array in zip(entry[2], given)]
        return values

    def finish(self, name):
        while name in self.chains:
            self.step([], [name])
        return self.done[name]


def by_core(value):
    return swap(value, 1)


def by_x(value):
    return swap(value, 2)


def by_z(value):
    return swap(value, 4)


def by_routes(pairs):
    return lambda value: lax.ppermute(value, BOTH, pairs)


def narrow(value):
    return value.astype(jnp.bfloat16)


def wide(value):
    return value.astype(jnp.float32)


def choose(value, axis, index):
    return lax.dynamic_index_in_dim(value, index, axis, keepdims=False)


def dot_rows(left, right):
    return jnp.einsum("tc,td->cd", left, right, preferred_element_type=jnp.float32)


def settle_x(spot, part):
    (given,) = yield [(by_x, choose(part, 1, 1 - spot.x))]
    return narrow(wide(choose(part, 1, spot.x)) + wide(given))


def settle_z(spot, part, holds):
    (given,) = yield [(by_z, choose(part, 0, 1 - spot.b))]
    block = wide(choose(part, 0, spot.b)) + wide(given)
    (given,) = yield [(by_routes(hop_pairs(holds, False)), narrow(block))]
    return block + wide(given)


def split_rows(spot, block):
    pieces = block.reshape(2, block.shape[0] // 2, block.shape[1])
    (given,) = yield [(by_core, narrow(choose(pieces, 0, 1 - spot.c)))]
    return jnp.where(spot.c == spot.h, choose(pieces, 0, spot.c), wide(given))


def quarters(own):
    rows, cols = own.shape
    return own.reshape(2, 2, rows // 4, cols)


def reduce_both(spot, halves, grads):
    mine = pick(spot.c, halves[0], halves[1])
    theirs = pick(spot.c, halves[1], halves[0])
    grad_own = pick(spot.y, grads[0], grads[1])
    grad_other = pick(spot.y, grads[1], grads[0])
    given = yield [(by_core, narrow(dot_rows(theirs, g))) for g in (grad_own, grad_other)]
    own = dot_rows(mine, grad_own) + wide(given[0])
    other = dot_rows(mine, grad_other) + wide(given[1])
    (given,) = yield [(swap_seq, narrow(other))]
    part = quarters(narrow(own + wide(given)))
    part = yield from settle_x(spot, part)
    block = yield from settle_z(spot, part, core_holds)
    return (yield from split_rows(spot, block))


def reduce_rows(spot, halves, grad):
    mine = pick(spot.c, halves[0], halves[1])
    theirs = pick(spot.c, halves[1], halves[0])
    (given,) = yield [(by_core, narrow(dot_rows(theirs, grad)))]
    part = quarters(narrow(dot_rows(mine, grad) + wide(given)))
    part = yield from settle_x(spot, part)
    block = yield from settle_z(spot, part, core_holds)
    return (yield from split_rows(spot, block))


def reduce_down(spot, left, grads):
    mine = pick(spot.c, grads[0], grads[1])
    theirs = pick(spot.c, grads[1], grads[0])
    (given,) = yield [(by_core, narrow(dot_rows(left, theirs)))]
    part = quarters(narrow(dot_rows(left, mine) + wide(given)))
    part = yield from settle_x(spot, part)
    block = yield from settle_z(spot, part, seq_holds)
    pieces = block.reshape(2, block.shape[0] // 2, block.shape[1])
    same, cross = choose(pieces, 0, spot.c), choose(pieces, 0, 1 - spot.c)
    first, second = corner_pairs(True)
    crossed, across = yield [(by_routes(first), narrow(cross)), (by_routes(second), narrow(same))]
    inner = jnp.where(spot.y == spot.h, same, wide(across))
    return jnp.where(spot.c == spot.y, inner, wide(crossed))


def total_over_all(value):
    for bit in (1, 2, 4, 8):
        value = value + swap(value, bit)
    return value + swap_seq(value)


def gather_images(spot, value):
    for bit, flag in ((1, spot.c), (2, spot.x), (4, spot.b), (8, spot.h)):
        value = pair(flag, value, swap(value, bit))
    return value


def attend(q_src, kv_src, gains, cosine, sine, heads, q_at, k_at, v_at, keys):
    width = heads * HEAD_DIM

    def heads_of(source, at):
        return source[:, at : at + width].reshape(source.shape[0], heads, HEAD_DIM)

    def prepared(source, at, which):
        v = normalize(heads_of(source, at)) * gains[which]
        if cosine is not None:
            q1, q2, q3, q4 = jnp.split(v, 4, axis=-1)
            other = jnp.concatenate([q2, q1, q4, q3], -1)
            v = v * cosine[:, None, :HEAD_DIM] + other * sine[:, None, :HEAD_DIM]
        return v.astype(jnp.bfloat16)

    q, k = prepared(q_src, q_at, 0), prepared(kv_src, k_at, 1)
    v = heads_of(kv_src, v_at).astype(jnp.bfloat16)
    s = jnp.einsum("qhd,khd->hqk", q, k, preferred_element_type=jnp.float32) * HEAD_DIM**-0.5
    s = jnp.where(jnp.arange(kv_src.shape[0]) < keys, s, -1e9)
    p = jax.nn.softmax(s, axis=-1).astype(jnp.bfloat16)
    o = jnp.einsum("hqk,khd->qhd", p, v, preferred_element_type=jnp.float32)
    return o.reshape(q_src.shape[0], width)


def attend_forward(
    q_src, kv_src, cosine, sine, gains, helpers, heads, q_at, k_at, v_at, keys
):
    q32, kv32 = q_src.astype(jnp.float32), kv_src.astype(jnp.float32)
    o, back = jax.vjp(
        lambda a, b, g: attend(a, b, g, cosine, sine, heads, q_at, k_at, v_at, keys),
        q32,
        kv32,
        gains[:2, :HEAD_DIM],
    )
    return narrow(o), back, None, None


def attend_backward(
    q_src, kv_src, cosine, sine, gains, helpers, back, kn, vn, out, grad_out, heads, q_at, k_at, v_at
):
    dq, dk, dg = back(grad_out.astype(jnp.float32))
    dg = jnp.pad(dg * gains[:2, :HEAD_DIM], ((0, 0), (0, LANES - HEAD_DIM)))
    if q_src is kv_src:
        return narrow(dq + dk), dg
    return narrow(dq), narrow(dk), dg


def rope_tables(pos_rows, pos_cols):
    quarter = HEAD_DIM // 4
    frequency = 10000.0 ** (-jnp.arange(quarter, dtype=jnp.float32) / quarter)
    row_angles = pos_rows[:, None] * frequency[None, :]
    col_angles = pos_cols[:, None] * frequency[None, :]
    angles = jnp.concatenate([row_angles, row_angles, col_angles, col_angles], -1)
    sign = jnp.where((jnp.arange(HEAD_DIM) // quarter) % 2 == 0, -1.0, 1.0)
    wide = ((0, 0), (0, LANES - HEAD_DIM))
    return jnp.pad(jnp.cos(angles), wide), jnp.pad(jnp.sin(angles) * sign[None, :], wide)


def gain_rows(gains):
    return jnp.pad(gains, ((0, 0), (0, LANES - HEAD_DIM)))


def gelu(values):
    return jax.nn.gelu(values, approximate=True)


def halves_of(value):
    mid = value.shape[1] // 2
    return value[:, :mid], value[:, mid:]


def norm_parts(values):
    center = values - jnp.mean(values, axis=-1, keepdims=True)
    scale = lax.rsqrt(jnp.mean(center * center, axis=-1, keepdims=True) + EPSILON)
    return center * scale, scale


def norm_grad(grad, values, gain):
    normal, scale = norm_parts(values)
    gain_grad = jnp.sum(grad * normal, axis=0)
    grad = grad * gain
    mean = jnp.mean(grad, axis=-1, keepdims=True)
    mean_product = jnp.mean(grad * normal, axis=-1, keepdims=True)
    return scale * (grad - mean - normal * mean_product), gain_grad


def fast_body(
    hidden_in,
    skip_in,
    clip_text,
    mt5_text,
    time_ids,
    null_text,
    loss_weight,
    patch_pos,
    out_cot,
    skip_weight,
    time_first,
    time_second,
    attn_qkv,
    attn_out,
    cross_qproj,
    cross_kvproj,
    cross_out,
    text_proj,
    mlp_up,
    mlp_down,
    norm_gains,
    head_gains,
):
    spot = Spot()
    _, local, width = hidden_in.shape
    narrow_width = width // 2
    heads_here = HEADS // 2
    clip_len = clip_text.shape[1]
    text_len = clip_len + mt5_text.shape[1]
    text_pad = -(-text_len // LANES) * LANES
    y = spot.y
    bf16 = jnp.bfloat16

    time_rows = lax.all_gather(jnp.concatenate([time_first, time_second], 0), DP)
    time_cut = time_first.shape[0]
    time_weights = [
        rows.reshape(-1, narrow_width) for rows in (time_rows[:, :time_cut], time_rows[:, time_cut:])
    ]
    flow = Flow()
    hidden = hidden_in[0]
    skip = skip_in[0]
    scaled_cot = out_cot[0].astype(jnp.float32) * loss_weight[0]
    cot_low = narrow(scaled_cot)
    pos = patch_pos[:, 0].astype(jnp.float32)
    pos_far = swap_seq(pos)

    def both_halves(value, axis=1):
        return pair(y, value, swap_seq(value), axis)

    a, m, e = (attn_qkv[:, i * narrow_width : (i + 1) * narrow_width] for i in range(3))
    moved = swap_seq(m)
    qkv_shard = jnp.concatenate([pick(y, a, moved), pick(y, e, a), pick(y, moved, e)], 1)

    def gather(shard):
        return lax.all_gather(shard, DP, axis=0, tiled=True)

    def with_far(own):
        return own, swap_seq(own)

    def scatter_rows(grad):
        return wide(lax.psum_scatter(narrow(grad), DP, scatter_dimension=0, tiled=True))

    def scatter_both(grad):
        first, second = halves_of(scatter_rows(grad))
        return pick(y, first, second) + wide(swap_seq(narrow(pick(y, second, first))))

    def times(value, sides):
        return pair(y, project(value, sides[0]), project(value, sides[1]), 1)

    def times_back(grad, sides):
        first, second = halves_of(grad)
        own, far = pick(y, first, second), pick(y, second, first)
        return project_back(own, sides[0]) + project_back(far, sides[1])

    w_skip = with_far(gather(skip_weight))
    w_qkv = gather(qkv_shard)
    w_text = gather(text_proj)
    w_ckv = gather(cross_kvproj)
    out_rows = lax.all_gather(jnp.concatenate([attn_out, cross_qproj, cross_out], 0), DP)
    out_sides = with_far(out_rows.reshape(out_rows.shape[0], 3, -1, narrow_width))
    w_aout, w_cq, w_cout = (
        tuple(side[:, k].reshape(-1, narrow_width) for side in out_sides) for k in range(3)
    )
    w_up = gather(mlp_up)
    down_rows = lax.all_gather(mlp_down, DP)
    middle = down_rows.shape[0] // 2
    upper_rows, lower_rows = down_rows[:middle], down_rows[middle:]
    w_down = tuple(
        side.reshape(-1, narrow_width)
        for side in (
            pick(y, upper_rows, lower_rows),
            swap_seq(pick(y, lower_rows, upper_rows)),
        )
    )
    cot_far = swap_seq(cot_low)

    feats = time_features(time_ids).astype(bf16)
    before = both_halves(project(feats, time_weights[0]))
    lifted = jax.nn.silu(before).astype(bf16)
    shift = both_halves(project(lifted, time_weights[1]))

    cosine, sine = rope_tables(*jnp.concatenate([pos, pos_far], 1))
    helpers = []
    merged = times(jnp.concatenate([hidden, skip], -1), w_skip)
    resid0 = scaled_norm(merged, norm_gains[0])
    normed1 = narrow(scaled_norm(resid0, norm_gains[1]) + shift)

    normed1_both = jnp.concatenate([normed1, swap_seq(normed1)], 0)
    packed = narrow(project(normed1_both, w_qkv))
    self_gains = gain_rows(head_gains[0:2])
    self_o, self_q, self_k, self_v = attend_forward(
        packed,
        packed,
        cosine,
        sine,
        self_gains,
        helpers,
        heads_here,
        0,
        narrow_width,
        2 * narrow_width,
        2 * local,
    )
    far_o = swap_seq(self_o[local:])

    keep_text = (1 - null_text[0]).astype(bf16)
    projected = both_halves(narrow(project(mt5_text[0], w_text)))
    context = jnp.concatenate([clip_text[0], projected], 0) * keep_text
    context = jnp.pad(context, ((0, text_pad - text_len), (0, 0)))
    text_kv = both_halves(narrow(project(context, w_ckv)))
    own_o = self_o[:local]

    attn_halves = pick(y, own_o, far_o), pick(y, far_o, own_o)
    attn_flat = jnp.concatenate(attn_halves, 1)
    resid1 = resid0 + times(attn_flat, w_aout)
    normed2 = narrow(scaled_norm(resid1, norm_gains[2]))
    cross_pre = narrow(times(normed2, w_cq))
    cross_gains = gain_rows(head_gains[2:4])
    cross_o, cross_q, cross_k, cross_v = attend_forward(
        cross_pre, text_kv, None, None, cross_gains, helpers, HEADS, 0, 0, width, text_len
    )
    resid2 = resid1 + times(cross_o, w_cout)
    normed3 = narrow(scaled_norm(resid2, norm_gains[3]))

    normed3_both = jnp.concatenate([normed3, swap_seq(normed3)], 0)
    upper = narrow(project(normed3_both, w_up))
    active = narrow(gelu(upper.astype(jnp.float32)))
    mixed = times(active, w_down)
    final = resid2 + mixed[:local] + wide(swap_seq(narrow(mixed[local:])))
    block_out = narrow(final)[None]

    cot_both = jnp.concatenate([cot_low, cot_far], 0)
    d_active = times_back(cot_both, w_down)
    _, gelu_back = jax.vjp(gelu, upper.astype(jnp.float32))
    d_upper = narrow(gelu_back(d_active)[0])
    flow.add(8, reduce_down(spot, active, halves_of(cot_both)))
    (d_upper,) = flow.step([d_upper], [8])
    d_both = project_back(d_upper, w_up)
    d_far = swap_seq(narrow(d_both[local:]))
    flow.add(7, reduce_rows(spot, halves_of(normed3_both), d_upper))
    d_own, d_far = flow.step([d_both[:local], d_far], [8, 7])
    d_normed3 = d_own + wide(d_far)
    d_resid, d_gain3 = norm_grad(d_normed3, resid2, norm_gains[3])
    resid_grad = scaled_cot + d_resid

    grad_low = narrow(resid_grad)
    d_cmix = narrow(times_back(grad_low, w_cout))
    g_cout = scatter_both(dot_rows(cross_o, grad_low))
    d_cpre, d_textkv, d_cross_gains = attend_backward(
        cross_pre,
        text_kv,
        None,
        None,
        cross_gains,
        helpers,
        cross_q,
        cross_k,
        cross_v,
        cross_o,
        d_cmix,
        HEADS,
        0,
        0,
        width,
    )
    g_cquery = scatter_both(dot_rows(normed2, d_cpre))
    d_cpre, d_textkv = flow.step([d_cpre, d_textkv], [8, 7])
    d_text = halves_of(d_textkv)
    d_text_far = swap_seq(pick(y, d_text[1], d_text[0]))
    d_normed2 = times_back(d_cpre, w_cq)
    d_resid, d_gain2 = norm_grad(d_normed2, resid1, norm_gains[2])
    resid_grad = resid_grad + d_resid
    grad_low = narrow(resid_grad)
    d_attn = halves_of(narrow(times_back(grad_low, w_aout)))
    d_far = swap_seq(pick(y, d_attn[1], d_attn[0]))
    d_text = narrow(wide(pick(y, d_text[0], d_text[1])) + wide(d_text_far))
    g_aout = scatter_both(dot_rows(attn_flat, grad_low))
    g_ckv = scatter_rows(dot_rows(context, d_text))
    d_context = halves_of(project_back(d_text[clip_len:text_len], w_ckv))
    d_context_far = swap_seq(narrow(pick(y, d_context[1], d_context[0])))
    d_proj = pick(y, d_context[0], d_context[1]) + wide(d_context_far)
    d_proj = narrow(d_proj * keep_text.astype(jnp.float32))
    g_tproj = scatter_rows(dot_rows(mt5_text[0], d_proj))

    d_heads = jnp.concatenate([pick(y, d_attn[0], d_attn[1]), d_far], 0)
    (d_heads,) = flow.step([d_heads], [8])
    d_packed, d_self_gains = attend_backward(
        packed,
        packed,
        cosine,
        sine,
        self_gains,
        helpers,
        self_q,
        self_k,
        self_v,
        self_o,
        d_heads,
        heads_here,
        0,
        narrow_width,
        2 * narrow_width,
    )
    (d_packed,) = flow.step([d_packed], [8, 7])
    d_both = project_back(d_packed, w_qkv)
    d_far = swap_seq(narrow(d_both[local:]))
    flow.add(1, reduce_rows(spot, halves_of(normed1_both), d_packed))
    d_own, d_far = flow.step(
        [d_both[:local], d_far],
        [7, 1],
    )
    d_normed1 = d_own + wide(d_far)

    d_shift = jnp.sum(d_normed1, axis=0)
    d_resid, d_gain1 = norm_grad(d_normed1, resid0, norm_gains[1])
    resid_grad = resid_grad + d_resid
    d_merged, d_gain0 = norm_grad(resid_grad, merged, norm_gains[0])
    d_merged = narrow(d_merged)
    flow.add(0, reduce_both(spot, (hidden, skip), halves_of(d_merged)))
    (d_merged,) = flow.step(
        [d_merged],
        [0, 7, 1],
    )
    d_joined = times_back(d_merged, w_skip)
    hidden_grad, skip_grad = d_joined[:, :width][None], d_joined[:, width:][None]

    d_shift = d_shift + swap_seq(d_shift)
    features = jnp.pad(feats.astype(jnp.float32), ((0, 0), (0, width - FREQ)))
    rows = gather_images(spot, jnp.stack([before[0], features[0], d_shift], 0)[None])
    before_all, features_all, d_shift_all = rows[:, 0], rows[:, 1, :FREQ], rows[:, 2]
    silu_all, silu_back = jax.vjp(jax.nn.silu, before_all)
    lifted_all = wide(narrow(silu_all))
    d_shift_cols = pick(y, *halves_of(d_shift_all))
    d_lifted = jnp.einsum(
        "bd,cd->bc", d_shift_cols, time_weights[1].astype(jnp.float32), precision=HIGHEST
    )
    d_before = silu_back(d_lifted + swap_seq(d_lifted))[0]

    def block(left, cols, left_rows):
        mine = lax.dynamic_slice_in_dim(left, spot.d * left_rows, left_rows, 1)
        return jnp.einsum("bc,bd->cd", mine, cols, precision=HIGHEST)

    g_tsecond = block(lifted_all, d_shift_cols, time_second.shape[0])
    g_tfirst = block(features_all, pick(y, *halves_of(d_before)), time_first.shape[0])

    d_head_gains = jnp.concatenate([d_self_gains, d_cross_gains], 0)[:, :HEAD_DIM] / head_gains
    d_norm_gains = jnp.stack([d_gain0, d_gain1, d_gain2, d_gain3], 0)
    totals = total_over_all(
        jnp.concatenate([d_norm_gains.reshape(-1), d_head_gains.reshape(-1)])
    )
    norm_total = totals[: 4 * width].reshape(4, width)
    head_total = totals[4 * width :].reshape(4, HEAD_DIM)

    while flow.chains:
        flow.step([], list(flow.chains))
    g_skipw, g_qkv, g_up, g_down = (flow.done[name] for name in (0, 1, 7, 8))
    q_cols, k_cols, v_cols = (
        g_qkv[:, i * narrow_width : (i + 1) * narrow_width] for i in range(3)
    )
    moved = wide(swap_seq(narrow(pick(y, v_cols, q_cols))))
    g_qkv = jnp.concatenate([pick(y, q_cols, k_cols), moved, pick(y, k_cols, v_cols)], 1)
    return (
        block_out,
        hidden_grad,
        skip_grad,
        g_skipw,
        g_tfirst,
        g_tsecond,
        g_qkv,
        g_aout,
        g_cquery,
        g_ckv,
        g_cout,
        g_tproj,
        g_up,
        g_down,
        norm_total,
        head_total,
    )


def solution(mesh):
    placed = (
        P(DP, SEQ, None),
        P(DP, SEQ, None),
        P(DP, None, None),
        P(DP, None, None),
        P(DP),
        P(DP),
        P(DP),
        P(None, DP, SEQ),
        P(DP, SEQ, None),
        P(DP, SEQ),
        P(DP, SEQ),
        P(DP, SEQ),
        P(DP, SEQ),
        P(DP, SEQ),
        P(DP, SEQ),
        P(DP, SEQ),
        P(DP, SEQ),
        P(DP, SEQ),
        P(DP, SEQ),
        P(DP, SEQ),
        P(),
        P(),
    )
    split = mesh.shape[DP] == 16 and mesh.shape[SEQ] == 2
    return jax.shard_map(
        fast_body if split else whole_body,
        mesh=mesh,
        in_specs=placed,
        out_specs=(
            P(DP, SEQ, None),
            P(DP, SEQ, None),
            P(DP, SEQ, None),
            P(DP, SEQ),
            P(DP, SEQ),
            P(DP, SEQ),
            P(DP, SEQ),
            P(DP, SEQ),
            P(DP, SEQ),
            P(DP, SEQ),
            P(DP, SEQ),
            P(DP, SEQ),
            P(DP, SEQ),
            P(DP, SEQ),
            P(),
            P(),
        ),
        check_vma=False,
    )
```

```python
import math

import jax
import jax.numpy as jnp
from jax import lax
from jax.sharding import PartitionSpec as P

DP = "dp"
SEQ = "seq"
HEADS = 16
HEAD_DIM = 88
FREQ = 256


EPSILON = 1e-06
HIGHEST = lax.Precision.HIGHEST


def normalize(values):
    center = values - jnp.mean(values, axis=-1, keepdims=True)
    variance = jnp.mean(center * center, axis=-1, keepdims=True)
    return center * lax.rsqrt(variance + EPSILON)


def scaled_norm(values, gain_row):
    return normalize(values) * gain_row


def rotate(values, pos_rows, pos_cols):
    quarter = values.shape[-1] // 4
    frequency = 10000.0 ** (-jnp.arange(quarter, dtype=jnp.float32) / quarter)

    def turn(halfpart, position):
        angles = position[:, None] * frequency[None, :]
        cosine = jnp.cos(angles)[:, None, :]
        sine_part = jnp.sin(angles)[:, None, :]
        former = halfpart[..., :quarter]
        latter = halfpart[..., quarter:]
        return jnp.concatenate(
            [former * cosine - latter * sine_part, former * sine_part + latter * cosine], -1
        )

    return jnp.concatenate(
        [turn(values[..., : 2 * quarter], pos_rows), turn(values[..., 2 * quarter :], pos_cols)], -1
    )


def time_features(step_ids):
    half_count = FREQ // 2
    frequency = jnp.exp(-math.log(10000.0) * jnp.arange(half_count, dtype=jnp.float32) / half_count)
    angles = step_ids.astype(jnp.float32)[:, None] * frequency[None, :]
    return jnp.concatenate([jnp.cos(angles), jnp.sin(angles)], -1)


def project(left, right):
    return jnp.einsum("tc,cd->td", left, right, preferred_element_type=jnp.float32)


def project_back(grad_low, right):
    return jnp.einsum("td,cd->tc", grad_low, right, preferred_element_type=jnp.float32)


def weight_grad(left, grad_low):
    return jnp.einsum("tc,td->cd", left, grad_low, preferred_element_type=jnp.float32)


def whole_body(
    hidden_in,
    skip_in,
    clip_text,
    mt5_text,
    time_ids,
    null_text,
    loss_weight,
    patch_pos,
    out_cot,
    skip_weight,
    time_first,
    time_second,
    attn_qkv,
    attn_out,
    cross_qproj,
    cross_kvproj,
    cross_out,
    text_proj,
    mlp_up,
    mlp_down,
    norm_gains,
    head_gains,
):
    images, local, width = hidden_in.shape
    groups = lax.axis_size(SEQ)
    heads_here = HEADS // groups
    narrow = width // groups
    tokens = images * local
    full_len = local * groups
    clip_len = clip_text.shape[1]
    text_len = clip_len + mt5_text.shape[1]
    score_scale = HEAD_DIM ** (-0.5)
    pos_rows = patch_pos[0].reshape(tokens).astype(jnp.float32)
    pos_cols = patch_pos[1].reshape(tokens).astype(jnp.float32)
    col_full = (
        lax.all_gather(skip_weight, SEQ, axis=1, tiled=True),
        lax.all_gather(time_first, SEQ, axis=1, tiled=True),
        lax.all_gather(time_second, SEQ, axis=1, tiled=True),
        lax.all_gather(attn_qkv, SEQ, axis=1, tiled=True),
        lax.all_gather(attn_out, SEQ, axis=1, tiled=True),
        lax.all_gather(cross_qproj, SEQ, axis=1, tiled=True),
        lax.all_gather(cross_kvproj, SEQ, axis=1, tiled=True),
        lax.all_gather(cross_out, SEQ, axis=1, tiled=True),
        lax.all_gather(text_proj, SEQ, axis=1, tiled=True),
        lax.all_gather(mlp_up, SEQ, axis=1, tiled=True),
        lax.all_gather(mlp_down, SEQ, axis=1, tiled=True),
    )
    weight_set = (
        lax.all_gather(col_full[0], DP, axis=0, tiled=True),
        lax.all_gather(col_full[1], DP, axis=0, tiled=True),
        lax.all_gather(col_full[2], DP, axis=0, tiled=True),
        lax.all_gather(col_full[3], DP, axis=0, tiled=True),
        lax.all_gather(col_full[4], DP, axis=0, tiled=True),
        lax.all_gather(col_full[5], DP, axis=0, tiled=True),
        lax.all_gather(col_full[6], DP, axis=0, tiled=True),
        lax.all_gather(col_full[7], DP, axis=0, tiled=True),
        lax.all_gather(col_full[8], DP, axis=0, tiled=True),
        lax.all_gather(col_full[9], DP, axis=0, tiled=True),
        lax.all_gather(col_full[10], DP, axis=0, tiled=True),
    )
    w_skip, w_first, w_second, w_qkv, w_aout, w_cq, w_ckv, w_cout, w_text, w_up, w_down = weight_set
    joined = jnp.concatenate([hidden_in, skip_in], -1).reshape(tokens, 2 * width)
    merged = project(joined, w_skip)
    resid0 = scaled_norm(merged, norm_gains[0])
    feats = time_features(time_ids).astype(jnp.bfloat16)
    before = project(feats, w_first)
    lifted = jax.nn.silu(before).astype(jnp.bfloat16)
    shift = project(lifted, w_second)
    shift_tok = jnp.repeat(shift, local, axis=0)
    normed1 = (scaled_norm(resid0, norm_gains[1]) + shift_tok).astype(jnp.bfloat16)
    packed = project(normed1, w_qkv).reshape(tokens, 3, HEADS, HEAD_DIM)

    def query_prep(values, gain_row):
        return rotate(scaled_norm(values, gain_row), pos_rows, pos_cols)

    self_q = query_prep(packed[:, 0], head_gains[0]).astype(jnp.bfloat16)
    self_k = query_prep(packed[:, 1], head_gains[1]).astype(jnp.bfloat16)
    self_v = packed[:, 2].astype(jnp.bfloat16)
    stacked = jnp.stack([self_q, self_k, self_v], 1).reshape(images, local, 3, width)

    def self_block(operand):
        queries, keyset, valueset = operand
        scores = (
            jnp.einsum("qd,kd->qk", queries, keyset, preferred_element_type=jnp.float32)
            * score_scale
        )
        top_score = jnp.max(scores, axis=-1, keepdims=True)
        exponent = jnp.exp(scores - top_score)
        totals = jnp.sum(exponent, axis=-1, keepdims=True)
        mixed_out = jnp.einsum(
            "qk,kd->qd",
            (exponent / totals).astype(jnp.bfloat16),
            valueset,
            preferred_element_type=jnp.float32,
        )
        return (mixed_out.astype(jnp.bfloat16), (top_score + jnp.log(totals))[:, 0])

    pieces = lax.all_to_all(stacked, SEQ, split_axis=3, concat_axis=1, tiled=True)
    item_count = pieces.shape[0]
    length = pieces.shape[1]
    split_heads = pieces.reshape(item_count, length, 3, heads_here, HEAD_DIM)
    triple_set = jnp.transpose(split_heads, (2, 0, 3, 1, 4)).reshape(
        3, item_count * heads_here, length, HEAD_DIM
    )
    mixed_out, logsum = lax.map(self_block, (triple_set[0], triple_set[1], triple_set[2]))
    joined_heads = jnp.transpose(
        mixed_out.reshape(item_count, heads_here, length, HEAD_DIM), (0, 2, 1, 3)
    ).reshape(item_count, length, narrow)
    returned = lax.all_to_all(joined_heads, SEQ, split_axis=1, concat_axis=2, tiled=True)
    self_logsum = logsum.reshape(item_count, heads_here, length)
    attn_flat = returned.reshape(tokens, width)
    resid1 = resid0 + project(attn_flat, w_aout)
    normed2 = scaled_norm(resid1, norm_gains[2]).astype(jnp.bfloat16)
    cross_pre = project(normed2, w_cq).reshape(tokens, HEADS, HEAD_DIM)
    cross_q = (
        scaled_norm(cross_pre, head_gains[2])
        .astype(jnp.bfloat16)
        .reshape(images, local, HEADS, HEAD_DIM)
    )
    keep_text = (1 - null_text).astype(jnp.bfloat16)
    projected = jnp.einsum(
        "btc,cd->btd", mt5_text, w_text, preferred_element_type=jnp.float32
    ).astype(jnp.bfloat16)
    context = jnp.concatenate([clip_text, projected], 1) * keep_text[:, None, None]
    text_kv = jnp.einsum("btc,cd->btd", context, w_ckv, preferred_element_type=jnp.float32).reshape(
        images, text_len, 2, HEADS, HEAD_DIM
    )
    cross_k = scaled_norm(text_kv[:, :, 0], head_gains[3]).astype(jnp.bfloat16)
    cross_v = text_kv[:, :, 1].astype(jnp.bfloat16)
    cross_scores = (
        jnp.einsum("bqhd,bkhd->bhqk", cross_q, cross_k, preferred_element_type=jnp.float32)
        * score_scale
    )
    cross_top = jnp.max(cross_scores, axis=-1, keepdims=True)
    cross_exp = jnp.exp(cross_scores - cross_top)
    cross_total = jnp.sum(cross_exp, axis=-1, keepdims=True)
    cross_logsum = cross_top + jnp.log(cross_total)
    cross_mix = jnp.einsum(
        "bhqk,bkhd->bqhd",
        (cross_exp / cross_total).astype(jnp.bfloat16),
        cross_v,
        preferred_element_type=jnp.float32,
    ).astype(jnp.bfloat16)
    cross_flat = cross_mix.reshape(tokens, width)
    resid2 = resid1 + project(cross_flat, w_cout)
    normed3 = scaled_norm(resid2, norm_gains[3]).astype(jnp.bfloat16)
    upper = project(normed3, w_up)
    active = jax.nn.gelu(upper, approximate=True).astype(jnp.bfloat16)
    final = resid2 + project(active, w_down)
    block_out = final.astype(jnp.bfloat16).reshape(images, local, width)
    again_full = (
        lax.all_gather(skip_weight, SEQ, axis=1, tiled=True),
        lax.all_gather(time_first, SEQ, axis=1, tiled=True),
        lax.all_gather(time_second, SEQ, axis=1, tiled=True),
        lax.all_gather(attn_qkv, SEQ, axis=1, tiled=True),
        lax.all_gather(attn_out, SEQ, axis=1, tiled=True),
        lax.all_gather(cross_qproj, SEQ, axis=1, tiled=True),
        lax.all_gather(cross_kvproj, SEQ, axis=1, tiled=True),
        lax.all_gather(cross_out, SEQ, axis=1, tiled=True),
        lax.all_gather(text_proj, SEQ, axis=1, tiled=True),
        lax.all_gather(mlp_up, SEQ, axis=1, tiled=True),
        lax.all_gather(mlp_down, SEQ, axis=1, tiled=True),
    )
    weight_set = (
        lax.all_gather(again_full[0], DP, axis=0, tiled=True),
        lax.all_gather(again_full[1], DP, axis=0, tiled=True),
        lax.all_gather(again_full[2], DP, axis=0, tiled=True),
        lax.all_gather(again_full[3], DP, axis=0, tiled=True),
        lax.all_gather(again_full[4], DP, axis=0, tiled=True),
        lax.all_gather(again_full[5], DP, axis=0, tiled=True),
        lax.all_gather(again_full[6], DP, axis=0, tiled=True),
        lax.all_gather(again_full[7], DP, axis=0, tiled=True),
        lax.all_gather(again_full[8], DP, axis=0, tiled=True),
        lax.all_gather(again_full[9], DP, axis=0, tiled=True),
        lax.all_gather(again_full[10], DP, axis=0, tiled=True),
    )
    w_skip, w_first, w_second, w_qkv, w_aout, w_cq, w_ckv, w_cout, w_text, w_up, w_down = weight_set
    scaled_cot = (out_cot.astype(jnp.float32) * loss_weight[:, None, None]).reshape(tokens, width)
    grad_low = scaled_cot.astype(jnp.bfloat16)
    g_down = weight_grad(active, grad_low)
    d_active = project_back(grad_low, w_down)
    upper_vals, gelu_back = jax.vjp(lambda values: jax.nn.gelu(values, approximate=True), upper)
    d_upper = gelu_back(d_active)[0].astype(jnp.bfloat16)
    g_up = weight_grad(normed3, d_upper)
    d_normed3 = project_back(d_upper, w_up)
    norm_vals, norm_back = jax.vjp(scaled_norm, resid2, norm_gains[3])
    d_resid, d_gain3 = norm_back(d_normed3)
    resid_grad = scaled_cot + d_resid
    grad_low = resid_grad.astype(jnp.bfloat16)
    g_cout = weight_grad(cross_flat, grad_low)
    d_cmix = (
        project_back(grad_low, w_cout).astype(jnp.bfloat16).reshape(images, local, HEADS, HEAD_DIM)
    )
    cross_weights = jnp.exp(cross_scores - cross_logsum)
    d_cweights = jnp.einsum("bqhd,bkhd->bhqk", d_cmix, cross_v, preferred_element_type=jnp.float32)
    row_dot = jnp.sum(cross_weights * d_cweights, axis=-1, keepdims=True)
    d_cscores = (cross_weights * (d_cweights - row_dot)).astype(jnp.bfloat16)
    d_cquery = (
        jnp.einsum("bhqk,bkhd->bqhd", d_cscores, cross_k, preferred_element_type=jnp.float32)
        * score_scale
    ).astype(jnp.bfloat16)
    d_ckey = (
        jnp.einsum("bhqk,bqhd->bkhd", d_cscores, cross_q, preferred_element_type=jnp.float32)
        * score_scale
    )
    d_cval = jnp.einsum(
        "bhqk,bqhd->bkhd",
        cross_weights.astype(jnp.bfloat16),
        d_cmix,
        preferred_element_type=jnp.float32,
    )
    cq_vals, cq_back = jax.vjp(scaled_norm, cross_pre, head_gains[2])
    d_cpre, d_hgain2 = cq_back(d_cquery.astype(jnp.float32).reshape(tokens, HEADS, HEAD_DIM))
    d_cpre_low = d_cpre.reshape(tokens, width).astype(jnp.bfloat16)
    g_cquery = weight_grad(normed2, d_cpre_low)
    d_normed2 = project_back(d_cpre_low, w_cq)
    norm_vals, norm_back = jax.vjp(scaled_norm, resid1, norm_gains[2])
    d_resid, d_gain2 = norm_back(d_normed2)
    resid_grad = resid_grad + d_resid
    ck_vals, ck_back = jax.vjp(scaled_norm, text_kv[:, :, 0], head_gains[3])
    d_kpre, d_hgain3 = ck_back(d_ckey)
    d_textkv = (
        jnp.stack([d_kpre, d_cval], 2).reshape(images, text_len, 2 * width).astype(jnp.bfloat16)
    )
    g_ckv = jnp.einsum("btc,btd->cd", context, d_textkv, preferred_element_type=jnp.float32)
    d_context = jnp.einsum("btd,cd->btc", d_textkv, w_ckv, preferred_element_type=jnp.float32)
    d_proj = (d_context[:, clip_len:] * keep_text.astype(jnp.float32)[:, None, None]).astype(
        jnp.bfloat16
    )
    g_tproj = jnp.einsum("btc,btd->cd", mt5_text, d_proj, preferred_element_type=jnp.float32)
    grad_low = resid_grad.astype(jnp.bfloat16)
    g_aout = weight_grad(attn_flat, grad_low)
    d_attn = project_back(grad_low, w_aout).astype(jnp.bfloat16).reshape(images, local, width)
    d_heads = lax.all_to_all(d_attn, SEQ, split_axis=2, concat_axis=1, tiled=True)

    def self_back(operand):
        queries, keyset, valueset, d_mixed, logsum = operand
        scores = (
            jnp.einsum("qd,kd->qk", queries, keyset, preferred_element_type=jnp.float32)
            * score_scale
        )
        weights = jnp.exp(scores - logsum[:, None])
        d_weights = jnp.einsum("qd,kd->qk", d_mixed, valueset, preferred_element_type=jnp.float32)
        row_sum = jnp.sum(weights * d_weights, axis=-1, keepdims=True)
        d_scores = (weights * (d_weights - row_sum)).astype(jnp.bfloat16)
        d_query = (
            jnp.einsum("qk,kd->qd", d_scores, keyset, preferred_element_type=jnp.float32)
            * score_scale
        )
        d_key = (
            jnp.einsum("qk,qd->kd", d_scores, queries, preferred_element_type=jnp.float32)
            * score_scale
        )
        d_value = jnp.einsum(
            "qk,qd->kd", weights.astype(jnp.bfloat16), d_mixed, preferred_element_type=jnp.float32
        )
        return (
            d_query.astype(jnp.bfloat16),
            d_key.astype(jnp.bfloat16),
            d_value.astype(jnp.bfloat16),
        )

    head_split = pieces.reshape(images, full_len, 3, heads_here, HEAD_DIM)
    triple_set = jnp.transpose(head_split, (2, 0, 3, 1, 4)).reshape(
        3, images * heads_here, full_len, HEAD_DIM
    )
    d_split = jnp.transpose(
        d_heads.reshape(images, full_len, heads_here, HEAD_DIM), (0, 2, 1, 3)
    ).reshape(images * heads_here, full_len, HEAD_DIM)
    d_query, d_key, d_value = lax.map(
        self_back,
        (
            triple_set[0],
            triple_set[1],
            triple_set[2],
            d_split,
            self_logsum.reshape(images * heads_here, full_len),
        ),
    )
    d_triple = jnp.stack([d_query, d_key, d_value], 0).reshape(
        3, images, heads_here, full_len, HEAD_DIM
    )
    d_triple = jnp.transpose(d_triple, (1, 3, 0, 2, 4)).reshape(images, full_len, 3, narrow)
    d_stacked = lax.all_to_all(d_triple, SEQ, split_axis=1, concat_axis=3, tiled=True)
    d_packed_in = d_stacked.reshape(tokens, 3, HEADS, HEAD_DIM).astype(jnp.float32)
    q_vals, q_back = jax.vjp(query_prep, packed[:, 0], head_gains[0])
    d_qpre, d_hgain0 = q_back(d_packed_in[:, 0])
    k_vals, k_back = jax.vjp(query_prep, packed[:, 1], head_gains[1])
    d_kself, d_hgain1 = k_back(d_packed_in[:, 1])
    d_packed = (
        jnp.stack([d_qpre, d_kself, d_packed_in[:, 2]], 1)
        .reshape(tokens, 3 * width)
        .astype(jnp.bfloat16)
    )
    g_qkv = weight_grad(normed1, d_packed)
    d_normed1 = project_back(d_packed, w_qkv)
    d_shift = jnp.sum(d_normed1.reshape(images, local, width), axis=1)
    norm_vals, norm_back = jax.vjp(scaled_norm, resid0, norm_gains[1])
    d_resid, d_gain1 = norm_back(d_normed1)
    resid_grad = resid_grad + d_resid
    g_tsecond = jnp.einsum("bc,bd->cd", lifted.astype(jnp.float32), d_shift, precision=HIGHEST)
    d_lifted = jnp.einsum("bd,cd->bc", d_shift, w_second.astype(jnp.float32), precision=HIGHEST)
    silu_vals, silu_back = jax.vjp(jax.nn.silu, before)
    d_before = silu_back(d_lifted)[0]
    g_tfirst = jnp.einsum("bc,bd->cd", feats.astype(jnp.float32), d_before, precision=HIGHEST)
    norm_vals, norm_back = jax.vjp(scaled_norm, merged, norm_gains[0])
    d_merged, d_gain0 = norm_back(resid_grad)
    d_merged_low = d_merged.astype(jnp.bfloat16)
    g_skipw = weight_grad(joined, d_merged_low)
    d_joined = project_back(d_merged_low, w_skip)
    hidden_grad = d_joined[:, :width].reshape(images, local, width)
    skip_grad = d_joined[:, width:].reshape(images, local, width)
    row_sums = (
        lax.psum_scatter(
            g_skipw.astype(jnp.bfloat16), DP, scatter_dimension=0, tiled=True
        ).astype(jnp.float32),
        lax.psum_scatter(
            g_tfirst.astype(jnp.bfloat16), DP, scatter_dimension=0, tiled=True
        ).astype(jnp.float32),
        lax.psum_scatter(
            g_tsecond.astype(jnp.bfloat16), DP, scatter_dimension=0, tiled=True
        ).astype(jnp.float32),
        lax.psum_scatter(g_qkv.astype(jnp.bfloat16), DP, scatter_dimension=0, tiled=True).astype(
            jnp.float32
        ),
        lax.psum_scatter(g_aout.astype(jnp.bfloat16), DP, scatter_dimension=0, tiled=True).astype(
            jnp.float32
        ),
        lax.psum_scatter(
            g_cquery.astype(jnp.bfloat16), DP, scatter_dimension=0, tiled=True
        ).astype(jnp.float32),
        lax.psum_scatter(g_ckv.astype(jnp.bfloat16), DP, scatter_dimension=0, tiled=True).astype(
            jnp.float32
        ),
        lax.psum_scatter(g_cout.astype(jnp.bfloat16), DP, scatter_dimension=0, tiled=True).astype(
            jnp.float32
        ),
        lax.psum_scatter(
            g_tproj.astype(jnp.bfloat16), DP, scatter_dimension=0, tiled=True
        ).astype(jnp.float32),
        lax.psum_scatter(g_up.astype(jnp.bfloat16), DP, scatter_dimension=0, tiled=True).astype(
            jnp.float32
        ),
        lax.psum_scatter(g_down.astype(jnp.bfloat16), DP, scatter_dimension=0, tiled=True).astype(
            jnp.float32
        ),
    )
    owned = (
        lax.psum_scatter(
            row_sums[0].astype(jnp.bfloat16), SEQ, scatter_dimension=1, tiled=True
        ).astype(jnp.float32),
        lax.psum_scatter(
            row_sums[1].astype(jnp.bfloat16), SEQ, scatter_dimension=1, tiled=True
        ).astype(jnp.float32),
        lax.psum_scatter(
            row_sums[2].astype(jnp.bfloat16), SEQ, scatter_dimension=1, tiled=True
        ).astype(jnp.float32),
        lax.psum_scatter(
            row_sums[3].astype(jnp.bfloat16), SEQ, scatter_dimension=1, tiled=True
        ).astype(jnp.float32),
        lax.psum_scatter(
            row_sums[4].astype(jnp.bfloat16), SEQ, scatter_dimension=1, tiled=True
        ).astype(jnp.float32),
        lax.psum_scatter(
            row_sums[5].astype(jnp.bfloat16), SEQ, scatter_dimension=1, tiled=True
        ).astype(jnp.float32),
        lax.psum_scatter(
            row_sums[6].astype(jnp.bfloat16), SEQ, scatter_dimension=1, tiled=True
        ).astype(jnp.float32),
        lax.psum_scatter(
            row_sums[7].astype(jnp.bfloat16), SEQ, scatter_dimension=1, tiled=True
        ).astype(jnp.float32),
        lax.psum_scatter(
            row_sums[8].astype(jnp.bfloat16), SEQ, scatter_dimension=1, tiled=True
        ).astype(jnp.float32),
        lax.psum_scatter(
            row_sums[9].astype(jnp.bfloat16), SEQ, scatter_dimension=1, tiled=True
        ).astype(jnp.float32),
        lax.psum_scatter(
            row_sums[10].astype(jnp.bfloat16), SEQ, scatter_dimension=1, tiled=True
        ).astype(jnp.float32),
    )
    gain_totals = lax.psum(
        (
            jnp.stack([d_gain0, d_gain1, d_gain2, d_gain3], 0),
            jnp.stack([d_hgain0, d_hgain1, d_hgain2, d_hgain3], 0),
        ),
        (DP, SEQ),
    )
    return (
        block_out,
        hidden_grad,
        skip_grad,
        owned[0],
        owned[1],
        owned[2],
        owned[3],
        owned[4],
        owned[5],
        owned[6],
        owned[7],
        owned[8],
        owned[9],
        owned[10],
        gain_totals[0],
        gain_totals[1],
    )


BOTH = (DP, SEQ)
FLIP = [(0, 1), (1, 0)]
LOG2E = 1.4426950408889634
LANES = 128


def swap(value, bit):
    return lax.ppermute(value, DP, [(i, i ^ bit) for i in range(16)])


def swap_seq(value):
    return lax.ppermute(value, SEQ, FLIP)


def core_holds(dp_index, seq_index):
    return dp_index % 2 == dp_index // 8


def seq_holds(dp_index, seq_index):
    return seq_index == dp_index // 8


def hop_pairs(holds, outward):
    pairs = []
    for i in range(16):
        for s in range(2):
            if holds(i, s):
                there = ((i ^ 8) * 2 + s, i * 2 + s)
                pairs.append(there[::-1] if outward else there)
    return pairs


def corner_pairs(outward):
    first, second = [], []
    for i in range(16):
        h = i // 8
        base = i - i % 2
        if i % 2 == 0:
            for core in range(2):
                source = (base + core) * 2 + h
                first.append((source, (base + 1 - core) * 2 + core))
            core = 1 - h
            second.append(((base + core) * 2 + h, (base + core) * 2 + 1 - h))
    if not outward:
        return [p[::-1] for p in first], [p[::-1] for p in second]
    return first, second


def pair(flag, own, other, axis=0):
    return jnp.where(
        flag == 0,
        jnp.concatenate([own, other], axis),
        jnp.concatenate([other, own], axis),
    )


def pick(flag, first, second):
    return jnp.where(flag == 0, first, second)


class Spot:
    def __init__(self):
        self.d = lax.axis_index(DP)
        self.y = lax.axis_index(SEQ)
        self.z = self.d // 4
        self.x = (self.d // 2) % 2
        self.c = self.d % 2
        self.b = self.z % 2
        self.h = self.z // 2


class Flow:
    def __init__(self):
        self.chains = {}
        self.done = {}

    def add(self, name, chain):
        self.chains[name] = [chain, None, next(chain)]

    def step(self, values, names):
        for name in names:
            entry = self.chains[name]
            if entry[1] is not None:
                try:
                    entry[1:] = [None, entry[0].send(entry[1])]
                except StopIteration as end:
                    self.done[name] = end.value
                    del self.chains[name]
        moving = [name for name in names if name in self.chains]
        arrays = [[array for _, array in self.chains[name][2]] for name in moving]
        ended = [self.done[name] for name in names if name in self.done]
        values, arrays, ended = lax.optimization_barrier((list(values), arrays, ended))
        for name, value in zip([n for n in names if n in self.done], ended):
            self.done[name] = value
        for name, given in zip(moving, arrays):
            entry = self.chains[name]
            entry[1] = [route(array) for (route, _), array in zip(entry[2], given)]
        return values

    def finish(self, name):
        while name in self.chains:
            self.step([], [name])
        return self.done[name]


def by_core(value):
    return swap(value, 1)


def by_x(value):
    return swap(value, 2)


def by_z(value):
    return swap(value, 4)


def by_routes(pairs):
    return lambda value: lax.ppermute(value, BOTH, pairs)


def narrow(value):
    return value.astype(jnp.bfloat16)


def wide(value):
    return value.astype(jnp.float32)


def choose(value, axis, index):
    return lax.dynamic_index_in_dim(value, index, axis, keepdims=False)


def dot_rows(left, right):
    return jnp.einsum("tc,td->cd", left, right, preferred_element_type=jnp.float32)


def settle_x(spot, part):
    (given,) = yield [(by_x, choose(part, 1, 1 - spot.x))]
    return narrow(wide(choose(part, 1, spot.x)) + wide(given))


def settle_z(spot, part, holds):
    (given,) = yield [(by_z, choose(part, 0, 1 - spot.b))]
    block = wide(choose(part, 0, spot.b)) + wide(given)
    (given,) = yield [(by_routes(hop_pairs(holds, False)), narrow(block))]
    return block + wide(given)


def split_rows(spot, block):
    pieces = block.reshape(2, block.shape[0] // 2, block.shape[1])
    (given,) = yield [(by_core, narrow(choose(pieces, 0, 1 - spot.c)))]
    return jnp.where(spot.c == spot.h, choose(pieces, 0, spot.c), wide(given))


def quarters(own):
    rows, cols = own.shape
    return own.reshape(2, 2, rows // 4, cols)


def reduce_both(spot, halves, grads):
    mine = pick(spot.c, halves[0], halves[1])
    theirs = pick(spot.c, halves[1], halves[0])
    grad_own = pick(spot.y, grads[0], grads[1])
    grad_other = pick(spot.y, grads[1], grads[0])
    given = yield [(by_core, narrow(dot_rows(theirs, g))) for g in (grad_own, grad_other)]
    own = dot_rows(mine, grad_own) + wide(given[0])
    other = dot_rows(mine, grad_other) + wide(given[1])
    (given,) = yield [(swap_seq, narrow(other))]
    part = quarters(narrow(own + wide(given)))
    part = yield from settle_x(spot, part)
    block = yield from settle_z(spot, part, core_holds)
    return (yield from split_rows(spot, block))


def reduce_rows(spot, halves, grad):
    mine = pick(spot.c, halves[0], halves[1])
    theirs = pick(spot.c, halves[1], halves[0])
    (given,) = yield [(by_core, narrow(dot_rows(theirs, grad)))]
    part = quarters(narrow(dot_rows(mine, grad) + wide(given)))
    part = yield from settle_x(spot, part)
    block = yield from settle_z(spot, part, core_holds)
    return (yield from split_rows(spot, block))


def reduce_down(spot, left, grads):
    mine = pick(spot.c, grads[0], grads[1])
    theirs = pick(spot.c, grads[1], grads[0])
    (given,) = yield [(by_core, narrow(dot_rows(left, theirs)))]
    part = quarters(narrow(dot_rows(left, mine) + wide(given)))
    part = yield from settle_x(spot, part)
    block = yield from settle_z(spot, part, seq_holds)
    pieces = block.reshape(2, block.shape[0] // 2, block.shape[1])
    same, cross = choose(pieces, 0, spot.c), choose(pieces, 0, 1 - spot.c)
    first, second = corner_pairs(True)
    crossed, across = yield [(by_routes(first), narrow(cross)), (by_routes(second), narrow(same))]
    inner = jnp.where(spot.y == spot.h, same, wide(across))
    return jnp.where(spot.c == spot.y, inner, wide(crossed))


def total_over_all(value):
    for bit in (1, 2, 4, 8):
        value = value + swap(value, bit)
    return value + swap_seq(value)


def gather_images(spot, value):
    for bit, flag in ((1, spot.c), (2, spot.x), (4, spot.b), (8, spot.h)):
        value = pair(flag, value, swap(value, bit))
    return value


def attend(q_src, kv_src, gains, cosine, sine, heads, q_at, k_at, v_at, keys):
    width = heads * HEAD_DIM

    def heads_of(source, at):
        return source[:, at : at + width].reshape(source.shape[0], heads, HEAD_DIM)

    def prepared(source, at, which):
        v = normalize(heads_of(source, at)) * gains[which]
        if cosine is not None:
            q1, q2, q3, q4 = jnp.split(v, 4, axis=-1)
            other = jnp.concatenate([q2, q1, q4, q3], -1)
            v = v * cosine[:, None, :HEAD_DIM] + other * sine[:, None, :HEAD_DIM]
        return v.astype(jnp.bfloat16)

    q, k = prepared(q_src, q_at, 0), prepared(kv_src, k_at, 1)
    v = heads_of(kv_src, v_at).astype(jnp.bfloat16)
    s = jnp.einsum("qhd,khd->hqk", q, k, preferred_element_type=jnp.float32) * HEAD_DIM**-0.5
    s = jnp.where(jnp.arange(kv_src.shape[0]) < keys, s, -1e9)
    p = jax.nn.softmax(s, axis=-1).astype(jnp.bfloat16)
    o = jnp.einsum("hqk,khd->qhd", p, v, preferred_element_type=jnp.float32)
    return o.reshape(q_src.shape[0], width)


def attend_forward(
    q_src, kv_src, cosine, sine, gains, helpers, heads, q_at, k_at, v_at, keys
):
    q32, kv32 = q_src.astype(jnp.float32), kv_src.astype(jnp.float32)
    o, back = jax.vjp(
        lambda a, b, g: attend(a, b, g, cosine, sine, heads, q_at, k_at, v_at, keys),
        q32,
        kv32,
        gains[:2, :HEAD_DIM],
    )
    return narrow(o), back, None, None


def attend_backward(
    q_src, kv_src, cosine, sine, gains, helpers, back, kn, vn, out, grad_out, heads, q_at, k_at, v_at
):
    dq, dk, dg = back(grad_out.astype(jnp.float32))
    dg = jnp.pad(dg * gains[:2, :HEAD_DIM], ((0, 0), (0, LANES - HEAD_DIM)))
    if q_src is kv_src:
        return narrow(dq + dk), dg
    return narrow(dq), narrow(dk), dg


def rope_tables(pos_rows, pos_cols):
    quarter = HEAD_DIM // 4
    frequency = 10000.0 ** (-jnp.arange(quarter, dtype=jnp.float32) / quarter)
    row_angles = pos_rows[:, None] * frequency[None, :]
    col_angles = pos_cols[:, None] * frequency[None, :]
    angles = jnp.concatenate([row_angles, row_angles, col_angles, col_angles], -1)
    sign = jnp.where((jnp.arange(HEAD_DIM) // quarter) % 2 == 0, -1.0, 1.0)
    wide = ((0, 0), (0, LANES - HEAD_DIM))
    return jnp.pad(jnp.cos(angles), wide), jnp.pad(jnp.sin(angles) * sign[None, :], wide)


def gain_rows(gains):
    return jnp.pad(gains, ((0, 0), (0, LANES - HEAD_DIM)))


def gelu(values):
    return jax.nn.gelu(values, approximate=True)


def halves_of(value):
    mid = value.shape[1] // 2
    return value[:, :mid], value[:, mid:]


def norm_parts(values):
    center = values - jnp.mean(values, axis=-1, keepdims=True)
    scale = lax.rsqrt(jnp.mean(center * center, axis=-1, keepdims=True) + EPSILON)
    return center * scale, scale


def norm_grad(grad, values, gain):
    normal, scale = norm_parts(values)
    gain_grad = jnp.sum(grad * normal, axis=0)
    grad = grad * gain
    mean = jnp.mean(grad, axis=-1, keepdims=True)
    mean_product = jnp.mean(grad * normal, axis=-1, keepdims=True)
    return scale * (grad - mean - normal * mean_product), gain_grad


def fast_body(
    hidden_in,
    skip_in,
    clip_text,
    mt5_text,
    time_ids,
    null_text,
    loss_weight,
    patch_pos,
    out_cot,
    skip_weight,
    time_first,
    time_second,
    attn_qkv,
    attn_out,
    cross_qproj,
    cross_kvproj,
    cross_out,
    text_proj,
    mlp_up,
    mlp_down,
    norm_gains,
    head_gains,
):
    spot = Spot()
    _, local, width = hidden_in.shape
    narrow_width = width // 2
    heads_here = HEADS // 2
    clip_len = clip_text.shape[1]
    text_len = clip_len + mt5_text.shape[1]
    text_pad = -(-text_len // LANES) * LANES
    y = spot.y
    bf16 = jnp.bfloat16

    time_rows = lax.all_gather(jnp.concatenate([time_first, time_second], 0), DP)
    time_cut = time_first.shape[0]
    time_weights = [
        rows.reshape(-1, narrow_width) for rows in (time_rows[:, :time_cut], time_rows[:, time_cut:])
    ]
    flow = Flow()
    hidden = hidden_in[0]
    skip = skip_in[0]
    scaled_cot = out_cot[0].astype(jnp.float32) * loss_weight[0]
    cot_low = narrow(scaled_cot)
    pos = patch_pos[:, 0].astype(jnp.float32)
    pos_far = swap_seq(pos)

    def both_halves(value, axis=1):
        return pair(y, value, swap_seq(value), axis)

    a, m, e = (attn_qkv[:, i * narrow_width : (i + 1) * narrow_width] for i in range(3))
    moved = swap_seq(m)
    qkv_shard = jnp.concatenate([pick(y, a, moved), pick(y, e, a), pick(y, moved, e)], 1)

    def gather(shard):
        return lax.all_gather(shard, DP, axis=0, tiled=True)

    def with_far(own):
        return own, swap_seq(own)

    def scatter_rows(grad):
        return wide(lax.psum_scatter(narrow(grad), DP, scatter_dimension=0, tiled=True))

    def scatter_both(grad):
        first, second = halves_of(scatter_rows(grad))
        return pick(y, first, second) + wide(swap_seq(narrow(pick(y, second, first))))

    def times(value, sides):
        return pair(y, project(value, sides[0]), project(value, sides[1]), 1)

    def times_back(grad, sides):
        first, second = halves_of(grad)
        own, far = pick(y, first, second), pick(y, second, first)
        return project_back(own, sides[0]) + project_back(far, sides[1])

    w_skip = with_far(gather(skip_weight))
    w_qkv = gather(qkv_shard)
    w_text = gather(text_proj)
    w_ckv = gather(cross_kvproj)
    out_rows = lax.all_gather(jnp.concatenate([attn_out, cross_qproj, cross_out], 0), DP)
    out_sides = with_far(out_rows.reshape(out_rows.shape[0], 3, -1, narrow_width))
    w_aout, w_cq, w_cout = (
        tuple(side[:, k].reshape(-1, narrow_width) for side in out_sides) for k in range(3)
    )
    w_up = gather(mlp_up)
    down_rows = lax.all_gather(pair(y, mlp_down, swap_seq(mlp_down), 1), DP)
    middle = down_rows.shape[0] // 2
    w_down = pick(y, down_rows[:middle], down_rows[middle:]).reshape(-1, width)
    cot_far = swap_seq(cot_low)

    feats = time_features(time_ids).astype(bf16)
    before = both_halves(project(feats, time_weights[0]))
    lifted = jax.nn.silu(before).astype(bf16)
    shift = both_halves(project(lifted, time_weights[1]))

    cosine, sine = rope_tables(*jnp.concatenate([pos, pos_far], 1))
    helpers = []
    merged = times(jnp.concatenate([hidden, skip], -1), w_skip)
    resid0 = scaled_norm(merged, norm_gains[0])
    normed1 = narrow(scaled_norm(resid0, norm_gains[1]) + shift)

    normed1_both = jnp.concatenate([normed1, swap_seq(normed1)], 0)
    packed = narrow(project(normed1_both, w_qkv))
    self_gains = gain_rows(head_gains[0:2])
    self_o, self_q, self_k, self_v = attend_forward(
        packed,
        packed,
        cosine,
        sine,
        self_gains,
        helpers,
        heads_here,
        0,
        narrow_width,
        2 * narrow_width,
        2 * local,
    )
    far_o = swap_seq(self_o[local:])

    keep_text = (1 - null_text[0]).astype(bf16)
    projected = both_halves(narrow(project(mt5_text[0], w_text)))
    context = jnp.concatenate([clip_text[0], projected], 0) * keep_text
    context = jnp.pad(context, ((0, text_pad - text_len), (0, 0)))
    text_kv = both_halves(narrow(project(context, w_ckv)))
    own_o = self_o[:local]

    attn_halves = pick(y, own_o, far_o), pick(y, far_o, own_o)
    attn_flat = jnp.concatenate(attn_halves, 1)
    resid1 = resid0 + times(attn_flat, w_aout)
    normed2 = narrow(scaled_norm(resid1, norm_gains[2]))
    cross_pre = narrow(times(normed2, w_cq))
    cross_gains = gain_rows(head_gains[2:4])
    cross_o, cross_q, cross_k, cross_v = attend_forward(
        cross_pre, text_kv, None, None, cross_gains, helpers, HEADS, 0, 0, width, text_len
    )
    resid2 = resid1 + times(cross_o, w_cout)
    normed3 = narrow(scaled_norm(resid2, norm_gains[3]))

    normed3_both = jnp.concatenate([normed3, swap_seq(normed3)], 0)
    upper = narrow(project(normed3_both, w_up))
    active = narrow(gelu(upper.astype(jnp.float32)))
    mixed = project(active, w_down)
    final = resid2 + mixed[:local] + wide(swap_seq(narrow(mixed[local:])))
    block_out = narrow(final)[None]

    cot_both = jnp.concatenate([cot_low, cot_far], 0)
    d_active = project_back(cot_both, w_down)
    _, gelu_back = jax.vjp(gelu, upper.astype(jnp.float32))
    d_upper = narrow(gelu_back(d_active)[0])
    flow.add(8, reduce_down(spot, active, halves_of(cot_both)))
    (d_upper,) = flow.step([d_upper], [8])
    d_both = project_back(d_upper, w_up)
    d_far = swap_seq(narrow(d_both[local:]))
    flow.add(7, reduce_rows(spot, halves_of(normed3_both), d_upper))
    d_own, d_far = flow.step([d_both[:local], d_far], [8, 7])
    d_normed3 = d_own + wide(d_far)
    d_resid, d_gain3 = norm_grad(d_normed3, resid2, norm_gains[3])
    resid_grad = scaled_cot + d_resid

    grad_low = narrow(resid_grad)
    d_cmix = narrow(times_back(grad_low, w_cout))
    g_cout = scatter_both(dot_rows(cross_o, grad_low))
    d_cpre, d_textkv, d_cross_gains = attend_backward(
        cross_pre,
        text_kv,
        None,
        None,
        cross_gains,
        helpers,
        cross_q,
        cross_k,
        cross_v,
        cross_o,
        d_cmix,
        HEADS,
        0,
        0,
        width,
    )
    g_cquery = scatter_both(dot_rows(normed2, d_cpre))
    d_cpre, d_textkv = flow.step([d_cpre, d_textkv], [8, 7])
    d_text = halves_of(d_textkv)
    d_text_far = swap_seq(pick(y, d_text[1], d_text[0]))
    d_normed2 = times_back(d_cpre, w_cq)
    d_resid, d_gain2 = norm_grad(d_normed2, resid1, norm_gains[2])
    resid_grad = resid_grad + d_resid
    grad_low = narrow(resid_grad)
    d_attn = halves_of(narrow(times_back(grad_low, w_aout)))
    d_far = swap_seq(pick(y, d_attn[1], d_attn[0]))
    d_text = narrow(wide(pick(y, d_text[0], d_text[1])) + wide(d_text_far))
    g_aout = scatter_both(dot_rows(attn_flat, grad_low))
    g_ckv = scatter_rows(dot_rows(context, d_text))
    d_context = halves_of(project_back(d_text[clip_len:text_len], w_ckv))
    d_context_far = swap_seq(narrow(pick(y, d_context[1], d_context[0])))
    d_proj = pick(y, d_context[0], d_context[1]) + wide(d_context_far)
    d_proj = narrow(d_proj * keep_text.astype(jnp.float32))
    g_tproj = scatter_rows(dot_rows(mt5_text[0], d_proj))

    d_heads = jnp.concatenate([pick(y, d_attn[0], d_attn[1]), d_far], 0)
    (d_heads,) = flow.step([d_heads], [8])
    d_packed, d_self_gains = attend_backward(
        packed,
        packed,
        cosine,
        sine,
        self_gains,
        helpers,
        self_q,
        self_k,
        self_v,
        self_o,
        d_heads,
        heads_here,
        0,
        narrow_width,
        2 * narrow_width,
    )
    (d_packed,) = flow.step([d_packed], [8, 7])
    d_both = project_back(d_packed, w_qkv)
    d_far = swap_seq(narrow(d_both[local:]))
    flow.add(1, reduce_rows(spot, halves_of(normed1_both), d_packed))
    d_own, d_far = flow.step(
        [d_both[:local], d_far],
        [7, 1],
    )
    d_normed1 = d_own + wide(d_far)

    d_shift = jnp.sum(d_normed1, axis=0)
    d_resid, d_gain1 = norm_grad(d_normed1, resid0, norm_gains[1])
    resid_grad = resid_grad + d_resid
    d_merged, d_gain0 = norm_grad(resid_grad, merged, norm_gains[0])
    d_merged = narrow(d_merged)
    flow.add(0, reduce_both(spot, (hidden, skip), halves_of(d_merged)))
    (d_merged,) = flow.step(
        [d_merged],
        [0, 7, 1],
    )
    d_joined = times_back(d_merged, w_skip)
    hidden_grad, skip_grad = d_joined[:, :width][None], d_joined[:, width:][None]

    d_shift = d_shift + swap_seq(d_shift)
    features = jnp.pad(feats.astype(jnp.float32), ((0, 0), (0, width - FREQ)))
    rows = gather_images(spot, jnp.stack([before[0], features[0], d_shift], 0)[None])
    before_all, features_all, d_shift_all = rows[:, 0], rows[:, 1, :FREQ], rows[:, 2]
    silu_all, silu_back = jax.vjp(jax.nn.silu, before_all)
    lifted_all = wide(narrow(silu_all))
    d_shift_cols = pick(y, *halves_of(d_shift_all))
    d_lifted = jnp.einsum(
        "bd,cd->bc", d_shift_cols, time_weights[1].astype(jnp.float32), precision=HIGHEST
    )
    d_before = silu_back(d_lifted + swap_seq(d_lifted))[0]

    def block(left, cols, left_rows):
        mine = lax.dynamic_slice_in_dim(left, spot.d * left_rows, left_rows, 1)
        return jnp.einsum("bc,bd->cd", mine, cols, precision=HIGHEST)

    g_tsecond = block(lifted_all, d_shift_cols, time_second.shape[0])
    g_tfirst = block(features_all, pick(y, *halves_of(d_before)), time_first.shape[0])

    d_head_gains = jnp.concatenate([d_self_gains, d_cross_gains], 0)[:, :HEAD_DIM] / head_gains
    d_norm_gains = jnp.stack([d_gain0, d_gain1, d_gain2, d_gain3], 0)
    totals = total_over_all(
        jnp.concatenate([d_norm_gains.reshape(-1), d_head_gains.reshape(-1)])
    )
    norm_total = totals[: 4 * width].reshape(4, width)
    head_total = totals[4 * width :].reshape(4, HEAD_DIM)

    while flow.chains:
        flow.step([], list(flow.chains))
    g_skipw, g_qkv, g_up, g_down = (flow.done[name] for name in (0, 1, 7, 8))
    q_cols, k_cols, v_cols = (
        g_qkv[:, i * narrow_width : (i + 1) * narrow_width] for i in range(3)
    )
    moved = wide(swap_seq(narrow(pick(y, v_cols, q_cols))))
    g_qkv = jnp.concatenate([pick(y, q_cols, k_cols), moved, pick(y, k_cols, v_cols)], 1)
    return (
        block_out,
        hidden_grad,
        skip_grad,
        g_skipw,
        g_tfirst,
        g_tsecond,
        g_qkv,
        g_aout,
        g_cquery,
        g_ckv,
        g_cout,
        g_tproj,
        g_up,
        g_down,
        norm_total,
        head_total,
    )


def solution(mesh):
    placed = (
        P(DP, SEQ, None),
        P(DP, SEQ, None),
        P(DP, None, None),
        P(DP, None, None),
        P(DP),
        P(DP),
        P(DP),
        P(None, DP, SEQ),
        P(DP, SEQ, None),
        P(DP, SEQ),
        P(DP, SEQ),
        P(DP, SEQ),
        P(DP, SEQ),
        P(DP, SEQ),
        P(DP, SEQ),
        P(DP, SEQ),
        P(DP, SEQ),
        P(DP, SEQ),
        P(DP, SEQ),
        P(DP, SEQ),
        P(),
        P(),
    )
    split = mesh.shape[DP] == 16 and mesh.shape[SEQ] == 2
    return jax.shard_map(
        fast_body if split else whole_body,
        mesh=mesh,
        in_specs=placed,
        out_specs=(
            P(DP, SEQ, None),
            P(DP, SEQ, None),
            P(DP, SEQ, None),
            P(DP, SEQ),
            P(DP, SEQ),
            P(DP, SEQ),
            P(DP, SEQ),
            P(DP, SEQ),
            P(DP, SEQ),
            P(DP, SEQ),
            P(DP, SEQ),
            P(DP, SEQ),
            P(DP, SEQ),
            P(DP, SEQ),
            P(),
            P(),
        ),
        check_vma=False,
    )
```
